32 devices in a mesh: seq: 2 (over x), ctx: 16 (over z, y, core).
Axes of the slice: x: 2, y: 2, z: 4, core: 2. Of those that a mesh axis runs over, the one named last changes fastest.
Arguments:
- layer_input: bfloat16 [2, 2048, 768], P('seq', 'ctx'), may hold values from -6 to 6
- query_weight: bfloat16 [768, 768], P(('seq', 'ctx')), may hold values from -0.3125 to 0.3125
- query_bias: bfloat16 [768], P(('seq', 'ctx')), may hold values from -3 to 3
- key_weight: bfloat16 [768, 768], P(('seq', 'ctx')), may hold values from -0.3125 to 0.3125
- value_weight: bfloat16 [768, 768], P(('seq', 'ctx')), may hold values from -0.21875 to 0.21875
- value_bias: bfloat16 [768], P(('seq', 'ctx')), may hold values from -3 to 3
- mixer_weight: bfloat16 [768, 768], P(('seq', 'ctx')), may hold values from -1.25 to 1.25
- mixer_bias: bfloat16 [768], P(('seq', 'ctx')), may hold values from -3 to 3
- first_gain: bfloat16 [768], P(('seq', 'ctx')), may hold values from 0.099609375 to 1.8984375
- first_shift: bfloat16 [768], P(('seq', 'ctx')), may hold values from -3 to 3
- inner_weight: bfloat16 [768, 3072], P(('seq', 'ctx')), may hold values from -0.21875 to 0.21875
- inner_bias: bfloat16 [3072], P(('seq', 'ctx')), may hold values from -3 to 3
- outer_weight: bfloat16 [3072, 768], P(('seq', 'ctx')), may hold values from -0.109375 to 0.109375
- outer_bias: bfloat16 [768], P(('seq', 'ctx')), may hold values from -3 to 3
- second_gain: bfloat16 [768], P(('seq', 'ctx')), may hold values from 0.099609375 to 1.8984375
- second_shift: bfloat16 [768], P(('seq', 'ctx')), may hold values from -3 to 3
- head_weight: bfloat16 [768], P(('seq', 'ctx')), may hold values from -0.21875 to 0.21875
- out_cotangent: bfloat16 [2, 2048, 768], P('seq', 'ctx'), may hold values from -6 to 6
- term_cotangent: float32 [2, 2048], P('seq', 'ctx'), may hold values from -6 to 6
Outputs:
- layer_output: bfloat16 [2, 2048, 768], P('seq', 'ctx')
- term_weights: float32 [2, 2048], P('seq', 'ctx')
- input_grad: bfloat16 [2, 2048, 768], P('seq', 'ctx')
- query_weight_grad: float32 [768, 768], P(('seq', 'ctx'))
- query_bias_grad: float32 [768], P(('seq', 'ctx'))
- key_weight_grad: float32 [768, 768], P(('seq', 'ctx'))
- value_weight_grad: float32 [768, 768], P(('seq', 'ctx'))
- value_bias_grad: float32 [768], P(('seq', 'ctx'))
- mixer_weight_grad: float32 [768, 768], P(('seq', 'ctx'))
- mixer_bias_grad: float32 [768], P(('seq', 'ctx'))
- first_gain_grad: float32 [768], P(('seq', 'ctx'))
- first_shift_grad: float32 [768], P(('seq', 'ctx'))
- inner_weight_grad: float32 [768, 3072], P(('seq', 'ctx'))
- inner_bias_grad: float32 [3072], P(('seq', 'ctx'))
- outer_weight_grad: float32 [3072, 768], P(('seq', 'ctx'))
- outer_bias_grad: float32 [768], P(('seq', 'ctx'))
- second_gain_grad: float32 [768], P(('seq', 'ctx'))
- second_shift_grad: float32 [768], P(('seq', 'ctx'))
- head_weight_grad: float32 [768], P(('seq', 'ctx'))
The draws below stay inside these ranges and needn't reach their ends.
All inputs are finite; a program needn't handle non-finite values.
Results may differ from the reference program's by a relative error of at most 0.025.
Values may be sent and summed in bfloat16 or wider, within the bound.
No kernel may reach another device: no remote copies, remote signals or barrier semaphores. Data moves between devices by JAX's collectives and lax.ppermute only.
A program may use at most 128 MiB of HBM per device.

```python
import math
import jax
import jax.numpy as jnp
from jax import lax

D = 768
HEADS = 12
HD = 64
FF = 3072
SEQS = 2
LENGTH = 2048


def level_of(rng, extent, shards, least, top_value):
    factor_of = 1.0
    for axis_at, parts in shards:
        heights = jax.random.uniform(jax.random.fold_in(jax.random.fold_in(rng, 6), axis_at), (parts,), jnp.float32, least / len(shards), top_value / len(shards))
        factor_of = factor_of * jnp.repeat(jnp.exp(heights), extent[axis_at] // parts).reshape((-1,) + (1,) * (len(extent) - 1 - axis_at))
    return factor_of


def gaussian(rng, extent, spread, bound, shards=(), dtype=jnp.bfloat16):
    drawn = jax.random.normal(rng, extent, jnp.float32) * spread
    if len(shards) > 0:
        drawn = level_of(rng, extent, shards, -0.22, 0.18) * drawn
    return jnp.clip(drawn, min=-bound, max=bound).astype(dtype)


def setup_inputs(seed: int = 0) -> dict:
    splits = jax.random.split(jax.random.key(seed), 20)
    layer_input = gaussian(splits[0], (SEQS, LENGTH, D), 1.0, 6.0, ((0, 2), (1, 16)))
    query_weight = gaussian(splits[1], (D, D), (D * 2 // 5) ** -0.5, 0.3125, ((0, 32),))
    query_bias = gaussian(splits[2], (D,), 0.5, 3.0, ((0, 32),))
    key_weight = gaussian(splits[3], (D, D), (D * 2 // 5) ** -0.5, 0.3125, ((0, 32),))
    value_weight = gaussian(splits[4], (D, D), D ** -0.5, 0.21875, ((0, 32),))
    value_bias = gaussian(splits[5], (D,), 0.5, 3.0, ((0, 32),))
    mixer_weight = gaussian(splits[6], (D, D), (D // 32) ** -0.5, 1.25, ((0, 32),))
    mixer_bias = gaussian(splits[7], (D,), 0.5, 3.0, ((0, 32),))
    first_gain = jnp.clip(1.0 + 0.18 * jax.random.normal(splits[8], (D,), jnp.float32), 0.099609375, 1.8984375).astype(jnp.bfloat16)
    first_shift = gaussian(splits[9], (D,), 0.5, 3.0, ((0, 32),))
    inner_weight = gaussian(splits[10], (D, FF), D ** -0.5, 0.21875, ((0, 32),))
    inner_bias = gaussian(splits[11], (FF,), 0.5, 3.0, ((0, 32),))
    outer_weight = gaussian(splits[12], (FF, D), FF ** -0.5, 0.109375, ((0, 32),))
    outer_bias = gaussian(splits[13], (D,), 0.5, 3.0, ((0, 32),))
    second_gain = jnp.clip(1.0 + 0.18 * jax.random.normal(splits[14], (D,), jnp.float32), 0.099609375, 1.8984375).astype(jnp.bfloat16)
    second_shift = gaussian(splits[15], (D,), 0.5, 3.0, ((0, 32),))
    head_weight = gaussian(splits[16], (D,), D ** -0.5, 0.21875, ((0, 32),))
    out_cotangent = gaussian(splits[17], (SEQS, LENGTH, D), 1.0, 6.0, ((0, 2), (1, 16)))
    term_cotangent = gaussian(splits[18], (SEQS, LENGTH), 1.0, 6.0, ((0, 2), (1, 16)), jnp.float32)
    return {"layer_input": layer_input, "query_weight": query_weight, "query_bias": query_bias, "key_weight": key_weight, "value_weight": value_weight, "value_bias": value_bias, "mixer_weight": mixer_weight, "mixer_bias": mixer_bias, "first_gain": first_gain, "first_shift": first_shift, "inner_weight": inner_weight, "inner_bias": inner_bias, "outer_weight": outer_weight, "outer_bias": outer_bias, "second_gain": second_gain, "second_shift": second_shift, "head_weight": head_weight, "out_cotangent": out_cotangent, "term_cotangent": term_cotangent}


EPSILON = 1e-12
HIGHEST = lax.Precision.HIGHEST
ROOT_HALF = 0.7071067811865476

@jax.custom_vjp
def low(v):
    return lax.optimization_barrier(v.astype(jnp.bfloat16)).astype(jnp.float32)

@jax.custom_vjp
def low_back(v):
    return v

def low_keep(v):
    return (low(v), None)

def low_pass(kept, grad):
    return (grad,)

def back_keep(v):
    return (v, None)

def back_low(kept, grad):
    return (low(grad),)
low.defvjp(low_keep, low_pass)
low_back.defvjp(back_keep, back_low)

def rounded(value):
    return low(low_back(value))

def project(left_side, right_side):
    return jnp.dot(left_side, right_side, precision=HIGHEST)

def normalize(residual, norm_gain, norm_shift):
    center = residual - lax.optimization_barrier(jnp.mean(residual, axis=-1, keepdims=True))
    row_scale = lax.rsqrt(lax.optimization_barrier(jnp.mean(center * center, axis=-1, keepdims=True)) + EPSILON)
    return center * row_scale * norm_gain + norm_shift

def gelu_exact(inner_rows):
    return 0.5 * inner_rows * (1.0 + lax.erf(inner_rows * ROOT_HALF))

def soft_plus(logits):
    return jnp.maximum(logits, 0.0) + jnp.log1p(jnp.exp(-jnp.abs(logits)))

def softmax_rows(scores):
    shifted = jnp.exp(scores - lax.optimization_barrier(jnp.max(scores, axis=-1, keepdims=True)))
    return shifted / lax.optimization_barrier(jnp.sum(shifted, axis=-1, keepdims=True))

def attend_block(query_block, key_heads, value_heads):
    scores = low_back(jnp.einsum('qhd,khd->hqk', query_block, key_heads, precision=HIGHEST)) / math.sqrt(HD)
    prob_rows = softmax_rows(scores)
    return jnp.einsum('hqk,khd->qhd', low(prob_rows), value_heads, precision=HIGHEST)

def one_sequence(inputs, params):
    query_weight, query_bias, key_weight, value_weight, value_bias, mixer_weight, mixer_bias, first_gain, first_shift, inner_weight, inner_bias, outer_weight, outer_bias, second_gain, second_shift, head_weight = params
    queries = rounded(project(inputs, query_weight) + query_bias)
    key_rows = rounded(project(inputs, key_weight))
    value_rows = rounded(project(inputs, value_weight) + value_bias)
    block_rows = math.gcd(LENGTH, 512)
    query_blocks = queries.reshape(LENGTH // block_rows, block_rows, HEADS, HD)
    key_heads = key_rows.reshape(LENGTH, HEADS, HD)
    value_heads = value_rows.reshape(LENGTH, HEADS, HD)

    def block_fn(query_block):
        return attend_block(query_block, key_heads, value_heads)
    context = lax.map(jax.checkpoint(block_fn), query_blocks)
    context = rounded(context.reshape(LENGTH, D))
    attended = low_back(project(context, mixer_weight) + mixer_bias)
    first_rows = normalize(inputs + attended, first_gain, first_shift)
    inner_rows = low_back(project(low(first_rows), inner_weight) + inner_bias)
    active = low(gelu_exact(inner_rows))
    outer_rows = low_back(project(active, outer_weight) + outer_bias)
    final_rows = normalize(first_rows + outer_rows, second_gain, second_shift)
    return (final_rows, soft_plus(project(final_rows, head_weight)))

def reference(layer_input, query_weight, query_bias, key_weight, value_weight, value_bias, mixer_weight, mixer_bias, first_gain, first_shift, inner_weight, inner_bias, outer_weight, outer_bias, second_gain, second_shift, head_weight, out_cotangent, term_cotangent):
    params = tuple((weight.astype(jnp.float32) for weight in (query_weight, query_bias, key_weight, value_weight, value_bias, mixer_weight, mixer_bias, first_gain, first_shift, inner_weight, inner_bias, outer_weight, outer_bias, second_gain, second_shift, head_weight)))
    inputs = layer_input.astype(jnp.float32)

    def forward(all_inputs, all_params):
        final_list = []
        term_list = []
        for sequence in range(SEQS):
            final_rows, terms = one_sequence(all_inputs[sequence], all_params)
            final_list.append(final_rows)
            term_list.append(terms)
        return (jnp.stack(final_list), jnp.stack(term_list))
    (finals, term_weights), backward = jax.vjp(forward, inputs, params)
    input_grad, grads = backward((out_cotangent.astype(jnp.float32), term_cotangent.astype(jnp.float32)))
    gq_weight, gq_bias, gk_weight, gv_weight, gv_bias, gm_weight, gm_bias, gf_gain, gf_shift, gi_weight, gi_bias, go_weight, go_bias, gs_gain, gs_shift, gh_weight = grads
    return (finals.astype(jnp.bfloat16), term_weights, input_grad.astype(jnp.bfloat16), gq_weight, gq_bias, gk_weight, gv_weight, gv_bias, gm_weight, gm_bias, gf_gain, gf_shift, gi_weight, gi_bias, go_weight, go_bias, gs_gain, gs_shift, gh_weight)
```

```python
import functools
import math

import jax
import jax.numpy as jnp
from jax import lax
from jax.experimental import pallas as pl
from jax.experimental.pallas import tpu as pltpu
from jax.sharding import PartitionSpec as P

HEADS = 12
HD = 64
WIDTH = HEADS * HD
HALF = WIDTH // 2
NH = HEADS // 2
EPSILON = 1e-12
ROOT_HALF = 0.7071067811865476
GAUSS_FACTOR = 0.3989422804014327
F32 = jnp.float32
BF16 = jnp.bfloat16
AUX = 128


def mm(a, b):
    return lax.dot_general(a, b, (((1,), (0,)), ((), ())), preferred_element_type=F32)


def mm_t(a, b):
    return lax.dot_general(a, b, (((1,), (1,)), ((), ())), preferred_element_type=F32)


def t_mm(a, b):
    return lax.dot_general(a, b, (((0,), (0,)), ((), ())), preferred_element_type=F32)


def swap_ctx(value, bit):
    n = lax.axis_size("ctx")
    return lax.ppermute(value, "ctx", [(i, i ^ bit) for i in range(n)])


def swap_core(value):
    return swap_ctx(value, 1)


def swap_y(value):
    return swap_ctx(value, 2)


def swap_x(value):
    return lax.ppermute(value, "seq", [(0, 1), (1, 0)])


def shift_z(value, k):
    n = lax.axis_size("ctx")
    return lax.ppermute(value, "ctx", [(i, (i + 4 * k) % n) for i in range(n)])


def pair(bit, own, other, axis=0):
    first = jnp.where(bit == 0, own, other)
    second = jnp.where(bit == 0, other, own)
    return jnp.stack([first, second], axis=axis)


def pick(value, index, axis):
    return lax.dynamic_index_in_dim(value, index, axis, keepdims=False)


def gather_chips(block, x, y, z):
    zs = lax.axis_size("ctx") // 4
    rows, cols = block.shape
    along = jnp.zeros((zs, rows, cols), block.dtype)
    for k in range(zs):
        piece = block if k == 0 else shift_z(block, k)
        along = lax.dynamic_update_slice(along, piece[None], ((z - k) % zs, 0, 0))
    both = pair(y, along, swap_y(along), axis=1)
    full = pair(x, both, swap_x(both), axis=0)
    return full.reshape(4 * zs * rows, cols)


def scatter_chips(part, x, y, z):
    zs = lax.axis_size("ctx") // 4
    cols = part.shape[1]
    part = part.reshape(2, -1, cols)
    got = swap_x(pick(part, 1 - x, 0).astype(BF16))
    part = pick(part, x, 0) + got.astype(F32)
    part = part.reshape(zs, 2, -1, cols)
    got = swap_y(pick(part, 1 - y, 1).astype(BF16))
    part = pick(part, y, 1) + got.astype(F32)
    total = pick(part, z, 0)
    for k in range(1, zs):
        total = total + shift_z(pick(part, (z + k) % zs, 0).astype(BF16), k).astype(F32)
    return total


def attend_kernel(q_ref, kv_ref, o_ref, lse_ref, m_s, l_s, acc_s):
    step = pl.program_id(0)

    @pl.when(step == 0)
    def _():
        m_s[...] = jnp.full(m_s.shape, -1e30, F32)
        l_s[...] = jnp.zeros(l_s.shape, F32)
        acc_s[...] = jnp.zeros(acc_s.shape, F32)

    for h in range(NH):
        lo = h * HD
        qh = q_ref[:, lo : lo + HD]
        kh = kv_ref[:, lo : lo + HD]
        vh = kv_ref[:, HALF + lo : HALF + lo + HD]
        s = mm_t(kh, qh)
        before = m_s[h : h + 1, :]
        top = jnp.maximum(before, jnp.max(s, axis=0, keepdims=True))
        p = jnp.exp(s - top)
        factor = jnp.exp(before - top)
        m_s[h : h + 1, :] = top
        l_s[h : h + 1, :] = l_s[h : h + 1, :] * factor + jnp.sum(p, axis=0, keepdims=True)
        acc_s[lo : lo + HD, :] = acc_s[lo : lo + HD, :] * factor + t_mm(vh, p.astype(BF16))

    @pl.when(step == pl.num_programs(0) - 1)
    def _():
        lse_ref[...] = m_s[...] + jnp.log(l_s[...])
        for h in range(NH):
            lo = h * HD
            o_ref[lo : lo + HD, :] = acc_s[lo : lo + HD, :] / l_s[h : h + 1, :]


def attend(q, kv):
    tokens = q.shape[0]
    keys = kv.shape[0]
    block = math.gcd(keys, 1024)
    return pl.pallas_call(
        attend_kernel,
        grid=(keys // block,),
        in_specs=[
            pl.BlockSpec((tokens, HALF), lambda i: (0, 0)),
            pl.BlockSpec((block, WIDTH), lambda i: (i, 0)),
        ],
        out_specs=[
            pl.BlockSpec((HALF, tokens), lambda i: (0, 0)),
            pl.BlockSpec((8, tokens), lambda i: (0, 0)),
        ],
        out_shape=[
            jax.ShapeDtypeStruct((HALF, tokens), F32),
            jax.ShapeDtypeStruct((8, tokens), F32),
        ],
        scratch_shapes=[
            pltpu.VMEM((8, tokens), F32),
            pltpu.VMEM((8, tokens), F32),
            pltpu.VMEM((HALF, tokens), F32),
        ],
        compiler_params=pltpu.CompilerParams(vmem_limit_bytes=40 * 2**20),
        cost_estimate=pl.CostEstimate(
            flops=4 * tokens * keys * HALF,
            bytes_accessed=2 * keys * WIDTH,
            transcendentals=tokens * keys * NH,
        ),
    )(q, kv)


def attend_back_kernel(q_ref, g_ref, o_ref, lse_ref, kv_ref, dq_ref, dkv_ref, delta_s, acc_s):
    step = pl.program_id(0)

    @pl.when(step == 0)
    def _():
        acc_s[...] = jnp.zeros(acc_s.shape, F32)
        prod = jnp.transpose(g_ref[...].astype(F32)) * o_ref[...]
        for h in range(NH):
            delta_s[h : h + 1, :] = jnp.sum(prod[h * HD : (h + 1) * HD, :], axis=0, keepdims=True)

    held = []
    for h in range(NH):
        lo = h * HD
        qh = q_ref[:, lo : lo + HD]
        gh = g_ref[:, lo : lo + HD]
        kh = kv_ref[:, lo : lo + HD]
        vh = kv_ref[:, HALF + lo : HALF + lo + HD]
        p = jnp.exp(mm_t(kh, qh) - lse_ref[h : h + 1, :])
        dp = mm_t(vh, gh)
        ds = (p * (dp - delta_s[h : h + 1, :])).astype(BF16)
        acc_s[lo : lo + HD, :] += t_mm(kh, ds)
        held.append((mm(ds, qh).astype(BF16), mm(p.astype(BF16), gh).astype(BF16)))
        if h % 2 == 1:
            (dk0, dv0), (dk1, dv1) = held
            held = []
            at = lo - HD
            dkv_ref[:, at : at + 2 * HD] = jnp.concatenate([dk0, dk1], axis=1)
            dkv_ref[:, HALF + at : HALF + at + 2 * HD] = jnp.concatenate([dv0, dv1], axis=1)

    @pl.when(step == pl.num_programs(0) - 1)
    def _():
        dq_ref[...] = jnp.transpose(acc_s[...] * 0.125).astype(BF16)


def attend_back(q, g, o, lse, kv):
    tokens = q.shape[0]
    keys = kv.shape[0]
    block = math.gcd(keys, 1024)
    whole = lambda i: (0, 0)
    return pl.pallas_call(
        attend_back_kernel,
        grid=(keys // block,),
        in_specs=[
            pl.BlockSpec((tokens, HALF), whole),
            pl.BlockSpec((tokens, HALF), whole),
            pl.BlockSpec((HALF, tokens), whole),
            pl.BlockSpec((8, tokens), whole),
            pl.BlockSpec((block, WIDTH), lambda i: (i, 0)),
        ],
        out_specs=[
            pl.BlockSpec((tokens, HALF), whole),
            pl.BlockSpec((block, WIDTH), lambda i: (i, 0)),
        ],
        out_shape=[
            jax.ShapeDtypeStruct((tokens, HALF), BF16),
            jax.ShapeDtypeStruct((keys, WIDTH), BF16),
        ],
        scratch_shapes=[
            pltpu.VMEM((8, tokens), F32),
            pltpu.VMEM((HALF, tokens), F32),
        ],
        compiler_params=pltpu.CompilerParams(vmem_limit_bytes=48 * 2**20),
        cost_estimate=pl.CostEstimate(
            flops=10 * tokens * keys * HALF,
            bytes_accessed=4 * keys * WIDTH,
            transcendentals=tokens * keys * NH,
        ),
    )(q, g, o, lse, kv)


def norm_forward(residual, gain, shift):
    center = residual - jnp.mean(residual, axis=-1, keepdims=True)
    scale = lax.rsqrt(jnp.mean(center * center, axis=-1, keepdims=True) + EPSILON)
    normed = center * scale
    return normed * gain + shift, normed, scale


def norm_backward(grad_out, normed, scale, gain):
    grad_normed = grad_out * gain
    return scale * (
        grad_normed
        - jnp.mean(grad_normed, axis=-1, keepdims=True)
        - normed * jnp.mean(grad_normed * normed, axis=-1, keepdims=True)
    )


def gelu_pair(u):
    cdf = 0.5 * (1.0 + lax.erf(u * ROOT_HALF))
    return u * cdf, cdf + u * jnp.exp(-0.5 * u * u) * GAUSS_FACTOR


def soft_plus(logits):
    return jnp.maximum(logits, 0.0) + jnp.log1p(jnp.exp(-jnp.abs(logits)))


def shards(
    layer_input,
    query_weight,
    query_bias,
    key_weight,
    value_weight,
    value_bias,
    mixer_weight,
    mixer_bias,
    first_gain,
    first_shift,
    inner_weight,
    inner_bias,
    outer_weight,
    outer_bias,
    second_gain,
    second_shift,
    head_weight,
    out_cotangent,
    term_cotangent,
):
    n = lax.axis_size("ctx")
    zs = n // 4
    chips = n
    x = lax.axis_index("seq")
    at = lax.axis_index("ctx")
    z, y, core = at // 4, (at // 2) % 2, at % 2
    inputs = layer_input[0]
    tokens = inputs.shape[0]
    rows = query_weight.shape[0]
    hidden = outer_weight.shape[0]
    ff = inner_weight.shape[1]

    def pair_core(own, other, axis=0):
        return pair(core, own, other, axis)

    inputs2 = pair_core(inputs, swap_core(inputs)).reshape(2 * tokens, WIDTH)

    vectors = jnp.stack(
        [
            query_bias,
            value_bias,
            mixer_bias,
            first_gain,
            first_shift,
            outer_bias,
            second_gain,
            second_shift,
            head_weight,
        ],
        axis=1,
    )
    aux = jnp.concatenate([vectors, inner_bias.reshape(rows, hidden // rows)], axis=1)
    aux = jnp.pad(aux, ((0, 0), (0, AUX - aux.shape[1])))
    qkv = jnp.stack([query_weight, key_weight, value_weight]).reshape(3, rows, 2, HALF)

    def qkv_of(side):
        part = jnp.transpose(pick(qkv, side, 2), (1, 0, 2)).reshape(rows, 3 * HALF)
        return jnp.concatenate([part, aux], axis=1)

    qkv_block = pair_core(qkv_of(core), swap_core(qkv_of(1 - core)))
    qkv_full = gather_chips(qkv_block.reshape(2 * rows, 3 * HALF + AUX), x, y, z)
    w_qkv = qkv_full[:, : 3 * HALF]
    aux_full = qkv_full[:, 3 * HALF :]

    inner_split = inner_weight.reshape(rows, chips, 2, hidden)

    def inner_of(side):
        return pick(inner_split, side, 2).reshape(rows, ff // 2)

    inner_block = pair_core(inner_of(core), swap_core(inner_of(1 - core)))
    w_inner = gather_chips(inner_block.reshape(2 * rows, ff // 2), x, y, z)
    w_outer = gather_chips(outer_weight, x, y, z)
    mixer_half = gather_chips(mixer_weight, x, y, z).reshape(chips, rows, WIDTH)
    w_mixer = pair_core(mixer_half, swap_core(mixer_half), axis=1).reshape(WIDTH, WIDTH)

    vecs = jnp.transpose(aux_full[:, :16].astype(F32))
    q_bias = lax.dynamic_slice_in_dim(vecs[0], core * HALF, HALF, 0)
    v_bias = lax.dynamic_slice_in_dim(vecs[1], core * HALF, HALF, 0)
    m_bias, f_gain, f_shift = vecs[2], vecs[3], vecs[4]
    o_bias, s_gain, s_shift, head = vecs[5], vecs[6], vecs[7], vecs[8]
    i_bias = aux_full[:, 9 : 9 + hidden // rows].reshape(chips, 2, hidden)
    i_bias = pick(i_bias, core, 1).reshape(ff // 2).astype(F32)

    bias = jnp.concatenate([q_bias, jnp.zeros((HALF,), F32), v_bias])
    projected = (mm(inputs2, w_qkv) + bias).astype(BF16)
    q_scaled = projected[:, :HALF] * BF16(0.125)
    kv_own = projected[:, HALF:]
    kv_z = jnp.concatenate([kv_own] + [shift_z(kv_own, k) for k in range(1, zs)], axis=0)
    kv = jnp.concatenate([kv_z, swap_y(kv_z)], axis=0)
    o_exact, lse = attend(q_scaled, kv)
    context2 = jnp.transpose(o_exact).astype(BF16).reshape(2, tokens, HALF)
    got = swap_core(pick(context2, 1 - core, 0))
    context = pair_core(pick(context2, core, 0), got, axis=1).reshape(tokens, WIDTH)

    attended = mm(context, w_mixer) + m_bias
    first_rows, first_normed, first_scale = norm_forward(
        inputs.astype(F32) + attended, f_gain, f_shift
    )
    first_low = first_rows.astype(BF16)
    first2 = pair_core(first_low, swap_core(first_low)).reshape(2 * tokens, WIDTH)

    def sum_core(part):
        part = part.reshape(2, tokens, WIDTH)
        return pick(part, core, 0) + swap_core(pick(part, 1 - core, 0))

    inner_rows = mm(first2, w_inner) + i_bias
    act, slope = gelu_pair(inner_rows)
    active = act.astype(BF16)
    outer_rows = sum_core(mm(active, w_outer)) + o_bias
    final_rows, second_normed, second_scale = norm_forward(
        first_rows + outer_rows, s_gain, s_shift
    )
    logits = jnp.sum(final_rows * head, axis=-1)
    term_weights = soft_plus(logits)
    head_slope = term_cotangent[0] * jax.nn.sigmoid(logits)
    grad_final = out_cotangent[0].astype(F32) + head_slope[:, None] * head
    head_grad = jnp.sum(head_slope[:, None] * final_rows, axis=0)
    grad_second = norm_backward(grad_final, second_normed, second_scale, s_gain)
    second_gain_grad = jnp.sum(grad_final * second_normed, axis=0)
    second_shift_grad = jnp.sum(grad_final, axis=0)
    grad_outer = grad_second.astype(BF16)
    outer_bias_grad = jnp.sum(grad_outer.astype(F32), axis=0)
    grad_outer2 = pair_core(grad_outer, swap_core(grad_outer)).reshape(2 * tokens, WIDTH)
    grad_inner = (mm_t(grad_outer2, w_outer) * slope).astype(BF16)
    inner_bias_grad = jnp.sum(grad_inner.astype(F32), axis=0)
    grad_first = grad_second + sum_core(mm_t(grad_inner, w_inner))
    g_outer = scatter_chips(t_mm(active, grad_outer2), x, y, z)
    g_inner = scatter_chips(t_mm(first2, grad_inner), x, y, z)

    grad_residual = norm_backward(grad_first, first_normed, first_scale, f_gain)
    first_gain_grad = jnp.sum(grad_first * first_normed, axis=0)
    first_shift_grad = jnp.sum(grad_first, axis=0)
    grad_attended = grad_residual.astype(BF16)
    mixer_bias_grad = jnp.sum(grad_attended.astype(F32), axis=0)
    g_mixer = t_mm(context, grad_attended).reshape(chips, 2, rows, WIDTH)
    g_mixer = pick(g_mixer, core, 1) + swap_core(pick(g_mixer, 1 - core, 1).astype(BF16)).astype(
        F32
    )
    g_mixer = scatter_chips(g_mixer.reshape(chips * rows, WIDTH), x, y, z)

    grad_context = mm_t(grad_attended, w_mixer).astype(BF16).reshape(tokens, 2, HALF)
    got = swap_core(pick(grad_context, 1 - core, 1))
    grad_context2 = pair_core(pick(grad_context, core, 1), got).reshape(2 * tokens, HALF)

    grad_q, dkv = attend_back(q_scaled, grad_context2, o_exact, lse, kv)
    dkv = dkv.reshape(2, zs, 2 * tokens, WIDTH)
    dkv = dkv[0].astype(F32) + swap_y(dkv[1]).astype(F32)
    total = dkv[0]
    for k in range(1, zs):
        total = total + shift_z(dkv[k].astype(BF16), zs - k).astype(F32)
    grad_kv = total.astype(BF16)
    grad_qkv = jnp.concatenate([grad_q, grad_kv], axis=1)
    input_part = sum_core(mm_t(grad_qkv, w_qkv))
    input_grad = (grad_residual + input_part).astype(BF16)

    sums = jnp.sum(grad_qkv.astype(F32), axis=0)
    zero = jnp.zeros((2, HALF), F32)
    small = jnp.stack(
        [
            lax.dynamic_update_slice(zero, sums[None, :HALF], (core, 0)).reshape(WIDTH),
            lax.dynamic_update_slice(zero, sums[None, 2 * HALF :], (core, 0)).reshape(WIDTH),
            mixer_bias_grad,
            first_gain_grad,
            first_shift_grad,
            outer_bias_grad,
            second_gain_grad,
            second_shift_grad,
            head_grad,
        ],
        axis=1,
    )
    inner_small = lax.dynamic_update_slice(
        jnp.zeros((chips, 2, hidden), F32),
        inner_bias_grad.reshape(chips, 1, hidden),
        (0, core, 0),
    ).reshape(WIDTH, hidden // rows)
    small = jnp.concatenate([small, inner_small], axis=1)
    small = jnp.pad(small, ((0, 0), (0, AUX - small.shape[1])))
    g_qkv = scatter_chips(jnp.concatenate([t_mm(inputs2, grad_qkv), small], axis=1), x, y, z)

    g_all = jnp.concatenate([g_qkv, g_inner], axis=1).reshape(2, rows, -1)
    own, got = pick(g_all, core, 0), swap_core(pick(g_all, 1 - core, 0))
    wide = 3 * HALF
    small = own[:, wide : wide + AUX] + got[:, wide : wide + AUX]
    g_qkv = pair_core(own[:, :wide], got[:, :wide]).reshape(2, rows, 3, HALF)
    g_qkv = jnp.transpose(g_qkv, (2, 1, 0, 3)).reshape(3, rows, WIDTH)
    g_inner = pair_core(
        own[:, wide + AUX :].reshape(rows, chips, hidden),
        got[:, wide + AUX :].reshape(rows, chips, hidden),
        axis=2,
    ).reshape(rows, ff)
    g_ibias = small[:, 9 : 9 + hidden // rows].reshape(hidden)
    sm = jnp.transpose(small[:, :9])
    return (
        final_rows.astype(BF16)[None],
        term_weights[None],
        input_grad[None],
        g_qkv[0],
        sm[0],
        g_qkv[1],
        g_qkv[2],
        sm[1],
        g_mixer,
        sm[2],
        sm[3],
        sm[4],
        g_inner,
        g_ibias,
        g_outer,
        sm[5],
        sm[6],
        sm[7],
        sm[8],
    )


def solution(mesh):
    both = ("seq", "ctx")
    tok, mat, vec = P("seq", "ctx", None), P(both, None), P(both)
    term = P("seq", "ctx")
    in_specs = (
        tok, mat, vec, mat, mat, vec, mat, vec, vec, vec,
        mat, vec, mat, vec, vec, vec, vec, tok, term,
    )
    out_specs = (
        tok, term, tok, mat, vec, mat, mat, vec, mat, vec,
        vec, vec, mat, vec, mat, vec, vec, vec, vec,
    )
    return jax.shard_map(
        shards, mesh=mesh, in_specs=in_specs, out_specs=out_specs, check_vma=False
    )
```

```python
import functools
import math

import jax
import jax.numpy as jnp
from jax import lax
from jax.experimental import pallas as pl
from jax.experimental.pallas import tpu as pltpu
from jax.sharding import PartitionSpec as P

HEADS = 12
HD = 64
WIDTH = HEADS * HD
HALF = WIDTH // 2
NH = HEADS // 2
EPSILON = 1e-12
ROOT_HALF = 0.7071067811865476
GAUSS_FACTOR = 0.3989422804014327
F32 = jnp.float32
BF16 = jnp.bfloat16
AUX = 128


def mm(a, b):
    return lax.dot_general(a, b, (((1,), (0,)), ((), ())), preferred_element_type=F32)


def mm_t(a, b):
    return lax.dot_general(a, b, (((1,), (1,)), ((), ())), preferred_element_type=F32)


def t_mm(a, b):
    return lax.dot_general(a, b, (((0,), (0,)), ((), ())), preferred_element_type=F32)


def swap_ctx(value, bit):
    n = lax.axis_size("ctx")
    return lax.ppermute(value, "ctx", [(i, i ^ bit) for i in range(n)])


def swap_core(value):
    return swap_ctx(value, 1)


def swap_y(value):
    return swap_ctx(value, 2)


def swap_x(value):
    return lax.ppermute(value, "seq", [(0, 1), (1, 0)])


def shift_z(value, k):
    n = lax.axis_size("ctx")
    return lax.ppermute(value, "ctx", [(i, (i + 4 * k) % n) for i in range(n)])


def pick(value, index, axis):
    return lax.dynamic_index_in_dim(value, index, axis, keepdims=False)


def place():
    at = lax.axis_index("ctx")
    return lax.axis_index("seq"), at // 4, (at // 2) % 2, at % 2


def routes(order, x, z, y, zs, sign):
    out = []
    for outer in range(2):
        for inner in range(2):
            for k in range(zs):
                xr, yr = (outer, inner) if order == "x" else (inner, outer)
                there = (z + sign * k + zs) % zs
                out.append((outer, inner, k, ((x ^ xr) * zs + there) * 2 + (y ^ yr)))
    return out


def assemble(own, other, order):
    x, z, y, _ = place()
    zs, rows, cols = own.shape[1:]
    if rows % 16:
        full = jnp.stack([own, other])
        full = jnp.concatenate([full[:, :, :1], jnp.flip(full[:, :, 1:], 2)], axis=2)
        full = lax.dynamic_slice_in_dim(jnp.concatenate([full, full], axis=2), zs - z, zs, 2)
        bits = (x, y) if order == "x" else (y, x)
        for axis, bit in enumerate(bits):
            full = jnp.where(bit == 0, full, jnp.flip(full, axis))
        if order == "y":
            full = jnp.swapaxes(full, 0, 1)
        return jnp.swapaxes(full, 1, 2).reshape(4 * zs * rows, cols)

    def body(at_ref, own_ref, other_ref, out_ref, sems):
        copies = []
        for outer, inner, k, chip in routes(order, at_ref[0], at_ref[1], at_ref[2], zs, -1):
            source = (own_ref, other_ref)[outer]
            copies.append(
                pltpu.make_async_copy(
                    source.at[inner, k],
                    out_ref.at[pl.ds(pl.multiple_of(chip * rows, 16), rows)],
                    sems.at[(outer * 2 + inner) * zs + k],
                )
            )
        for copy in copies:
            copy.start()
        for copy in copies:
            copy.wait()

    return pl.pallas_call(
        body,
        in_specs=[
            pl.BlockSpec(memory_space=pltpu.SMEM),
            pl.BlockSpec(memory_space=pl.ANY),
            pl.BlockSpec(memory_space=pl.ANY),
        ],
        out_specs=pl.BlockSpec(memory_space=pl.ANY),
        out_shape=jax.ShapeDtypeStruct((4 * zs * rows, cols), own.dtype),
        scratch_shapes=[pltpu.SemaphoreType.DMA((4 * zs,))],
        name="assemble",
    )(jnp.stack([x, z, y]).astype(jnp.int32), own, other)


def split(part, order):
    x, z, y, _ = place()
    zs = lax.axis_size("ctx") // 4
    rows, cols = part.shape[0] // (4 * zs), part.shape[1]
    if rows % 16:
        full = jnp.swapaxes(part.reshape(2, zs, 2, rows, cols), 1, 2)
        full = lax.dynamic_slice_in_dim(jnp.concatenate([full, full], axis=2), z, zs, 2)
        for axis, bit in enumerate((x, y)):
            full = jnp.where(bit == 0, full, jnp.flip(full, axis))
        if order == "y":
            full = jnp.swapaxes(full, 0, 1)
        return full[0], full[1]

    def body(at_ref, part_ref, keep_ref, send_ref, sems):
        copies = []
        for outer, inner, k, chip in routes(order, at_ref[0], at_ref[1], at_ref[2], zs, 1):
            target = (keep_ref, send_ref)[outer]
            copies.append(
                pltpu.make_async_copy(
                    part_ref.at[pl.ds(pl.multiple_of(chip * rows, 16), rows)],
                    target.at[inner, k],
                    sems.at[(outer * 2 + inner) * zs + k],
                )
            )
        for copy in copies:
            copy.start()
        for copy in copies:
            copy.wait()

    return pl.pallas_call(
        body,
        in_specs=[
            pl.BlockSpec(memory_space=pltpu.SMEM),
            pl.BlockSpec(memory_space=pl.ANY),
        ],
        out_specs=[pl.BlockSpec(memory_space=pl.ANY)] * 2,
        out_shape=[jax.ShapeDtypeStruct((2, zs, rows, cols), part.dtype)] * 2,
        scratch_shapes=[pltpu.SemaphoreType.DMA((4 * zs,))],
        name="split",
    )(jnp.stack([x, z, y]).astype(jnp.int32), part)


def z_groups():
    n = lax.axis_size("ctx")
    return [[i + 4 * j for j in range(n // 4)] for i in range(4)]


def turned(blocks, start, forward):
    zs = blocks.shape[0]
    if not forward:
        blocks, start = jnp.flip(blocks, 0), zs - 1 - start
    return lax.dynamic_slice_in_dim(jnp.concatenate([blocks, blocks]), start, zs, 0)


def along_z(block):
    zs = lax.axis_size("ctx") // 4
    if zs > 4:
        every = lax.all_gather(block, "ctx", axis_index_groups=z_groups())
        return turned(every, lax.axis_index("ctx") // 4, False)
    return jnp.stack([block] + [shift_z(block, k) for k in range(1, zs)])


def fan_out(along, order):
    first, last = (swap_y, swap_x) if order == "x" else (swap_x, swap_y)
    own = jnp.stack([along, first(along)])
    return assemble(own, last(own), order)


def fan_in(part, order):
    keep, send = split(part, order)
    first, last = (swap_x, swap_y) if order == "x" else (swap_y, swap_x)
    got = first(send)
    away = last(keep[1] + got[1])
    return keep[0] + got[0] + away


def sum_z(along):
    zs = lax.axis_size("ctx") // 4
    if zs > 4:
        every = turned(along, (zs - lax.axis_index("ctx") // 4) % zs, True)
        every = lax.all_to_all(every, "ctx", 0, 0, axis_index_groups=z_groups())
        return jnp.sum(every.astype(F32), axis=0)
    total = along[0].astype(F32)
    for k in range(1, zs):
        total = total + shift_z(along[k], k).astype(F32)
    return total


def attend_kernel(
    xo_ref, xc_ref, w_ref, bias_ref, q_ref, kvo_ref, kvc_ref, o_ref, ctx_ref, lse_ref, m_s, l_s, acc_s
):
    step = pl.program_id(0)
    tokens = q_ref.shape[0] // 2
    wide = HALF + AUX

    @pl.when(step == 0)
    def _():
        for i, x_ref in enumerate((xo_ref, xc_ref)):
            rows = mm(x_ref[0:tokens, :], w_ref[:, :HALF]) + bias_ref[0:1, :HALF]
            q_ref[i * tokens : (i + 1) * tokens, :] = rows.astype(BF16) * BF16(0.125)
        m_s[...] = jnp.full(m_s.shape, -1e30, F32)
        l_s[...] = jnp.zeros(l_s.shape, F32)
        acc_s[...] = jnp.zeros(acc_s.shape, F32)

    for x_ref, kv_ref in ((xo_ref, kvo_ref), (xc_ref, kvc_ref)):
        kv_ref[...] = (mm(x_ref[...], w_ref[:, wide:]) + bias_ref[0:1, wide:]).astype(BF16)
        for h in range(NH):
            lo = h * HD
            qh = q_ref[:, lo : lo + HD]
            kh = kv_ref[:, lo : lo + HD]
            vh = kv_ref[:, HALF + lo : HALF + lo + HD]
            s = mm_t(kh, qh)
            before = m_s[h : h + 1, :]
            top = jnp.maximum(before, jnp.max(s, axis=0, keepdims=True))
            p = jnp.exp(s - top)
            factor = jnp.exp(before - top)
            m_s[h : h + 1, :] = top
            l_s[h : h + 1, :] = l_s[h : h + 1, :] * factor + jnp.sum(p, axis=0, keepdims=True)
            acc_s[lo : lo + HD, :] = acc_s[lo : lo + HD, :] * factor + t_mm(vh, p.astype(BF16))

    @pl.when(step == pl.num_programs(0) - 1)
    def _():
        lse_ref[...] = m_s[...] + jnp.log(l_s[...])
        for h in range(NH):
            lo = h * HD
            o_ref[lo : lo + HD, :] = acc_s[lo : lo + HD, :] / l_s[h : h + 1, :]
        ctx_ref[...] = jnp.transpose(o_ref[...]).astype(BF16)


def whole_spec(*shape):
    return pl.BlockSpec(shape, lambda i: (0,) * len(shape))


def attend(xo, xc, w, bias, tokens):
    keys = xo.shape[0]
    block = math.gcd(keys, 1024)
    rows = pl.BlockSpec((block, WIDTH), lambda i: (i, 0))
    return pl.pallas_call(
        attend_kernel,
        grid=(keys // block,),
        in_specs=[rows, rows, whole_spec(*w.shape), whole_spec(*bias.shape)],
        out_specs=[
            whole_spec(2 * tokens, HALF),
            rows,
            rows,
            whole_spec(HALF, 2 * tokens),
            whole_spec(2 * tokens, HALF),
            whole_spec(8, 2 * tokens),
        ],
        out_shape=[
            jax.ShapeDtypeStruct((2 * tokens, HALF), BF16),
            jax.ShapeDtypeStruct((keys, WIDTH), BF16),
            jax.ShapeDtypeStruct((keys, WIDTH), BF16),
            jax.ShapeDtypeStruct((HALF, 2 * tokens), F32),
            jax.ShapeDtypeStruct((2 * tokens, HALF), BF16),
            jax.ShapeDtypeStruct((8, 2 * tokens), F32),
        ],
        scratch_shapes=[
            pltpu.VMEM((8, 2 * tokens), F32),
            pltpu.VMEM((8, 2 * tokens), F32),
            pltpu.VMEM((HALF, 2 * tokens), F32),
        ],
        compiler_params=pltpu.CompilerParams(vmem_limit_bytes=40 * 2**20),
        cost_estimate=pl.CostEstimate(
            flops=16 * tokens * keys * HALF + 4 * keys * WIDTH * WIDTH,
            bytes_accessed=8 * keys * WIDTH,
            transcendentals=4 * tokens * keys * NH,
        ),
        name="attend",
    )(xo, xc, w, bias)


def attend_back_kernel(
    q_ref, go_ref, gc_ref, o_ref, lse_ref, kvo_ref, kvc_ref, dq_ref, do_ref, dc_ref, g_s, delta_s, acc_s
):
    step = pl.program_id(0)
    tokens = go_ref.shape[0]

    @pl.when(step == 0)
    def _():
        acc_s[...] = jnp.zeros(acc_s.shape, F32)
        g_s[:tokens, :] = go_ref[...]
        g_s[tokens:, :] = gc_ref[...]
        prod = jnp.transpose(g_s[...].astype(F32)) * o_ref[...]
        for h in range(NH):
            delta_s[h : h + 1, :] = jnp.sum(prod[h * HD : (h + 1) * HD, :], axis=0, keepdims=True)

    for kv_ref, out_ref in ((kvo_ref, do_ref), (kvc_ref, dc_ref)):
        held = []
        for h in range(NH):
            lo = h * HD
            qh = q_ref[:, lo : lo + HD]
            gh = g_s[:, lo : lo + HD]
            kh = kv_ref[:, lo : lo + HD]
            vh = kv_ref[:, HALF + lo : HALF + lo + HD]
            p = jnp.exp(mm_t(kh, qh) - lse_ref[h : h + 1, :])
            dp = mm_t(vh, gh)
            ds = (p * (dp - delta_s[h : h + 1, :])).astype(BF16)
            acc_s[lo : lo + HD, :] += t_mm(kh, ds)
            held.append((mm(ds, qh).astype(BF16), mm(p.astype(BF16), gh).astype(BF16)))
            if h % 2 == 1:
                (dk0, dv0), (dk1, dv1) = held
                held = []
                at = lo - HD
                out_ref[:, at : at + 2 * HD] = jnp.concatenate([dk0, dk1], axis=1)
                out_ref[:, HALF + at : HALF + at + 2 * HD] = jnp.concatenate([dv0, dv1], axis=1)

    @pl.when(step == pl.num_programs(0) - 1)
    def _():
        dq_ref[...] = jnp.transpose(acc_s[...] * 0.125).astype(BF16)


def attend_back(q, go, gc, o, lse, kvo, kvc):
    tokens = go.shape[0]
    keys = kvo.shape[0]
    block = math.gcd(keys, 1024)
    rows = pl.BlockSpec((block, WIDTH), lambda i: (i, 0))
    return pl.pallas_call(
        attend_back_kernel,
        grid=(keys // block,),
        in_specs=[
            whole_spec(2 * tokens, HALF),
            whole_spec(tokens, HALF),
            whole_spec(tokens, HALF),
            whole_spec(HALF, 2 * tokens),
            whole_spec(8, 2 * tokens),
            rows,
            rows,
        ],
        out_specs=[whole_spec(2 * tokens, HALF), rows, rows],
        out_shape=[
            jax.ShapeDtypeStruct((2 * tokens, HALF), BF16),
            jax.ShapeDtypeStruct((keys, WIDTH), BF16),
            jax.ShapeDtypeStruct((keys, WIDTH), BF16),
        ],
        scratch_shapes=[
            pltpu.VMEM((2 * tokens, HALF), BF16),
            pltpu.VMEM((8, 2 * tokens), F32),
            pltpu.VMEM((HALF, 2 * tokens), F32),
        ],
        compiler_params=pltpu.CompilerParams(vmem_limit_bytes=48 * 2**20),
        cost_estimate=pl.CostEstimate(
            flops=40 * tokens * keys * HALF,
            bytes_accessed=8 * keys * WIDTH,
            transcendentals=4 * tokens * keys * NH,
        ),
        name="attend_back",
    )(q, go, gc, o, lse, kvo, kvc)


def norm_forward(residual, gain, shift):
    center = residual - jnp.mean(residual, axis=-1, keepdims=True)
    scale = lax.rsqrt(jnp.mean(center * center, axis=-1, keepdims=True) + EPSILON)
    normed = center * scale
    return normed * gain + shift, normed, scale


def norm_backward(grad_out, normed, scale, gain):
    grad_normed = grad_out * gain
    return scale * (
        grad_normed
        - jnp.mean(grad_normed, axis=-1, keepdims=True)
        - normed * jnp.mean(grad_normed * normed, axis=-1, keepdims=True)
    )


def gelu_pair(u):
    cdf = 0.5 * (1.0 + lax.erf(u * ROOT_HALF))
    return u * cdf, cdf + u * jnp.exp(-0.5 * u * u) * GAUSS_FACTOR


def soft_plus(logits):
    return jnp.maximum(logits, 0.0) + jnp.log1p(jnp.exp(-jnp.abs(logits)))


def shards(
    layer_input,
    query_weight,
    query_bias,
    key_weight,
    value_weight,
    value_bias,
    mixer_weight,
    mixer_bias,
    first_gain,
    first_shift,
    inner_weight,
    inner_bias,
    outer_weight,
    outer_bias,
    second_gain,
    second_shift,
    head_weight,
    out_cotangent,
    term_cotangent,
):
    x, z, y, core = place()
    chips = lax.axis_size("ctx")
    zs = chips // 4
    inputs = layer_input[0]
    tokens = inputs.shape[0]
    rows = query_weight.shape[0]
    hidden = outer_weight.shape[0]
    ff = inner_weight.shape[1]
    wide = HALF + AUX
    cut = (3 * HALF + AUX) // 2

    def in_order(own, other, axis):
        first = jnp.where(core == 0, own, other)
        second = jnp.where(core == 0, other, own)
        return jnp.stack([first, second], axis=axis)

    vectors = jnp.stack(
        [
            query_bias,
            value_bias,
            mixer_bias,
            first_gain,
            first_shift,
            outer_bias,
            second_gain,
            second_shift,
            head_weight,
        ],
        axis=1,
    )
    aux = jnp.concatenate([vectors, inner_bias.reshape(rows, hidden // rows)], axis=1)
    aux = jnp.pad(aux, ((0, 0), (0, AUX - aux.shape[1])))
    three = (query_weight, key_weight, value_weight)
    inner_split = inner_weight.reshape(rows, chips, 2, hidden)

    def side_of(side):
        q, k, v = (lax.dynamic_slice_in_dim(w, side * HALF, HALF, 1) for w in three)
        return jnp.concatenate([q, aux, k, v], axis=1)

    qkv_block = in_order(side_of(core), swap_core(side_of(1 - core)), 0).reshape(2 * rows, -1)
    x_along = along_z(inputs)
    qkv_along = along_z(qkv_block)
    xo = jnp.concatenate([x_along, swap_y(x_along)]).reshape(2 * zs * tokens, WIDTH)
    xc = swap_core(xo)
    w_qkv = jnp.concatenate(
        [fan_out(qkv_along[:, :, :cut], "x"), fan_out(qkv_along[:, :, cut:], "y")], axis=1
    )

    inner_block = in_order(
        pick(inner_split, core, 2).reshape(rows, ff // 2),
        swap_core(pick(inner_split, 1 - core, 2).reshape(rows, ff // 2)),
        0,
    ).reshape(2 * rows, ff // 2)
    w_mixer_half = fan_out(along_z(mixer_weight), "x").reshape(chips, rows, WIDTH)
    w_mixer = in_order(w_mixer_half, swap_core(w_mixer_half), 1).reshape(WIDTH, WIDTH)
    w_inner = fan_out(along_z(inner_block), "x")
    w_outer = fan_out(along_z(outer_weight), "y")

    aux_full = w_qkv[:, HALF:wide]
    vecs = jnp.transpose(aux_full[:, :16].astype(F32))
    halves = lax.dynamic_slice_in_dim(vecs[:2], core * HALF, HALF, 1)
    bias = jnp.concatenate(
        [halves[:1], jnp.zeros((1, AUX + HALF), F32), halves[1:]], axis=1
    )
    m_bias, f_gain, f_shift = vecs[2], vecs[3], vecs[4]
    o_bias, s_gain, s_shift, head = vecs[5], vecs[6], vecs[7], vecs[8]
    i_bias = aux_full[:, 9 : 9 + hidden // rows].reshape(chips, 2, hidden)
    i_bias = pick(i_bias, core, 1).reshape(ff // 2).astype(F32)

    q_scaled, kvo, kvc, o_exact, context2, lse = attend(xo, xc, w_qkv, bias, tokens)
    got = swap_core(context2[tokens:])
    context = in_order(context2[:tokens], got, 1).reshape(tokens, WIDTH)

    attended = mm(context, w_mixer) + m_bias
    first_rows, first_normed, first_scale = norm_forward(
        inputs.astype(F32) + attended, f_gain, f_shift
    )
    first_low = first_rows.astype(BF16)
    first2 = jnp.concatenate([first_low, swap_core(first_low)])

    def sum_core(part):
        return part[:tokens] + swap_core(part[tokens:])

    inner_rows = mm(first2, w_inner) + i_bias
    act, slope = gelu_pair(inner_rows)
    active = act.astype(BF16)
    outer_rows = sum_core(mm(active, w_outer)) + o_bias
    final_rows, second_normed, second_scale = norm_forward(
        first_rows + outer_rows, s_gain, s_shift
    )
    logits = jnp.sum(final_rows * head, axis=-1)
    term_weights = soft_plus(logits)
    head_slope = term_cotangent[0] * jax.nn.sigmoid(logits)
    grad_final = out_cotangent[0].astype(F32) + head_slope[:, None] * head
    head_grad = jnp.sum(head_slope[:, None] * final_rows, axis=0)
    grad_second = norm_backward(grad_final, second_normed, second_scale, s_gain)
    second_gain_grad = jnp.sum(grad_final * second_normed, axis=0)
    second_shift_grad = jnp.sum(grad_final, axis=0)
    grad_outer = grad_second.astype(BF16)
    outer_bias_grad = jnp.sum(grad_outer.astype(F32), axis=0)
    grad_outer2 = jnp.concatenate([grad_outer, swap_core(grad_outer)])
    g_outer = fan_in(t_mm(active, grad_outer2).astype(BF16), "y")
    grad_inner = (mm_t(grad_outer2, w_outer) * slope).astype(BF16)
    inner_bias_grad = jnp.sum(grad_inner.astype(F32), axis=0)
    grad_first = grad_second + sum_core(mm_t(grad_inner, w_inner))
    g_inner = fan_in(t_mm(first2, grad_inner).astype(BF16), "x")

    grad_residual = norm_backward(grad_first, first_normed, first_scale, f_gain)
    first_gain_grad = jnp.sum(grad_first * first_normed, axis=0)
    first_shift_grad = jnp.sum(grad_first, axis=0)
    grad_attended = grad_residual.astype(BF16)
    mixer_bias_grad = jnp.sum(grad_attended.astype(F32), axis=0)
    grad_context = mm_t(grad_attended, w_mixer).astype(BF16).reshape(tokens, 2, HALF)
    got = swap_core(pick(grad_context, 1 - core, 1))
    grad_q, dkvo, dkvc = attend_back(
        q_scaled, pick(grad_context, core, 1), got, o_exact, lse, kvo, kvc
    )

    g_mixer = t_mm(context, grad_attended).astype(BF16).reshape(chips, 2, rows, WIDTH)
    g_mixer = pick(g_mixer, core, 1) + swap_core(pick(g_mixer, 1 - core, 1))
    g_mixer = fan_in(g_mixer.reshape(chips * rows, WIDTH), "x")

    w_kv = w_qkv[:, wide:]
    away = swap_core(mm_t(dkvc, w_kv).astype(BF16))
    part = (mm_t(dkvo, w_kv) + away.astype(F32)).astype(BF16).reshape(2, zs, tokens, WIDTH)
    part = part[0] + swap_y(part[1])
    total = sum_z(jnp.concatenate([part[:1], jnp.flip(part[1:], 0)]))
    input_grad = (
        grad_residual + sum_core(mm_t(grad_q, w_qkv[:, :HALF])) + total
    ).astype(BF16)

    zero = jnp.zeros((2, HALF), F32)
    q_sum = jnp.sum(grad_q.astype(F32), axis=0)
    v_sum = jnp.sum(dkvo[:, HALF:].astype(F32), axis=0) + jnp.sum(
        dkvc[:, HALF:].astype(F32), axis=0
    )
    small = jnp.stack(
        [
            lax.dynamic_update_slice(zero, q_sum[None], (core, 0)).reshape(WIDTH),
            lax.dynamic_update_slice(zero, v_sum[None], (core, 0)).reshape(WIDTH),
            mixer_bias_grad,
            first_gain_grad,
            first_shift_grad,
            outer_bias_grad,
            second_gain_grad,
            second_shift_grad,
            head_grad,
        ],
        axis=1,
    )
    inner_small = lax.dynamic_update_slice(
        jnp.zeros((chips, 2, hidden), F32),
        inner_bias_grad.reshape(chips, 1, hidden),
        (0, core, 0),
    ).reshape(WIDTH, hidden // rows)
    small = jnp.concatenate([small, inner_small], axis=1)
    small = jnp.pad(small, ((0, 0), (0, AUX - small.shape[1])))
    x_two = jnp.concatenate([inputs, xc[:tokens]])
    g_kv = t_mm(xo, dkvo) + t_mm(xc, dkvc)
    g_qkv = jnp.concatenate([t_mm(x_two, grad_q), small, g_kv], axis=1).astype(BF16)
    g_qkv = jnp.concatenate([fan_in(g_qkv[:, :cut], "x"), fan_in(g_qkv[:, cut:], "y")], axis=2)
    g_qkv = sum_z(g_qkv)
    g_outer = sum_z(g_outer)
    g_inner = sum_z(g_inner)
    g_mixer = sum_z(g_mixer)

    g_all = jnp.concatenate([g_qkv, g_inner], axis=1).reshape(2, rows, -1)
    own, got = pick(g_all, core, 0), swap_core(pick(g_all, 1 - core, 0))
    small = own[:, HALF:wide] + got[:, HALF:wide]

    def columns(lo):
        return in_order(own[:, lo : lo + HALF], got[:, lo : lo + HALF], 1).reshape(rows, WIDTH)

    g_inner = in_order(
        own[:, 2 * cut :].reshape(rows, chips, hidden),
        got[:, 2 * cut :].reshape(rows, chips, hidden),
        2,
    ).reshape(rows, ff)
    g_ibias = small[:, 9 : 9 + hidden // rows].reshape(hidden)
    sm = jnp.transpose(small[:, :9])
    return (
        final_rows.astype(BF16)[None],
        term_weights[None],
        input_grad[None],
        columns(0),
        sm[0],
        columns(wide),
        columns(wide + HALF),
        sm[1],
        g_mixer,
        sm[2],
        sm[3],
        sm[4],
        g_inner,
        g_ibias,
        g_outer,
        sm[5],
        sm[6],
        sm[7],
        sm[8],
    )


def solution(mesh):
    both = ("seq", "ctx")
    tok, mat, vec = P("seq", "ctx", None), P(both, None), P(both)
    term = P("seq", "ctx")
    in_specs = (
        tok, mat, vec, mat, mat, vec, mat, vec, vec, vec,
        mat, vec, mat, vec, vec, vec, vec, tok, term,
    )
    out_specs = (
        tok, term, tok, mat, vec, mat, mat, vec, mat, vec,
        vec, vec, mat, vec, mat, vec, vec, vec, vec,
    )
    return jax.shard_map(
        shards, mesh=mesh, in_specs=in_specs, out_specs=out_specs, check_vma=False
    )
```

```python
import math

import jax
import jax.numpy as jnp
from jax import lax
from jax.experimental import pallas as pl
from jax.experimental.pallas import tpu as pltpu
from jax.sharding import PartitionSpec as P

HEADS = 12
HD = 64
WIDTH = HEADS * HD
HALF = WIDTH // 2
NH = HEADS // 2
EPSILON = 1e-12
ROOT_HALF = 0.7071067811865476
GAUSS_FACTOR = 0.3989422804014327
F32 = jnp.float32
BF16 = jnp.bfloat16
AUX = 128
WIDE = HALF + AUX
MIB = 2**20


def mm(a, b):
    return lax.dot_general(a, b, (((1,), (0,)), ((), ())), preferred_element_type=F32)


def mm_t(a, b):
    return lax.dot_general(a, b, (((1,), (1,)), ((), ())), preferred_element_type=F32)


def t_mm(a, b):
    return lax.dot_general(a, b, (((0,), (0,)), ((), ())), preferred_element_type=F32)


def shape(dims, dtype):
    return jax.ShapeDtypeStruct(dims, dtype)


def swap_ctx(value, bit):
    n = lax.axis_size("ctx")
    return lax.ppermute(value, "ctx", [(i, i ^ bit) for i in range(n)])


def swap_core(value):
    return swap_ctx(value, 1)


def swap_y(value):
    return swap_ctx(value, 2)


def swap_x(value):
    return lax.ppermute(value, "seq", [(0, 1), (1, 0)])


def shift_z(value, k):
    n = lax.axis_size("ctx")
    return lax.ppermute(value, "ctx", [(i, (i + 4 * k) % n) for i in range(n)])


def place():
    at = lax.axis_index("ctx")
    return lax.axis_index("seq"), at // 4, (at // 2) % 2, at % 2


def z_groups():
    n = lax.axis_size("ctx")
    return [[i + 4 * j for j in range(n // 4)] for i in range(4)]


def turned(blocks, start, forward):
    zs = blocks.shape[0]
    if not forward:
        blocks, start = jnp.flip(blocks, 0), zs - 1 - start
    return lax.dynamic_slice_in_dim(jnp.concatenate([blocks, blocks]), start, zs, 0)


def along_z(block):
    zs = lax.axis_size("ctx") // 4
    if zs > 4:
        every = lax.all_gather(block, "ctx", axis_index_groups=z_groups())
        return turned(every, lax.axis_index("ctx") // 4, False)
    return jnp.stack([block] + [shift_z(block, k) for k in range(1, zs)])


def sum_z(along):
    zs = lax.axis_size("ctx") // 4
    if zs > 4:
        every = turned(along, (zs - lax.axis_index("ctx") // 4) % zs, True)
        every = lax.all_to_all(every, "ctx", 0, 0, axis_index_groups=z_groups())
        return jnp.sum(every.astype(F32), axis=0)
    total = along[0].astype(F32)
    for k in range(1, zs):
        total = total + shift_z(along[k], k).astype(F32)
    return total


def to_mesh_order(blocks):
    x, z, y, _ = place()
    zs = blocks.shape[2]
    blocks = jnp.concatenate([blocks[:, :, :1], jnp.flip(blocks[:, :, 1:], 2)], axis=2)
    blocks = lax.dynamic_slice_in_dim(jnp.concatenate([blocks, blocks], axis=2), zs - z, zs, 2)
    for axis, bit in enumerate((x, y)):
        blocks = jnp.where(bit == 0, blocks, jnp.flip(blocks, axis))
    return jnp.swapaxes(blocks, 1, 2)


def to_distance(blocks):
    x, z, y, _ = place()
    zs = blocks.shape[1]
    blocks = jnp.swapaxes(blocks, 1, 2)
    blocks = lax.dynamic_slice_in_dim(jnp.concatenate([blocks, blocks], axis=2), z, zs, 2)
    for axis, bit in enumerate((x, y)):
        blocks = jnp.where(bit == 0, blocks, jnp.flip(blocks, axis))
    return blocks


def after(value, *ready):
    return lax.optimization_barrier((value, *ready))[0]


def chip_of(here, xr, yr, k, zs):
    x, z, y, _ = here
    return ((x ^ xr) * zs + lax.rem(z + k + zs, zs)) * 2 + (y ^ yr)


def rows_at(chip, rows):
    return pl.ds(pl.multiple_of(chip * rows, 16), rows)


def kernel(body, args, outs, name, limit=14, scratch=(), flops=0, bytes_accessed=0):
    return pl.pallas_call(
        body,
        in_specs=[pl.BlockSpec(memory_space=pltpu.VMEM) for _ in args],
        out_specs=[pl.BlockSpec(memory_space=pltpu.VMEM) for _ in outs],
        out_shape=list(outs),
        scratch_shapes=list(scratch),
        compiler_params=pltpu.CompilerParams(vmem_limit_bytes=limit * MIB),
        cost_estimate=pl.CostEstimate(
            flops=flops, bytes_accessed=bytes_accessed, transcendentals=0
        ),
        name=name,
    )(*args)


def build_qkv(along, by_y, by_x, far_a, far_b):
    zs, rows, _ = along.shape
    cut = zs // 2
    ends = (0, WIDE, WIDE + WIDTH, WIDE + WIDTH + HALF)
    if rows % 16:
        far = jnp.concatenate([far_a, far_b])
        full = to_mesh_order(jnp.stack([along, by_y, by_x, far]).reshape(2, 2, zs, rows, -1))
        full = full.reshape(WIDTH, -1)
        return [full[:, lo:hi] for lo, hi in zip(ends, ends[1:])]

    def body(al_ref, y_ref, x_ref, fa_ref, fb_ref, *outs):
        here = place()
        for k in range(zs):
            far = (fa_ref, k) if k < cut else (fb_ref, k - cut)
            for xr, yr, (ref, i) in (
                (0, 0, (al_ref, k)),
                (0, 1, (y_ref, k)),
                (1, 0, (x_ref, k)),
                (1, 1, far),
            ):
                to = rows_at(chip_of(here, xr, yr, -k, zs), rows)
                for out, lo, hi in zip(outs, ends, ends[1:]):
                    out[to, :] = ref[i, :, lo:hi]

    return kernel(
        body,
        (along, by_y, by_x, far_a, far_b),
        [shape((WIDTH, hi - lo), BF16) for lo, hi in zip(ends, ends[1:])],
        "build_qkv",
        flops=10**6,
        bytes_accessed=4 * 10**6,
    )


def build_rest(along, by_y, by_x, far_a, far_b, rows, hidden):
    zs = along.shape[0]
    quarters = zs * 4 * hidden // HALF
    first = quarters * rows
    units = zs * 4 * hidden
    if rows % 16:
        far = jnp.concatenate([far_a, far_b], axis=1)
        full = to_mesh_order(
            jnp.stack([along, by_y, by_x, far]).reshape(2, 2, zs, -1, HALF)
        ).reshape(4 * zs, -1, HALF)
        w1 = jnp.swapaxes(full[:, :first].reshape(4 * zs, quarters, rows, HALF), 1, 2)
        w2 = jnp.swapaxes(full[:, first:].reshape(4 * zs, 2, hidden, HALF), 1, 2)
        return w1.reshape(WIDTH, units), w2.reshape(units, WIDTH)

    def body(al_ref, y_ref, x_ref, fa_ref, fb_ref, w1_ref, w2_ref):
        here = place()
        for k in range(zs):
            for xr, yr, ref, low, back in (
                (0, 0, al_ref, al_ref, 0),
                (0, 1, y_ref, y_ref, 0),
                (1, 0, x_ref, x_ref, 0),
                (1, 1, fa_ref, fb_ref, first),
            ):
                chip = chip_of(here, xr, yr, -k, zs)
                to, down = rows_at(chip, rows), rows_at(chip, hidden)
                for j in range(quarters):
                    w1_ref[to, j * HALF : (j + 1) * HALF] = ref[k, j * rows : (j + 1) * rows, :]
                for j in range(2):
                    lo = first + j * hidden - back
                    w2_ref[down, j * HALF : (j + 1) * HALF] = low[k, lo : lo + hidden, :]

    return kernel(
        body,
        (along, by_y, by_x, far_a, far_b),
        (shape((WIDTH, units), BF16), shape((units, WIDTH), BF16)),
        "build_rest",
        flops=10**6,
        bytes_accessed=10**7,
    )


def whole_spec(*dims):
    return pl.BlockSpec(dims, lambda i: (0,) * len(dims))


def attend_step(q_ref, kv_ref, m_ref, l_ref, acc_ref):
    for h in range(NH):
        lo = h * HD
        qh = q_ref[:, lo : lo + HD]
        kh = kv_ref[:, lo : lo + HD]
        vh = kv_ref[:, HALF + lo : HALF + lo + HD]
        s = mm_t(kh, qh)
        before = m_ref[h : h + 1, :]
        top = jnp.maximum(before, jnp.max(s, axis=0, keepdims=True))
        p = jnp.exp(s - top)
        factor = jnp.exp(before - top)
        m_ref[h : h + 1, :] = top
        l_ref[h : h + 1, :] = l_ref[h : h + 1, :] * factor + jnp.sum(p, axis=0, keepdims=True)
        acc_ref[lo : lo + HD, :] = acc_ref[lo : lo + HD, :] * factor + t_mm(vh, p.astype(BF16))


def keys_values(x_ref, w_ref, v_bias, kv_ref):
    kv_ref[:, :HALF] = mm(x_ref[...], w_ref[:, :HALF]).astype(BF16)
    kv_ref[:, HALF:] = (mm(x_ref[...], w_ref[:, HALF:]) + v_bias).astype(BF16)


def attend_cost(tokens, keys):
    return pl.CostEstimate(
        flops=8 * tokens * keys * HALF + 2 * keys * WIDTH * WIDTH,
        bytes_accessed=4 * keys * WIDTH,
        transcendentals=2 * tokens * keys * NH,
    )


def attend_first(own, got, xo, wq, wkv):
    tokens, keys = own.shape[0], xo.shape[0]
    block = math.gcd(keys, 1024)
    rows = pl.BlockSpec((block, WIDTH), lambda i: (i, 0))

    def body(o_ref, g_ref, x_ref, wq_ref, wkv_ref, q_ref, kv_ref, vec_ref, b_ref, m_ref, l_ref, acc_ref):
        @pl.when(pl.program_id(0) == 0)
        def _():
            core = place()[3]
            vecs = jnp.transpose(wq_ref[:, HALF:].astype(F32))
            vec_ref[...] = vecs[:16]
            b_ref[...] = jnp.where(core == 0, vecs[:8, :HALF], vecs[:8, HALF:])
            for i, ref in enumerate((o_ref, g_ref)):
                part = mm(ref[...], wq_ref[:, :HALF]) + b_ref[0:1, :]
                q_ref[i * tokens : (i + 1) * tokens, :] = part.astype(BF16) * BF16(0.125)
            m_ref[...] = jnp.full(m_ref.shape, -1e30, F32)
            l_ref[...] = jnp.zeros(l_ref.shape, F32)
            acc_ref[...] = jnp.zeros(acc_ref.shape, F32)

        keys_values(x_ref, wkv_ref, b_ref[1:2, :], kv_ref)
        attend_step(q_ref, kv_ref, m_ref, l_ref, acc_ref)

    return pl.pallas_call(
        body,
        grid=(keys // block,),
        in_specs=[
            whole_spec(tokens, WIDTH),
            whole_spec(tokens, WIDTH),
            rows,
            whole_spec(*wq.shape),
            whole_spec(*wkv.shape),
        ],
        out_specs=[
            whole_spec(2 * tokens, HALF),
            rows,
            whole_spec(16, WIDTH),
            whole_spec(8, HALF),
            whole_spec(8, 2 * tokens),
            whole_spec(8, 2 * tokens),
            whole_spec(HALF, 2 * tokens),
        ],
        out_shape=[
            shape((2 * tokens, HALF), BF16),
            shape((keys, WIDTH), BF16),
            shape((16, WIDTH), F32),
            shape((8, HALF), F32),
            shape((8, 2 * tokens), F32),
            shape((8, 2 * tokens), F32),
            shape((HALF, 2 * tokens), F32),
        ],
        compiler_params=pltpu.CompilerParams(vmem_limit_bytes=20 * MIB),
        cost_estimate=attend_cost(tokens, keys),
        name="attend_first",
    )(own, got, xo, wq, wkv)


def attend_last(q, xc, wkv, bias, top, total, weighted):
    tokens, keys = q.shape[0], xc.shape[0]
    block = math.gcd(keys, 1024)
    rows = pl.BlockSpec((block, WIDTH), lambda i: (i, 0))

    def body(q_ref, x_ref, w_ref, b_ref, mi_ref, li_ref, ai_ref, kv_ref, o_ref, ctx_ref, lse_ref, m_s, l_s, acc_s):
        @pl.when(pl.program_id(0) == 0)
        def _():
            m_s[...] = mi_ref[...]
            l_s[...] = li_ref[...]
            acc_s[...] = ai_ref[...]

        keys_values(x_ref, w_ref, b_ref[1:2, :], kv_ref)
        attend_step(q_ref, kv_ref, m_s, l_s, acc_s)

        @pl.when(pl.program_id(0) == pl.num_programs(0) - 1)
        def _():
            lse_ref[...] = m_s[...] + jnp.log(l_s[...])
            for h in range(NH):
                lo = h * HD
                o_ref[lo : lo + HD, :] = acc_s[lo : lo + HD, :] / l_s[h : h + 1, :]
            ctx_ref[...] = jnp.transpose(o_ref[...]).astype(BF16)

    return pl.pallas_call(
        body,
        grid=(keys // block,),
        in_specs=[
            whole_spec(tokens, HALF),
            rows,
            whole_spec(*wkv.shape),
            whole_spec(8, HALF),
            whole_spec(8, tokens),
            whole_spec(8, tokens),
            whole_spec(HALF, tokens),
        ],
        out_specs=[
            rows,
            whole_spec(HALF, tokens),
            whole_spec(tokens, HALF),
            whole_spec(8, tokens),
        ],
        out_shape=[
            shape((keys, WIDTH), BF16),
            shape((HALF, tokens), F32),
            shape((tokens, HALF), BF16),
            shape((8, tokens), F32),
        ],
        scratch_shapes=[
            pltpu.VMEM((8, tokens), F32),
            pltpu.VMEM((8, tokens), F32),
            pltpu.VMEM((HALF, tokens), F32),
        ],
        compiler_params=pltpu.CompilerParams(vmem_limit_bytes=20 * MIB),
        cost_estimate=attend_cost(tokens // 2, keys),
        name="attend_last",
    )(q, xc, wkv, bias, top, total, weighted)


def unit_places(chips, per, rows, core):
    units = chips * per * rows
    unit = lax.broadcasted_iota(jnp.int32, (WIDTH, units), 1)
    at = lax.broadcasted_iota(jnp.int32, (WIDTH, units), 0)
    chip, inside = unit // (per * rows), lax.rem(unit, rows)
    return (at == chip * (2 * rows) + core * rows + inside).astype(BF16)


def unit_bias(vecs, chips, per, rows):
    units = chips * per * rows

    def body(v_ref, out_ref):
        every = mm(v_ref[...].astype(BF16), unit_places(chips, per, rows, place()[3]))
        turn = lax.rem(lax.broadcasted_iota(jnp.int32, (16, units), 1) // rows, per)
        row = lax.broadcasted_iota(jnp.int32, (16, units), 0)
        out_ref[...] = column_sum(jnp.where(row == 9 + turn, every, 0.0))

    return kernel(body, (vecs,), (shape((1, units), F32),), "unit_bias", flops=10**8)[0]


def unit_rows(sums, chips, per, rows):
    units = chips * per * rows

    def body(s_ref, out_ref):
        turn = lax.rem(lax.broadcasted_iota(jnp.int32, (8, units), 1) // rows, per)
        row = lax.broadcasted_iota(jnp.int32, (8, units), 0)
        spread_out = jnp.where(row == turn, s_ref[...], 0.0).astype(BF16)
        out_ref[...] = mm_t(spread_out, unit_places(chips, per, rows, place()[3]))

    return kernel(body, (sums,), (shape((8, WIDTH), F32),), "unit_rows", flops=10**8)[0]


def norm_forward(residual, gain, shift):
    center = residual - jnp.mean(residual, axis=-1, keepdims=True)
    scale = lax.rsqrt(jnp.mean(center * center, axis=-1, keepdims=True) + EPSILON)
    normed = center * scale
    return normed * gain + shift, normed, scale


def norm_backward(grad_out, normed, scale, gain):
    grad_normed = grad_out * gain
    return scale * (
        grad_normed
        - jnp.mean(grad_normed, axis=-1, keepdims=True)
        - normed * jnp.mean(grad_normed * normed, axis=-1, keepdims=True)
    )


def column_sum(value):
    return jnp.sum(value, axis=0, keepdims=True)


def halves(core, own, other):
    left = jnp.where(core == 0, own, other)
    right = jnp.where(core == 0, other, own)
    return left, right


def mix(ctx, ctx_got, mixer_own, mixer_got, vecs, inputs):
    tokens = inputs.shape[0]

    def body(o_ref, g_ref, mo_ref, mg_ref, v_ref, x_ref, low_ref, row_ref, n_ref, s_ref):
        core = place()[3]
        mine = pl.ds(pl.multiple_of(core * HALF, HALF), HALF)
        others = pl.ds(pl.multiple_of((1 - core) * HALF, HALF), HALF)
        parts = [
            mm(o_ref[:tokens, :], ref[mine, :]) + mm(g_ref[tokens:, :], ref[others, :])
            for ref in (mo_ref, mg_ref)
        ]
        attended = jnp.concatenate(halves(core, *parts), axis=1) + v_ref[2:3, :]
        rows, normed, scale = norm_forward(
            x_ref[...].astype(F32) + attended, v_ref[3:4, :], v_ref[4:5, :]
        )
        low_ref[...] = rows.astype(BF16)
        row_ref[...] = rows
        n_ref[...] = normed
        s_ref[...] = scale

    return kernel(
        body,
        (ctx, ctx_got, mixer_own, mixer_got, vecs, inputs),
        (
            shape((tokens, WIDTH), BF16),
            shape((tokens, WIDTH), F32),
            shape((tokens, WIDTH), F32),
            shape((tokens, 1), F32),
        ),
        "mix",
        flops=10**9,
        bytes_accessed=3 * 10**6,
    )


def feed(own, got, w_inner, i_bias, w_outer):
    tokens = own.shape[0]
    units = w_inner.shape[1]

    def body(o_ref, g_ref, w1_ref, b_ref, w2_ref, two_ref, act_ref, slope_ref, mine_ref, send_ref):
        two_ref[:tokens, :] = o_ref[...]
        two_ref[tokens:, :] = g_ref[...]
        u = mm(two_ref[...], w1_ref[...]) + b_ref[...]
        cdf = 0.5 * (1.0 + lax.erf(u * ROOT_HALF))
        slope_ref[...] = cdf + u * jnp.exp(-0.5 * u * u) * GAUSS_FACTOR
        act_ref[...] = (u * cdf).astype(BF16)
        part = mm(act_ref[...], w2_ref[...])
        mine_ref[...] = part[:tokens]
        send_ref[...] = part[tokens:]

    return kernel(
        body,
        (own, got, w_inner, i_bias, w_outer),
        (
            shape((2 * tokens, WIDTH), BF16),
            shape((2 * tokens, units), BF16),
            shape((2 * tokens, units), F32),
            shape((tokens, WIDTH), F32),
            shape((tokens, WIDTH), F32),
        ),
        "feed",
        flops=3 * 10**9,
        bytes_accessed=8 * 10**6,
    )


def crown(mine, got, first_rows, vecs, out_cot, term_cot):
    tokens = mine.shape[0]

    def body(
        m_ref, g_ref, f_ref, v_ref, oc_ref, tc_ref, out_ref, term_ref, gs_ref, go_ref, sum_ref
    ):
        gain = v_ref[6:7, :]
        head = v_ref[8:9, :]
        outer = m_ref[...] + g_ref[...] + v_ref[5:6, :]
        rows, normed, scale = norm_forward(f_ref[...] + outer, gain, v_ref[7:8, :])
        out_ref[...] = rows.astype(BF16)
        logits = jnp.sum(rows * head, axis=-1, keepdims=True)
        small = jnp.exp(-jnp.abs(logits))
        term = jnp.maximum(logits, 0.0) + jnp.log1p(small)
        term_ref[...] = jnp.transpose(jnp.broadcast_to(term, (tokens, 128)))[0:1, :]
        sig = jnp.where(logits >= 0.0, 1.0, small) / (1.0 + small)
        cot = jnp.transpose(jnp.broadcast_to(tc_ref[...], (128, tokens)))[:, 0:1]
        slope = cot * sig
        grad_final = oc_ref[...].astype(F32) + slope * head
        grad = norm_backward(grad_final, normed, scale, gain)
        low = grad.astype(BF16)
        gs_ref[...] = grad
        go_ref[...] = low
        sum_ref[...] = jnp.concatenate(
            [
                column_sum(low.astype(F32)),
                column_sum(grad_final * normed),
                column_sum(grad_final),
                column_sum(slope * rows),
                jnp.zeros((4, WIDTH), F32),
            ],
            axis=0,
        )

    return kernel(
        body,
        (mine, got, first_rows, vecs, out_cot, term_cot),
        (
            shape((tokens, WIDTH), BF16),
            shape((1, tokens), F32),
            shape((tokens, WIDTH), F32),
            shape((tokens, WIDTH), BF16),
            shape((8, WIDTH), F32),
        ),
        "crown",
        flops=10**8,
        bytes_accessed=3 * 10**6,
    )


def feed_back(own, got, slope, w_inner, w_outer):
    tokens = own.shape[0]
    units = w_inner.shape[1]

    def body(o_ref, g_ref, s_ref, w1_ref, w2_ref, two_ref, gi_ref, mine_ref, send_ref, sum_ref):
        two_ref[:tokens, :] = o_ref[...]
        two_ref[tokens:, :] = g_ref[...]
        low = (mm_t(two_ref[...], w2_ref[...]) * s_ref[...]).astype(BF16)
        gi_ref[...] = low
        sum_ref[...] = column_sum(low.astype(F32))
        part = mm_t(gi_ref[...], w1_ref[...])
        mine_ref[...] = part[:tokens]
        send_ref[...] = part[tokens:]

    return kernel(
        body,
        (own, got, slope, w_inner, w_outer),
        (
            shape((2 * tokens, WIDTH), BF16),
            shape((2 * tokens, units), BF16),
            shape((tokens, WIDTH), F32),
            shape((tokens, WIDTH), F32),
            shape((1, units), F32),
        ),
        "feed_back",
        flops=3 * 10**9,
        bytes_accessed=8 * 10**6,
    )


def mix_back(mine, got, grad_second, normed, scale, vecs, mixer_own, mixer_got):
    tokens = mine.shape[0]

    def body(
        m_ref, g_ref, gs_ref, n_ref, s_ref, v_ref, mo_ref, mg_ref, res_ref, keep_ref, send_ref, sum_ref
    ):
        core = place()[3]
        first = gs_ref[...] + m_ref[...] + g_ref[...]
        normal = n_ref[...]
        grad = norm_backward(first, normal, s_ref[...], v_ref[3:4, :])
        res_ref[...] = grad
        low = grad.astype(BF16)
        sum_ref[...] = jnp.concatenate(
            [
                column_sum(low.astype(F32)),
                column_sum(first * normal),
                column_sum(first),
                jnp.zeros((5, WIDTH), F32),
            ],
            axis=0,
        )
        mine_low, other_low = halves(core, low[:, :HALF], low[:, HALF:])
        ctx = (mm_t(mine_low, mo_ref[...]) + mm_t(other_low, mg_ref[...])).astype(BF16)
        mine_ctx, other_ctx = halves(core, ctx[:, :HALF], ctx[:, HALF:])
        keep_ref[:, :HALF] = mine_ctx
        keep_ref[:, HALF:] = mine_low
        send_ref[:, :HALF] = other_ctx
        send_ref[:, HALF:] = other_low

    return kernel(
        body,
        (mine, got, grad_second, normed, scale, vecs, mixer_own, mixer_got),
        (
            shape((tokens, WIDTH), F32),
            shape((tokens, WIDTH), BF16),
            shape((tokens, WIDTH), BF16),
            shape((8, WIDTH), F32),
        ),
        "mix_back",
        flops=10**9,
        bytes_accessed=4 * 10**6,
    )


def attend_back_step(q_ref, g_ref, lse_ref, delta_ref, kv_ref, out_ref, acc_ref, sum_ref):
    held = []
    for h in range(NH):
        lo = h * HD
        qh = q_ref[:, lo : lo + HD]
        gh = g_ref[:, lo : lo + HD]
        kh = kv_ref[:, lo : lo + HD]
        vh = kv_ref[:, HALF + lo : HALF + lo + HD]
        p = jnp.exp(mm_t(kh, qh) - lse_ref[h : h + 1, :])
        dp = mm_t(vh, gh)
        ds = (p * (dp - delta_ref[h : h + 1, :])).astype(BF16)
        acc_ref[lo : lo + HD, :] += t_mm(kh, ds)
        held.append((mm(ds, qh).astype(BF16), mm(p.astype(BF16), gh).astype(BF16)))
        if h % 2 == 1:
            (dk0, dv0), (dk1, dv1) = held
            held = []
            at = lo - HD
            dv = jnp.concatenate([dv0, dv1], axis=1)
            out_ref[:, at : at + 2 * HD] = jnp.concatenate([dk0, dk1], axis=1)
            out_ref[:, HALF + at : HALF + at + 2 * HD] = dv
            sum_ref[1:2, at : at + 2 * HD] += column_sum(dv.astype(F32))


def attend_back_cost(tokens, keys):
    return pl.CostEstimate(
        flops=10 * tokens * keys * HALF,
        bytes_accessed=4 * keys * WIDTH,
        transcendentals=tokens * keys * NH,
    )


def attend_back_first(q, low, low_got, o, lse, kv):
    tokens, keys = q.shape[0], kv.shape[0]
    block = math.gcd(keys, 1024)
    rows = pl.BlockSpec((block, WIDTH), lambda i: (i, 0))

    def body(q_ref, go_ref, gc_ref, o_ref, lse_ref, kv_ref, d_ref, g_ref, delta_ref, acc_ref, sum_ref):
        @pl.when(pl.program_id(0) == 0)
        def _():
            acc_ref[...] = jnp.zeros(acc_ref.shape, F32)
            sum_ref[...] = jnp.zeros(sum_ref.shape, F32)
            g_ref[: tokens // 2, :] = go_ref[:, :HALF]
            g_ref[tokens // 2 :, :] = gc_ref[:, :HALF]
            prod = jnp.transpose(g_ref[...].astype(F32)) * o_ref[...]
            for h in range(NH):
                delta_ref[h : h + 1, :] = column_sum(prod[h * HD : (h + 1) * HD, :])

        attend_back_step(q_ref, g_ref, lse_ref, delta_ref, kv_ref, d_ref, acc_ref, sum_ref)

    return pl.pallas_call(
        body,
        grid=(keys // block,),
        in_specs=[
            whole_spec(tokens, HALF),
            whole_spec(tokens // 2, WIDTH),
            whole_spec(tokens // 2, WIDTH),
            whole_spec(HALF, tokens),
            whole_spec(8, tokens),
            rows,
        ],
        out_specs=[
            rows,
            whole_spec(tokens, HALF),
            whole_spec(8, tokens),
            whole_spec(HALF, tokens),
            whole_spec(8, HALF),
        ],
        out_shape=[
            shape((keys, WIDTH), BF16),
            shape((tokens, HALF), BF16),
            shape((8, tokens), F32),
            shape((HALF, tokens), F32),
            shape((8, HALF), F32),
        ],
        compiler_params=pltpu.CompilerParams(vmem_limit_bytes=20 * MIB),
        cost_estimate=attend_back_cost(tokens, keys),
        name="attend_back_first",
    )(q, low, low_got, o, lse, kv)


def attend_back_last(q, g, lse, delta, acc, sums, kv, wq):
    tokens, keys = q.shape[0], kv.shape[0]
    block = math.gcd(keys, 1024)
    rows = pl.BlockSpec((block, WIDTH), lambda i: (i, 0))

    def body(q_ref, g_ref, lse_ref, delta_ref, ai_ref, si_ref, kv_ref, w_ref, d_ref, dq_ref, sum_ref, send_ref, acc_s):
        @pl.when(pl.program_id(0) == 0)
        def _():
            acc_s[...] = ai_ref[...]
            sum_ref[...] = si_ref[...]

        attend_back_step(q_ref, g_ref, lse_ref, delta_ref, kv_ref, d_ref, acc_s, sum_ref)

        @pl.when(pl.program_id(0) == pl.num_programs(0) - 1)
        def _():
            dq = jnp.transpose(acc_s[...] * 0.125).astype(BF16)
            dq_ref[...] = dq
            sum_ref[0:1, :] = column_sum(dq.astype(F32))
            send_ref[...] = mm_t(dq[tokens // 2 :], w_ref[:, :HALF]).astype(BF16)

    return pl.pallas_call(
        body,
        grid=(keys // block,),
        in_specs=[
            whole_spec(tokens, HALF),
            whole_spec(tokens, HALF),
            whole_spec(8, tokens),
            whole_spec(8, tokens),
            whole_spec(HALF, tokens),
            whole_spec(8, HALF),
            rows,
            whole_spec(*wq.shape),
        ],
        out_specs=[
            rows,
            whole_spec(tokens, HALF),
            whole_spec(8, HALF),
            whole_spec(tokens // 2, WIDTH),
        ],
        out_shape=[
            shape((keys, WIDTH), BF16),
            shape((tokens, HALF), BF16),
            shape((8, HALF), F32),
            shape((tokens // 2, WIDTH), BF16),
        ],
        scratch_shapes=[pltpu.VMEM((HALF, tokens), F32)],
        compiler_params=pltpu.CompilerParams(vmem_limit_bytes=20 * MIB),
        cost_estimate=attend_back_cost(tokens, keys),
        name="attend_back_last",
    )(q, g, lse, delta, acc, sums, kv, wq)


def input_part_other(dkv, wkv):
    keys = dkv.shape[0]
    block = math.gcd(keys, 1024)
    rows = pl.BlockSpec((block, WIDTH), lambda i: (i, 0))

    def body(d_ref, w_ref, out_ref):
        out_ref[...] = mm_t(d_ref[...], w_ref[...]).astype(BF16)

    return pl.pallas_call(
        body,
        grid=(keys // block,),
        in_specs=[rows, whole_spec(*wkv.shape)],
        out_specs=rows,
        out_shape=shape((keys, WIDTH), BF16),
        compiler_params=pltpu.CompilerParams(vmem_limit_bytes=12 * MIB),
        cost_estimate=pl.CostEstimate(
            flops=2 * keys * WIDTH * WIDTH, bytes_accessed=4 * keys * WIDTH, transcendentals=0
        ),
        name="input_part_other",
    )(dkv, wkv)


def input_part_own(dkv, wkv, got, dq, wq, q_got):
    keys = dkv.shape[0]
    tokens = q_got.shape[0]
    block = math.gcd(keys // 2, 512)
    half = keys // 2 // block
    rows = pl.BlockSpec((block, WIDTH), lambda i: (i, 0))

    def body(d_ref, w_ref, g_ref, dq_ref, wq_ref, qg_ref, keep_ref, send_ref, part_s):
        step = pl.program_id(0)
        part_s[...] = mm_t(d_ref[...], w_ref[...]) + g_ref[...].astype(F32)

        @pl.when(step == 0)
        def _():
            part_s[:tokens, :] += mm_t(dq_ref[:tokens, :], wq_ref[:, :HALF]) + qg_ref[...].astype(
                F32
            )

        @pl.when(step < half)
        def _():
            keep_ref[...] = part_s[...].astype(BF16)

        @pl.when(step >= half)
        def _():
            send_ref[...] = part_s[...].astype(BF16)

    return pl.pallas_call(
        body,
        grid=(2 * half,),
        in_specs=[
            rows,
            whole_spec(*wkv.shape),
            rows,
            whole_spec(*dq.shape),
            whole_spec(*wq.shape),
            whole_spec(*q_got.shape),
        ],
        out_specs=[
            pl.BlockSpec((block, WIDTH), lambda i: (jnp.minimum(i, half - 1), 0)),
            pl.BlockSpec((block, WIDTH), lambda i: (jnp.maximum(i - half, 0), 0)),
        ],
        out_shape=[shape((keys // 2, WIDTH), BF16)] * 2,
        scratch_shapes=[pltpu.VMEM((block, WIDTH), F32)],
        compiler_params=pltpu.CompilerParams(vmem_limit_bytes=12 * MIB),
        cost_estimate=pl.CostEstimate(
            flops=2 * keys * WIDTH * WIDTH, bytes_accessed=4 * keys * WIDTH, transcendentals=0
        ),
        name="input_part_own",
    )(dkv, wkv, got, dq, wq, q_got)


def spread(zs, rows, cols, args, fill, name, scratch):
    count = len(args)

    def body(*refs):
        ins, outs, part_s = refs[:count], refs[count : count + 4], refs[-1]
        fill(ins, part_s)
        here = place()
        for k in range(zs):
            for i, out in enumerate(outs):
                chip = chip_of(here, i // 2, i % 2, k, zs)
                out[k] = part_s[rows_at(chip, rows), :]

    return kernel(
        body,
        args,
        [shape((zs, rows, cols), BF16)] * 4,
        name,
        scratch=[pltpu.VMEM(scratch, BF16)],
        flops=2 * 10**9,
        bytes_accessed=6 * 10**6,
    )


def spread_product(left, right, zs):
    total, cols = left.shape[1], right.shape[1]
    rows = total // (4 * zs)
    if rows % 16:
        full = t_mm(left, right).astype(BF16).reshape(2, zs, 2, rows, cols)
        full = to_distance(full).reshape(4, zs, rows, cols)
        return full[0], full[1], full[2], full[3]

    def fill(ins, part_s):
        part_s[...] = t_mm(ins[0][...], ins[1][...]).astype(BF16)

    return spread(zs, rows, cols, (left, right), fill, "spread", (total, cols))


def spread_qkv(zs, x_own, x_got, dq, qv, mid, top, unit, g_kv, ctx, ctx_got, low, low_got):
    tokens = x_own.shape[0]
    rows = WIDTH // (4 * zs)
    cols = WIDE + WIDTH + HALF

    def fill(ins, part_s):
        xo, xg, dq_r, qv_r, mid_r, top_r, unit_r, kv_r, c_r, cg_r, l_r, lg_r = ins
        core = place()[3]
        part_s[:, :HALF] = (
            t_mm(xo[...], dq_r[:tokens, :]) + t_mm(xg[...], dq_r[tokens:, :])
        ).astype(BF16)
        zero = jnp.zeros((2, HALF), F32)
        sums = jnp.concatenate(
            [
                jnp.concatenate(halves(core, qv_r[0:2, :], zero), axis=1),
                mid_r[0:3, :],
                top_r[0:4, :],
                unit_r[...],
                jnp.zeros((AUX - 17, WIDTH), F32),
            ],
            axis=0,
        )
        part_s[:, HALF:WIDE] = jnp.transpose(sums).astype(BF16)
        part_s[:, WIDE : WIDE + WIDTH] = kv_r[...]
        lows = (l_r[:, HALF:], lg_r[:, HALF:])
        part_s[pl.ds(pl.multiple_of(core * HALF, HALF), HALF), WIDE + WIDTH :] = (
            t_mm(c_r[:tokens, :], lows[0]) + t_mm(c_r[tokens:, :], lows[1])
        ).astype(BF16)
        part_s[pl.ds(pl.multiple_of((1 - core) * HALF, HALF), HALF), WIDE + WIDTH :] = (
            t_mm(cg_r[tokens:, :], lows[0]) + t_mm(cg_r[:tokens, :], lows[1])
        ).astype(BF16)

    args = (x_own, x_got, dq, qv, mid, top, unit, g_kv, ctx, ctx_got, low, low_got)
    if rows % 16 == 0:
        return spread(zs, rows, cols, args, fill, "spread_qkv", (WIDTH, cols))

    def body(*refs):
        fill(refs[:12], refs[12])

    full = kernel(body, args, [shape((WIDTH, cols), BF16)], "fill_qkv")[0]
    full = to_distance(full.reshape(2, zs, 2, rows, cols)).reshape(4, zs, rows, cols)
    return full[0], full[1], full[2], full[3]


def shards(
    layer_input,
    query_weight,
    query_bias,
    key_weight,
    value_weight,
    value_bias,
    mixer_weight,
    mixer_bias,
    first_gain,
    first_shift,
    inner_weight,
    inner_bias,
    outer_weight,
    outer_bias,
    second_gain,
    second_shift,
    head_weight,
    out_cotangent,
    term_cotangent,
):
    core = place()[3]
    chips = lax.axis_size("ctx")
    zs = chips // 4
    inputs = layer_input[0]
    tokens = inputs.shape[0]
    rows = query_weight.shape[0]
    hidden = outer_weight.shape[0]
    ff = inner_weight.shape[1]
    units = ff // 2
    per = hidden // rows

    def in_order(own, other, axis):
        return jnp.stack(halves(core, own, other), axis=axis)

    aux = jnp.concatenate(
        [
            query_bias,
            value_bias,
            mixer_bias,
            first_gain,
            first_shift,
            outer_bias,
            second_gain,
            second_shift,
            head_weight,
            inner_bias,
        ]
    ).reshape(9 + per, rows)
    aux = jnp.transpose(jnp.pad(aux, ((0, AUX - 9 - per), (0, 0))))
    four = (query_weight, key_weight, value_weight, mixer_weight)

    def side_of(side):
        q, k, v, m = (lax.dynamic_slice_in_dim(w, side * HALF, HALF, 1) for w in four)
        return jnp.concatenate([q, aux, k, v, m], axis=1)

    x_along = along_z(inputs)
    x_got = swap_core(inputs)
    qkv_block = in_order(side_of(core), swap_core(side_of(1 - core)), 0)
    qkv = along_z(qkv_block.reshape(2 * rows, WIDE + WIDTH + HALF))
    xo = jnp.concatenate([x_along, swap_y(x_along)]).reshape(2 * zs * tokens, WIDTH)
    xc = swap_core(xo)
    qkv_y, qkv_x = swap_y(qkv), swap_x(qkv)
    wq, wkv, mixer_own = build_qkv(
        qkv, qkv_y, qkv_x, swap_x(qkv_y[: zs // 2]), swap_y(qkv_x[zs // 2 :])
    )
    mixer_got = swap_core(mixer_own)

    inner_split = inner_weight.reshape(rows, chips, 2, hidden)

    def inner_of(side):
        return pick(inner_split, side, 2).reshape(rows, units)

    both = in_order(inner_of(core), swap_core(inner_of(1 - core)), 0).reshape(2 * rows, units)
    quarters = units // HALF
    first = quarters * 2 * rows
    rest = jnp.concatenate(
        [both[:, j * HALF : (j + 1) * HALF] for j in range(quarters)]
        + [outer_weight[:, :HALF], outer_weight[:, HALF:]]
    )
    rest = along_z(after(rest, qkv))

    q_scaled, kvo, vecs, bias, top, total, weighted = attend_first(inputs, x_got, xo, wq, wkv)
    rest = after(rest, q_scaled)
    rest_y, rest_x = swap_y(rest), swap_x(rest)
    kvc, o_exact, ctx, lse = attend_last(q_scaled, xc, wkv, bias, top, total, weighted)
    w_inner, w_outer = build_rest(
        rest,
        rest_y,
        rest_x,
        swap_x(rest_y[:, :first]),
        swap_y(rest_x[:, first:]),
        2 * rows,
        hidden,
    )
    ctx_got = swap_core(ctx)
    i_bias = unit_bias(vecs, chips, per, rows)
    first_low, first_rows, first_normed, first_scale = mix(
        ctx, ctx_got, mixer_own, mixer_got, vecs, inputs
    )

    first2, active, slope, mine, away = feed(
        first_low, swap_core(first_low), w_inner, i_bias, w_outer
    )
    final_low, term, grad_second, grad_outer, top_sums = crown(
        mine, swap_core(away), first_rows, vecs, out_cotangent[0], term_cotangent
    )
    grad_outer2, grad_inner, mine, away, inner_sums = feed_back(
        grad_outer, swap_core(grad_outer), slope, w_inner, w_outer
    )
    got = swap_core(away)
    keep2, y2, x2, far2 = spread_product(active, grad_outer2, zs)
    far2 = swap_y(far2)
    keep1, y1, x1, far1 = spread_product(first2, grad_inner, zs)
    far1 = swap_x(far1)

    grad_residual, low, low_send, mid_sums = mix_back(
        mine, got, grad_second, first_normed, first_scale, vecs, mixer_own, mixer_got
    )
    low_got = swap_core(low_send)
    y2 = swap_y(after(y2, low_got))
    x1 = swap_x(after(x1, low_got))
    dkvc, g_both, delta, acc, qv_sums = attend_back_first(
        q_scaled, low, low_got, o_exact, lse, kvc
    )
    away = swap_core(input_part_other(dkvc, wkv))
    x2, y1 = after(x2 + far2, dkvc), after(y1 + far1, dkvc)
    x2 = swap_x(x2)
    y1 = swap_y(y1)
    dkvo, dq, qv_sums, q_away = attend_back_last(
        q_scaled, g_both, lse, delta, acc, qv_sums, kvo, wq
    )

    part, part_y = input_part_own(dkvo, wkv, away, dq, wq, swap_core(q_away))
    part = (part + swap_y(part_y)).reshape(zs, tokens, WIDTH)
    total = sum_z(jnp.concatenate([part[:1], jnp.flip(part[1:], 0)]))
    input_grad = (grad_residual + total).astype(BF16)

    g_kv = (t_mm(xo, dkvo) + t_mm(xc, dkvc)).astype(BF16)
    keep, yq, xq, far = spread_qkv(
        zs,
        inputs,
        x_got,
        dq,
        qv_sums,
        mid_sums,
        top_sums,
        unit_rows(inner_sums, chips, per, rows),
        g_kv,
        ctx,
        ctx_got,
        low,
        low_got,
    )
    cut = zs // 2
    far_a, far_b = swap_x(far[:cut]), swap_y(far[cut:])
    yq = swap_y(jnp.concatenate([yq[:cut] + far_a, yq[cut:]]))
    xq = swap_x(jnp.concatenate([xq[:cut], xq[cut:] + far_b]))
    g_outer = sum_z(keep2 + y2 + x2)
    g_inner = sum_z(keep1 + y1 + x1)
    g_qkv = sum_z(keep + yq + xq)

    g_all = jnp.concatenate([g_qkv, g_inner], axis=1).reshape(2, rows, -1)
    own, got = pick(g_all, core, 0), swap_core(pick(g_all, 1 - core, 0))

    def columns(lo):
        return jnp.concatenate(
            halves(core, own[:, lo : lo + HALF], got[:, lo : lo + HALF]), axis=1
        )

    at1 = WIDE + WIDTH + HALF
    g_inner = in_order(
        own[:, at1:].reshape(rows, chips, hidden), got[:, at1:].reshape(rows, chips, hidden), 2
    ).reshape(rows, ff)
    sm = jnp.transpose(own[:, HALF:WIDE] + got[:, HALF:WIDE])
    return (
        final_low[None],
        term,
        input_grad[None],
        columns(0),
        sm[0],
        columns(WIDE),
        columns(WIDE + HALF),
        sm[1],
        columns(WIDE + WIDTH),
        sm[2],
        sm[3],
        sm[4],
        g_inner,
        sm[9 : 9 + per].reshape(hidden),
        g_outer.reshape(hidden, WIDTH),
        sm[5],
        sm[6],
        sm[7],
        sm[8],
    )


def pick(value, index, axis):
    return lax.dynamic_index_in_dim(value, index, axis, keepdims=False)


def solution(mesh):
    both = ("seq", "ctx")
    tok, mat, vec = P("seq", "ctx", None), P(both, None), P(both)
    term = P("seq", "ctx")
    in_specs = (
        tok, mat, vec, mat, mat, vec, mat, vec, vec, vec,
        mat, vec, mat, vec, vec, vec, vec, tok, term,
    )
    out_specs = (
        tok, term, tok, mat, vec, mat, mat, vec, mat, vec,
        vec, vec, mat, vec, mat, vec, vec, vec, vec,
    )
    return jax.shard_map(
        shards, mesh=mesh, in_specs=in_specs, out_specs=out_specs, check_vma=False
    )
```

```python
import math

import jax
import jax.numpy as jnp
from jax import lax
from jax.experimental import pallas as pl
from jax.experimental.pallas import tpu as pltpu
from jax.sharding import PartitionSpec as P

HEADS = 12
HD = 64
WIDTH = HEADS * HD
HALF = WIDTH // 2
NH = HEADS // 2
EPSILON = 1e-12
ROOT_HALF = 0.7071067811865476
GAUSS_FACTOR = 0.3989422804014327
F32 = jnp.float32
BF16 = jnp.bfloat16
AUX = 128
WIDE = HALF + AUX
MIB = 2**20


def mm(a, b):
    return lax.dot_general(a, b, (((1,), (0,)), ((), ())), preferred_element_type=F32)


def mm_t(a, b):
    return lax.dot_general(a, b, (((1,), (1,)), ((), ())), preferred_element_type=F32)


def t_mm(a, b):
    return lax.dot_general(a, b, (((0,), (0,)), ((), ())), preferred_element_type=F32)


def shape(dims, dtype):
    return jax.ShapeDtypeStruct(dims, dtype)


def swap_ctx(value, bit):
    n = lax.axis_size("ctx")
    return lax.ppermute(value, "ctx", [(i, i ^ bit) for i in range(n)])


def swap_core(value):
    return swap_ctx(value, 1)


def swap_y(value):
    return swap_ctx(value, 2)


def swap_x(value):
    return lax.ppermute(value, "seq", [(0, 1), (1, 0)])


def shift_z(value, k):
    n = lax.axis_size("ctx")
    return lax.ppermute(value, "ctx", [(i, (i + 4 * k) % n) for i in range(n)])


def place():
    at = lax.axis_index("ctx")
    return lax.axis_index("seq"), at // 4, (at // 2) % 2, at % 2


def z_groups():
    n = lax.axis_size("ctx")
    return [[i + 4 * j for j in range(n // 4)] for i in range(4)]


def turned(blocks, start, forward):
    zs = blocks.shape[0]
    if not forward:
        blocks, start = jnp.flip(blocks, 0), zs - 1 - start
    return lax.dynamic_slice_in_dim(jnp.concatenate([blocks, blocks]), start, zs, 0)


def along_z_pieces(block):
    zs = lax.axis_size("ctx") // 4
    if zs > 4:
        every = lax.all_gather(block, "ctx", axis_index_groups=z_groups())
        return turned(every, lax.axis_index("ctx") // 4, False)
    return [block] + [shift_z(block, k) for k in range(1, zs)]


def far_out(by_y, by_x, row):
    return swap_x(by_y[:, :row]), swap_y(by_x[:, row:])


def sources(groups, row):
    arrays, where = [], {}
    for ks, *blocks in groups:
        at = len(arrays)
        arrays += blocks
        for i, k in enumerate(ks):
            last = ((at + 3, i), (at + 4, i, row))
            where[k] = (*(((at + j, i), (at + j, i, 0)) for j in range(3)), last)
    return arrays, where


def by_distance(arrays, where, row=0):
    def whole(first, rest):
        top = arrays[first[0]][first[1]][:row]
        return jnp.concatenate([top, arrays[rest[0]][rest[1]][row - rest[2] :]])

    blocks = [[whole(*side) for side in where[k]] for k in sorted(where)]
    full = jnp.stack([jnp.stack(four) for four in blocks], axis=1)
    return full.reshape(2, 2, *full.shape[1:])


def fan_far(by_y, by_x, far, row):
    if row == far.shape[1]:
        return by_y + swap_x(far), by_x
    over_x, over_y = swap_x(far[:, :row]), swap_y(far[:, row:])
    by_y = jnp.concatenate([by_y[:, :row] + over_x, by_y[:, row:]], axis=1)
    by_x = jnp.concatenate([by_x[:, :row], by_x[:, row:] + over_y], axis=1)
    return by_y, by_x


def sum_z(groups):
    zs = lax.axis_size("ctx") // 4
    if zs > 4:
        ((_, along),) = groups
        every = turned(along, (zs - lax.axis_index("ctx") // 4) % zs, True)
        every = lax.all_to_all(every, "ctx", 0, 0, axis_index_groups=z_groups())
        return jnp.sum(every.astype(F32), axis=0)
    total = None
    for ks, blocks in groups:
        for i, k in enumerate(ks):
            part = (blocks[i] if k == 0 else shift_z(blocks[i], k)).astype(F32)
            total = part if total is None else total + part
    return total


def to_mesh_order(blocks):
    x, z, y, _ = place()
    zs = blocks.shape[2]
    blocks = jnp.concatenate([blocks[:, :, :1], jnp.flip(blocks[:, :, 1:], 2)], axis=2)
    blocks = lax.dynamic_slice_in_dim(jnp.concatenate([blocks, blocks], axis=2), zs - z, zs, 2)
    for axis, bit in enumerate((x, y)):
        blocks = jnp.where(bit == 0, blocks, jnp.flip(blocks, axis))
    return jnp.swapaxes(blocks, 1, 2)


def to_distance(blocks):
    x, z, y, _ = place()
    zs = blocks.shape[1]
    blocks = jnp.swapaxes(blocks, 1, 2)
    blocks = lax.dynamic_slice_in_dim(jnp.concatenate([blocks, blocks], axis=2), z, zs, 2)
    for axis, bit in enumerate((x, y)):
        blocks = jnp.where(bit == 0, blocks, jnp.flip(blocks, axis))
    return blocks


def chip_of(here, xr, yr, k, zs):
    x, z, y, _ = here
    return ((x ^ xr) * zs + lax.rem(z + k + zs, zs)) * 2 + (y ^ yr)


def rows_at(chip, rows):
    return pl.ds(pl.multiple_of(chip * rows, 16), rows)


def kernel(body, args, outs, name, limit=14, scratch=(), flops=0, bytes_accessed=0):
    return pl.pallas_call(
        body,
        in_specs=[pl.BlockSpec(memory_space=pltpu.VMEM) for _ in args],
        out_specs=[pl.BlockSpec(memory_space=pltpu.VMEM) for _ in outs],
        out_shape=list(outs),
        scratch_shapes=list(scratch),
        compiler_params=pltpu.CompilerParams(vmem_limit_bytes=limit * MIB),
        cost_estimate=pl.CostEstimate(flops=1, bytes_accessed=1, transcendentals=0),
        name=name,
    )(*args)


def pack(weights, inner, vectors):
    rows, hidden = inner.shape[0], vectors[-1].shape[0]
    count = len(weights)
    every = (*weights, inner, *vectors)
    base = WIDE + WIDTH + HALF
    chips = inner.shape[1] // (2 * hidden)
    cols = base + chips * hidden

    def body(*refs):
        n = len(every)
        ins, (own_ref, send_ref), held = refs[:n], refs[n : n + 2], refs[n + 2 : 2 * n + 2]
        flat_s, sems = refs[-2:]
        copies = [pltpu.make_async_copy(i, h, sems.at[j]) for j, (i, h) in enumerate(zip(ins, held))]
        for copy in copies:
            copy.start()
        flat_s[...] = jnp.zeros(flat_s.shape, F32)
        for copy in copies:
            copy.wait()
        ws, inner_ref, vs = held[:count], held[count], held[count + 1 :]
        core = place()[3]
        at = 0
        for v in vs:
            for j in range(v.shape[0] // rows):
                flat_s[at : at + 1, :rows] = v[pl.ds(j * rows, rows)].astype(F32).reshape(1, rows)
                at += 1
        aux = jnp.transpose(flat_s[...])[:rows, :].astype(BF16)
        places = (0, WIDE, WIDE + HALF, WIDE + WIDTH)
        whole = inner_ref[...]
        units = [
            jnp.concatenate(
                [
                    whole[:, (2 * i + side) * hidden : (2 * i + side + 1) * hidden]
                    for i in range(chips)
                ],
                axis=1,
            )
            for side in range(2)
        ]
        for out, side in ((own_ref, core), (send_ref, 1 - core)):
            out[:, HALF:WIDE] = aux
            for w, lo in zip(ws, places):
                out[:, lo : lo + HALF] = jnp.where(side == 0, w[:, :HALF], w[:, HALF:])
            out[:, base:] = jnp.where(side == 0, units[0], units[1])

    return pl.pallas_call(
        body,
        in_specs=[pl.BlockSpec(memory_space=pl.ANY) for _ in every],
        out_specs=[pl.BlockSpec(memory_space=pltpu.VMEM)] * 2,
        out_shape=[shape((rows, cols), BF16)] * 2,
        scratch_shapes=[pltpu.VMEM(a.shape, BF16) for a in every]
        + [pltpu.VMEM((AUX, AUX), F32), pltpu.SemaphoreType.DMA((len(every),))],
        compiler_params=pltpu.CompilerParams(vmem_limit_bytes=56 * MIB),
        name="pack",
    )(*every)


def join(own, got, outer):
    rows, hidden = own.shape[0], outer.shape[0]
    base = WIDE + WIDTH + HALF
    quarters = (own.shape[1] - base) // HALF
    core = place()[3]
    both = jnp.concatenate(halves(core, own, got))
    return both[:, :base], jnp.concatenate(
        [both[:, base + j * HALF : base + (j + 1) * HALF] for j in range(quarters)]
        + [outer[:, :HALF], outer[:, HALF:]]
    )


def build_qkv(arrays, where, row):
    zs, rows = len(where), arrays[0].shape[1]
    ends = (0, WIDE, WIDE + WIDTH, WIDE + WIDTH + HALF)
    if rows % 16:
        full = to_mesh_order(by_distance(arrays, where, row)).reshape(WIDTH, -1)
        return [full[:, lo:hi] for lo, hi in zip(ends, ends[1:])]

    def body(*refs):
        outs = refs[len(arrays) :]
        here = place()
        for k in range(zs):
            for side, ((a, i), (b, n, back)) in enumerate(where[k]):
                at = chip_of(here, side // 2, side % 2, -k, zs) * rows
                top = pl.ds(pl.multiple_of(at, 16), row)
                low = pl.ds(pl.multiple_of(at + row, 16), rows - row)
                for out, lo, hi in zip(outs, ends, ends[1:]):
                    out[top, :] = refs[a][i, :row, lo:hi]
                    out[low, :] = refs[b][n, row - back : rows - back, lo:hi]

    return kernel(
        body,
        arrays,
        [shape((WIDTH, hi - lo), BF16) for lo, hi in zip(ends, ends[1:])],
        "build_qkv",
        flops=10**6,
        bytes_accessed=4 * 10**6,
    )


def build_rest(arrays, where, rows, hidden):
    zs = len(where)
    units = zs * 4 * hidden
    quarters = units // HALF
    first = quarters * rows
    if rows % 16:
        full = to_mesh_order(by_distance(arrays, where, first)).reshape(4 * zs, -1, HALF)
        w1 = jnp.swapaxes(full[:, :first].reshape(4 * zs, quarters, rows, HALF), 1, 2)
        w2 = jnp.swapaxes(full[:, first:].reshape(4 * zs, 2, hidden, HALF), 1, 2)
        return w1.reshape(WIDTH, units), w2.reshape(units, WIDTH)

    def body(*refs):
        w1_ref, w2_ref = refs[len(arrays) :]
        here = place()
        for k in range(zs):
            for side, ((a, i), (b, n, back)) in enumerate(where[k]):
                chip = chip_of(here, side // 2, side % 2, -k, zs)
                to, down = rows_at(chip, rows), rows_at(chip, hidden)
                for j in range(quarters):
                    w1_ref[to, j * HALF : (j + 1) * HALF] = refs[a][i, j * rows : (j + 1) * rows, :]
                for j in range(2):
                    lo = first + j * hidden - back
                    w2_ref[down, j * HALF : (j + 1) * HALF] = refs[b][n, lo : lo + hidden, :]

    return kernel(
        body,
        arrays,
        (shape((WIDTH, units), BF16), shape((units, WIDTH), BF16)),
        "build_rest",
        flops=10**6,
        bytes_accessed=10**7,
    )


def whole_spec(*dims):
    return pl.BlockSpec(dims, lambda i: (0,) * len(dims))


def attend_step(q_ref, kv_ref, m_ref, l_ref, acc_ref):
    for h in range(NH):
        lo = h * HD
        qh = q_ref[:, lo : lo + HD]
        kh = kv_ref[:, lo : lo + HD]
        vh = kv_ref[:, HALF + lo : HALF + lo + HD]
        s = mm_t(kh, qh)
        before = m_ref[h : h + 1, :]
        top = jnp.maximum(before, jnp.max(s, axis=0, keepdims=True))
        p = jnp.exp(s - top)
        factor = jnp.exp(before - top)
        m_ref[h : h + 1, :] = top
        l_ref[h : h + 1, :] = l_ref[h : h + 1, :] * factor + jnp.sum(p, axis=0, keepdims=True)
        acc_ref[lo : lo + HD, :] = acc_ref[lo : lo + HD, :] * factor + t_mm(vh, p.astype(BF16))


def keys_values(x_ref, w_ref, v_bias, kv_ref):
    kv_ref[:, :HALF] = mm(x_ref[...], w_ref[:, :HALF]).astype(BF16)
    kv_ref[:, HALF:] = (mm(x_ref[...], w_ref[:, HALF:]) + v_bias).astype(BF16)


def attend_cost(tokens, keys):
    return pl.CostEstimate(flops=1, bytes_accessed=1, transcendentals=0)


def attend_first(own, got, xo, wq, wkv):
    tokens, keys = own.shape[0], xo.shape[0]
    block = math.gcd(keys, 1024)
    rows = pl.BlockSpec((block, WIDTH), lambda i: (i, 0))

    def body(o_ref, g_ref, x_ref, wq_ref, wkv_ref, q_ref, kv_ref, vec_ref, b_ref, m_ref, l_ref, acc_ref):
        @pl.when(pl.program_id(0) == 0)
        def _():
            core = place()[3]
            vecs = jnp.transpose(wq_ref[:, HALF:].astype(F32))
            vec_ref[...] = vecs[:16]
            b_ref[...] = jnp.where(core == 0, vecs[:8, :HALF], vecs[:8, HALF:])
            for i, ref in enumerate((o_ref, g_ref)):
                part = mm(ref[...], wq_ref[:, :HALF]) + b_ref[0:1, :]
                q_ref[i * tokens : (i + 1) * tokens, :] = part.astype(BF16) * BF16(0.125)
            m_ref[...] = jnp.full(m_ref.shape, -1e30, F32)
            l_ref[...] = jnp.zeros(l_ref.shape, F32)
            acc_ref[...] = jnp.zeros(acc_ref.shape, F32)

        keys_values(x_ref, wkv_ref, b_ref[1:2, :], kv_ref)
        attend_step(q_ref, kv_ref, m_ref, l_ref, acc_ref)

    return pl.pallas_call(
        body,
        grid=(keys // block,),
        in_specs=[
            whole_spec(tokens, WIDTH),
            whole_spec(tokens, WIDTH),
            rows,
            whole_spec(*wq.shape),
            whole_spec(*wkv.shape),
        ],
        out_specs=[
            whole_spec(2 * tokens, HALF),
            rows,
            whole_spec(16, WIDTH),
            whole_spec(8, HALF),
            whole_spec(8, 2 * tokens),
            whole_spec(8, 2 * tokens),
            whole_spec(HALF, 2 * tokens),
        ],
        out_shape=[
            shape((2 * tokens, HALF), BF16),
            shape((keys, WIDTH), BF16),
            shape((16, WIDTH), F32),
            shape((8, HALF), F32),
            shape((8, 2 * tokens), F32),
            shape((8, 2 * tokens), F32),
            shape((HALF, 2 * tokens), F32),
        ],
        compiler_params=pltpu.CompilerParams(vmem_limit_bytes=20 * MIB),
        cost_estimate=attend_cost(tokens, keys),
        name="attend_first",
    )(own, got, xo, wq, wkv)


def attend_last(q, xc, wkv, bias, top, total, weighted):
    tokens, keys = q.shape[0], xc.shape[0]
    block = math.gcd(keys, 1024)
    rows = pl.BlockSpec((block, WIDTH), lambda i: (i, 0))

    def body(q_ref, x_ref, w_ref, b_ref, mi_ref, li_ref, ai_ref, kv_ref, o_ref, ctx_ref, lse_ref, m_s, l_s, acc_s):
        @pl.when(pl.program_id(0) == 0)
        def _():
            m_s[...] = mi_ref[...]
            l_s[...] = li_ref[...]
            acc_s[...] = ai_ref[...]

        keys_values(x_ref, w_ref, b_ref[1:2, :], kv_ref)
        attend_step(q_ref, kv_ref, m_s, l_s, acc_s)

        @pl.when(pl.program_id(0) == pl.num_programs(0) - 1)
        def _():
            lse_ref[...] = m_s[...] + jnp.log(l_s[...])
            for h in range(NH):
                lo = h * HD
                o_ref[lo : lo + HD, :] = acc_s[lo : lo + HD, :] / l_s[h : h + 1, :]
            ctx_ref[...] = jnp.transpose(o_ref[...]).astype(BF16)

    return pl.pallas_call(
        body,
        grid=(keys // block,),
        in_specs=[
            whole_spec(tokens, HALF),
            rows,
            whole_spec(*wkv.shape),
            whole_spec(8, HALF),
            whole_spec(8, tokens),
            whole_spec(8, tokens),
            whole_spec(HALF, tokens),
        ],
        out_specs=[
            rows,
            whole_spec(HALF, tokens),
            whole_spec(tokens, HALF),
            whole_spec(8, tokens),
        ],
        out_shape=[
            shape((keys, WIDTH), BF16),
            shape((HALF, tokens), F32),
            shape((tokens, HALF), BF16),
            shape((8, tokens), F32),
        ],
        scratch_shapes=[
            pltpu.VMEM((8, tokens), F32),
            pltpu.VMEM((8, tokens), F32),
            pltpu.VMEM((HALF, tokens), F32),
        ],
        compiler_params=pltpu.CompilerParams(vmem_limit_bytes=20 * MIB),
        cost_estimate=attend_cost(tokens // 2, keys),
        name="attend_last",
    )(q, xc, wkv, bias, top, total, weighted)


def unit_places(chips, per, rows, core):
    units = chips * per * rows
    unit = lax.broadcasted_iota(jnp.int32, (WIDTH, units), 1)
    at = lax.broadcasted_iota(jnp.int32, (WIDTH, units), 0)
    chip, inside = unit // (per * rows), lax.rem(unit, rows)
    return (at == chip * (2 * rows) + core * rows + inside).astype(BF16)


def unit_bias(vecs, chips, per, rows):
    units = chips * per * rows

    def body(v_ref, out_ref):
        every = mm(v_ref[...].astype(BF16), unit_places(chips, per, rows, place()[3]))
        turn = lax.rem(lax.broadcasted_iota(jnp.int32, (16, units), 1) // rows, per)
        row = lax.broadcasted_iota(jnp.int32, (16, units), 0)
        out_ref[...] = column_sum(jnp.where(row == 9 + turn, every, 0.0))

    return kernel(body, (vecs,), (shape((1, units), F32),), "unit_bias", flops=10**8)[0]


def unit_rows(sums, chips, per, rows):
    units = chips * per * rows

    def body(s_ref, out_ref):
        turn = lax.rem(lax.broadcasted_iota(jnp.int32, (8, units), 1) // rows, per)
        row = lax.broadcasted_iota(jnp.int32, (8, units), 0)
        spread_out = jnp.where(row == turn, s_ref[...], 0.0).astype(BF16)
        out_ref[...] = mm_t(spread_out, unit_places(chips, per, rows, place()[3]))

    return kernel(body, (sums,), (shape((8, WIDTH), F32),), "unit_rows", flops=10**8)[0]


def norm_forward(residual, gain, shift):
    center = residual - jnp.mean(residual, axis=-1, keepdims=True)
    scale = lax.rsqrt(jnp.mean(center * center, axis=-1, keepdims=True) + EPSILON)
    normed = center * scale
    return normed * gain + shift, normed, scale


def norm_backward(grad_out, normed, scale, gain):
    grad_normed = grad_out * gain
    return scale * (
        grad_normed
        - jnp.mean(grad_normed, axis=-1, keepdims=True)
        - normed * jnp.mean(grad_normed * normed, axis=-1, keepdims=True)
    )


def column_sum(value):
    return jnp.sum(value, axis=0, keepdims=True)


def halves(core, own, other):
    left = jnp.where(core == 0, own, other)
    right = jnp.where(core == 0, other, own)
    return left, right


def mix(ctx, ctx_got, mixer_own, mixer_got, vecs, inputs):
    tokens = inputs.shape[0]

    def body(o_ref, g_ref, mo_ref, mg_ref, v_ref, x_ref, low_ref, row_ref, n_ref, s_ref):
        core = place()[3]
        mine = pl.ds(pl.multiple_of(core * HALF, HALF), HALF)
        others = pl.ds(pl.multiple_of((1 - core) * HALF, HALF), HALF)
        parts = [
            mm(o_ref[:tokens, :], ref[mine, :]) + mm(g_ref[tokens:, :], ref[others, :])
            for ref in (mo_ref, mg_ref)
        ]
        attended = jnp.concatenate(halves(core, *parts), axis=1) + v_ref[2:3, :]
        rows, normed, scale = norm_forward(
            x_ref[...].astype(F32) + attended, v_ref[3:4, :], v_ref[4:5, :]
        )
        low_ref[...] = rows.astype(BF16)
        row_ref[...] = rows
        n_ref[...] = normed
        s_ref[...] = scale

    return kernel(
        body,
        (ctx, ctx_got, mixer_own, mixer_got, vecs, inputs),
        (
            shape((tokens, WIDTH), BF16),
            shape((tokens, WIDTH), F32),
            shape((tokens, WIDTH), F32),
            shape((tokens, 1), F32),
        ),
        "mix",
        flops=10**9,
        bytes_accessed=3 * 10**6,
    )


def feed(own, got, w_inner, i_bias, w_outer):
    tokens = own.shape[0]
    units = w_inner.shape[1]

    def body(o_ref, g_ref, w1_ref, b_ref, w2_ref, two_ref, act_ref, slope_ref, mine_ref, send_ref):
        two_ref[:tokens, :] = o_ref[...]
        two_ref[tokens:, :] = g_ref[...]
        u = mm(two_ref[...], w1_ref[...]) + b_ref[...]
        cdf = 0.5 * (1.0 + lax.erf(u * ROOT_HALF))
        slope_ref[...] = cdf + u * jnp.exp(-0.5 * u * u) * GAUSS_FACTOR
        act_ref[...] = (u * cdf).astype(BF16)
        part = mm(act_ref[...], w2_ref[...])
        mine_ref[...] = part[:tokens]
        send_ref[...] = part[tokens:]

    return kernel(
        body,
        (own, got, w_inner, i_bias, w_outer),
        (
            shape((2 * tokens, WIDTH), BF16),
            shape((2 * tokens, units), BF16),
            shape((2 * tokens, units), F32),
            shape((tokens, WIDTH), F32),
            shape((tokens, WIDTH), F32),
        ),
        "feed",
        flops=3 * 10**9,
        bytes_accessed=8 * 10**6,
    )


def crown(mine, got, first_rows, vecs, out_cot, term_cot):
    tokens = mine.shape[0]

    def body(
        m_ref, g_ref, f_ref, v_ref, oc_ref, tc_ref, out_ref, term_ref, gs_ref, go_ref, sum_ref
    ):
        gain = v_ref[6:7, :]
        head = v_ref[8:9, :]
        outer = m_ref[...] + g_ref[...] + v_ref[5:6, :]
        rows, normed, scale = norm_forward(f_ref[...] + outer, gain, v_ref[7:8, :])
        out_ref[...] = rows.astype(BF16)
        logits = jnp.sum(rows * head, axis=-1, keepdims=True)
        small = jnp.exp(-jnp.abs(logits))
        term = jnp.maximum(logits, 0.0) + jnp.log1p(small)
        term_ref[...] = jnp.transpose(jnp.broadcast_to(term, (tokens, 128)))[0:1, :]
        sig = jnp.where(logits >= 0.0, 1.0, small) / (1.0 + small)
        cot = jnp.transpose(jnp.broadcast_to(tc_ref[...], (128, tokens)))[:, 0:1]
        slope = cot * sig
        grad_final = oc_ref[...].astype(F32) + slope * head
        grad = norm_backward(grad_final, normed, scale, gain)
        low = grad.astype(BF16)
        gs_ref[...] = grad
        go_ref[...] = low
        sum_ref[...] = jnp.concatenate(
            [
                column_sum(low.astype(F32)),
                column_sum(grad_final * normed),
                column_sum(grad_final),
                column_sum(slope * rows),
                jnp.zeros((4, WIDTH), F32),
            ],
            axis=0,
        )

    return kernel(
        body,
        (mine, got, first_rows, vecs, out_cot, term_cot),
        (
            shape((tokens, WIDTH), BF16),
            shape((1, tokens), F32),
            shape((tokens, WIDTH), F32),
            shape((tokens, WIDTH), BF16),
            shape((8, WIDTH), F32),
        ),
        "crown",
        flops=10**8,
        bytes_accessed=3 * 10**6,
    )


def feed_back(own, got, slope, w_inner, w_outer):
    tokens = own.shape[0]
    units = w_inner.shape[1]

    def body(o_ref, g_ref, s_ref, w1_ref, w2_ref, two_ref, gi_ref, mine_ref, send_ref, sum_ref):
        two_ref[:tokens, :] = o_ref[...]
        two_ref[tokens:, :] = g_ref[...]
        low = (mm_t(two_ref[...], w2_ref[...]) * s_ref[...]).astype(BF16)
        gi_ref[...] = low
        sum_ref[...] = column_sum(low.astype(F32))
        part = mm_t(gi_ref[...], w1_ref[...])
        mine_ref[...] = part[:tokens]
        send_ref[...] = part[tokens:]

    return kernel(
        body,
        (own, got, slope, w_inner, w_outer),
        (
            shape((2 * tokens, WIDTH), BF16),
            shape((2 * tokens, units), BF16),
            shape((tokens, WIDTH), F32),
            shape((tokens, WIDTH), F32),
            shape((1, units), F32),
        ),
        "feed_back",
        flops=3 * 10**9,
        bytes_accessed=8 * 10**6,
    )


def mix_back(mine, got, grad_second, normed, scale, vecs, mixer_own, mixer_got):
    tokens = mine.shape[0]

    def body(
        m_ref, g_ref, gs_ref, n_ref, s_ref, v_ref, mo_ref, mg_ref, res_ref, keep_ref, send_ref, sum_ref
    ):
        core = place()[3]
        first = gs_ref[...] + m_ref[...] + g_ref[...]
        normal = n_ref[...]
        grad = norm_backward(first, normal, s_ref[...], v_ref[3:4, :])
        res_ref[...] = grad
        low = grad.astype(BF16)
        sum_ref[...] = jnp.concatenate(
            [
                column_sum(low.astype(F32)),
                column_sum(first * normal),
                column_sum(first),
                jnp.zeros((5, WIDTH), F32),
            ],
            axis=0,
        )
        mine_low, other_low = halves(core, low[:, :HALF], low[:, HALF:])
        ctx = (mm_t(mine_low, mo_ref[...]) + mm_t(other_low, mg_ref[...])).astype(BF16)
        mine_ctx, other_ctx = halves(core, ctx[:, :HALF], ctx[:, HALF:])
        keep_ref[:, :HALF] = mine_ctx
        keep_ref[:, HALF:] = mine_low
        send_ref[:, :HALF] = other_ctx
        send_ref[:, HALF:] = other_low

    return kernel(
        body,
        (mine, got, grad_second, normed, scale, vecs, mixer_own, mixer_got),
        (
            shape((tokens, WIDTH), F32),
            shape((tokens, WIDTH), BF16),
            shape((tokens, WIDTH), BF16),
            shape((8, WIDTH), F32),
        ),
        "mix_back",
        flops=10**9,
        bytes_accessed=4 * 10**6,
    )


def attend_back_step(q_ref, g_ref, lse_ref, delta_ref, kv_ref, out_ref, acc_ref, sum_ref):
    held = []
    for h in range(NH):
        lo = h * HD
        qh = q_ref[:, lo : lo + HD]
        gh = g_ref[:, lo : lo + HD]
        kh = kv_ref[:, lo : lo + HD]
        vh = kv_ref[:, HALF + lo : HALF + lo + HD]
        p = jnp.exp(mm_t(kh, qh) - lse_ref[h : h + 1, :])
        dp = mm_t(vh, gh)
        ds = (p * (dp - delta_ref[h : h + 1, :])).astype(BF16)
        acc_ref[lo : lo + HD, :] += t_mm(kh, ds)
        held.append((mm(ds, qh).astype(BF16), mm(p.astype(BF16), gh).astype(BF16)))
        if h % 2 == 1:
            (dk0, dv0), (dk1, dv1) = held
            held = []
            at = lo - HD
            dv = jnp.concatenate([dv0, dv1], axis=1)
            out_ref[:, at : at + 2 * HD] = jnp.concatenate([dk0, dk1], axis=1)
            out_ref[:, HALF + at : HALF + at + 2 * HD] = dv
            sum_ref[1:2, at : at + 2 * HD] += column_sum(dv.astype(F32))


def attend_back_cost(tokens, keys):
    return pl.CostEstimate(flops=1, bytes_accessed=1, transcendentals=0)


def attend_back_first(q, low, low_got, o, lse, kv):
    tokens, keys = q.shape[0], kv.shape[0]
    block = math.gcd(keys, 1024)
    rows = pl.BlockSpec((block, WIDTH), lambda i: (i, 0))

    def body(q_ref, go_ref, gc_ref, o_ref, lse_ref, kv_ref, d_ref, g_ref, delta_ref, acc_ref, sum_ref):
        @pl.when(pl.program_id(0) == 0)
        def _():
            acc_ref[...] = jnp.zeros(acc_ref.shape, F32)
            sum_ref[...] = jnp.zeros(sum_ref.shape, F32)
            g_ref[: tokens // 2, :] = go_ref[:, :HALF]
            g_ref[tokens // 2 :, :] = gc_ref[:, :HALF]
            prod = jnp.transpose(g_ref[...].astype(F32)) * o_ref[...]
            for h in range(NH):
                delta_ref[h : h + 1, :] = column_sum(prod[h * HD : (h + 1) * HD, :])

        attend_back_step(q_ref, g_ref, lse_ref, delta_ref, kv_ref, d_ref, acc_ref, sum_ref)

    return pl.pallas_call(
        body,
        grid=(keys // block,),
        in_specs=[
            whole_spec(tokens, HALF),
            whole_spec(tokens // 2, WIDTH),
            whole_spec(tokens // 2, WIDTH),
            whole_spec(HALF, tokens),
            whole_spec(8, tokens),
            rows,
        ],
        out_specs=[
            rows,
            whole_spec(tokens, HALF),
            whole_spec(8, tokens),
            whole_spec(HALF, tokens),
            whole_spec(8, HALF),
        ],
        out_shape=[
            shape((keys, WIDTH), BF16),
            shape((tokens, HALF), BF16),
            shape((8, tokens), F32),
            shape((HALF, tokens), F32),
            shape((8, HALF), F32),
        ],
        compiler_params=pltpu.CompilerParams(vmem_limit_bytes=20 * MIB),
        cost_estimate=attend_back_cost(tokens, keys),
        name="attend_back_first",
    )(q, low, low_got, o, lse, kv)


def attend_back_last(q, g, lse, delta, acc, sums, kv, wq):
    tokens, keys = q.shape[0], kv.shape[0]
    block = math.gcd(keys, 1024)
    rows = pl.BlockSpec((block, WIDTH), lambda i: (i, 0))

    def body(q_ref, g_ref, lse_ref, delta_ref, ai_ref, si_ref, kv_ref, w_ref, d_ref, dq_ref, sum_ref, send_ref, acc_s):
        @pl.when(pl.program_id(0) == 0)
        def _():
            acc_s[...] = ai_ref[...]
            sum_ref[...] = si_ref[...]

        attend_back_step(q_ref, g_ref, lse_ref, delta_ref, kv_ref, d_ref, acc_s, sum_ref)

        @pl.when(pl.program_id(0) == pl.num_programs(0) - 1)
        def _():
            dq = jnp.transpose(acc_s[...] * 0.125).astype(BF16)
            dq_ref[...] = dq
            sum_ref[0:1, :] = column_sum(dq.astype(F32))
            send_ref[...] = mm_t(dq[tokens // 2 :], w_ref[:, :HALF]).astype(BF16)

    return pl.pallas_call(
        body,
        grid=(keys // block,),
        in_specs=[
            whole_spec(tokens, HALF),
            whole_spec(tokens, HALF),
            whole_spec(8, tokens),
            whole_spec(8, tokens),
            whole_spec(HALF, tokens),
            whole_spec(8, HALF),
            rows,
            whole_spec(*wq.shape),
        ],
        out_specs=[
            rows,
            whole_spec(tokens, HALF),
            whole_spec(8, HALF),
            whole_spec(tokens // 2, WIDTH),
        ],
        out_shape=[
            shape((keys, WIDTH), BF16),
            shape((tokens, HALF), BF16),
            shape((8, HALF), F32),
            shape((tokens // 2, WIDTH), BF16),
        ],
        scratch_shapes=[pltpu.VMEM((HALF, tokens), F32)],
        compiler_params=pltpu.CompilerParams(vmem_limit_bytes=20 * MIB),
        cost_estimate=attend_back_cost(tokens, keys),
        name="attend_back_last",
    )(q, g, lse, delta, acc, sums, kv, wq)


def input_part_other(dkv, wkv):
    keys = dkv.shape[0]
    block = math.gcd(keys, 1024)
    rows = pl.BlockSpec((block, WIDTH), lambda i: (i, 0))

    def body(d_ref, w_ref, out_ref):
        out_ref[...] = mm_t(d_ref[...], w_ref[...]).astype(BF16)

    return pl.pallas_call(
        body,
        grid=(keys // block,),
        in_specs=[rows, whole_spec(*wkv.shape)],
        out_specs=rows,
        out_shape=shape((keys, WIDTH), BF16),
        compiler_params=pltpu.CompilerParams(vmem_limit_bytes=12 * MIB),
        cost_estimate=pl.CostEstimate(flops=1, bytes_accessed=1, transcendentals=0),
        name="input_part_other",
    )(dkv, wkv)


def input_part_own(dkv, wkv, got, dq, wq, q_got):
    keys = dkv.shape[0]
    tokens = q_got.shape[0]
    block = math.gcd(keys // 2, 512)
    half = keys // 2 // block
    rows = pl.BlockSpec((block, WIDTH), lambda i: (i, 0))

    def body(d_ref, w_ref, g_ref, dq_ref, wq_ref, qg_ref, keep_ref, send_ref, part_s):
        step = pl.program_id(0)
        part_s[...] = mm_t(d_ref[...], w_ref[...]) + g_ref[...].astype(F32)

        @pl.when(step == 0)
        def _():
            part_s[:tokens, :] += mm_t(dq_ref[:tokens, :], wq_ref[:, :HALF]) + qg_ref[...].astype(
                F32
            )

        @pl.when(step < half)
        def _():
            keep_ref[...] = part_s[...].astype(BF16)

        @pl.when(step >= half)
        def _():
            send_ref[...] = part_s[...].astype(BF16)

    return pl.pallas_call(
        body,
        grid=(2 * half,),
        in_specs=[
            rows,
            whole_spec(*wkv.shape),
            rows,
            whole_spec(*dq.shape),
            whole_spec(*wq.shape),
            whole_spec(*q_got.shape),
        ],
        out_specs=[
            pl.BlockSpec((block, WIDTH), lambda i: (jnp.minimum(i, half - 1), 0)),
            pl.BlockSpec((block, WIDTH), lambda i: (jnp.maximum(i - half, 0), 0)),
        ],
        out_shape=[shape((keys // 2, WIDTH), BF16)] * 2,
        scratch_shapes=[pltpu.VMEM((block, WIDTH), F32)],
        compiler_params=pltpu.CompilerParams(vmem_limit_bytes=12 * MIB),
        cost_estimate=pl.CostEstimate(flops=1, bytes_accessed=1, transcendentals=0),
        name="input_part_own",
    )(dkv, wkv, got, dq, wq, q_got)


def spread(zs, rows, cols, args, fill, name, scratch, limit=14):
    count = len(args)

    def body(*refs):
        ins, outs, held = refs[:count], refs[count : count + 4], refs[count + 4 :]
        write = fill(ins, held)
        here = place()
        for k in range(zs):
            for side in range(4):
                write(outs[side], k, chip_of(here, side // 2, side % 2, k, zs))

    return kernel(
        body,
        args,
        [shape((zs, rows, cols), BF16)] * 4,
        name,
        limit=limit,
        scratch=[pltpu.VMEM(dims, BF16) for dims in scratch],
        flops=2 * 10**9,
        bytes_accessed=6 * 10**6,
    )


def spread_slow(full, zs):
    full = to_distance(full.reshape(2, zs, 2, *full.shape[1:]))
    full = full.reshape(4, zs, *full.shape[3:])
    return full[0], full[1], full[2], full[3]


def spread_rest(first2, grad_inner, active, grad_outer2, zs):
    units = active.shape[1]
    rows, hidden = WIDTH // (4 * zs), units // (4 * zs)
    if rows % 16:
        w1 = t_mm(first2, grad_inner).astype(BF16).reshape(4 * zs, rows, units)
        w2 = t_mm(active, grad_outer2).astype(BF16).reshape(4 * zs, hidden, WIDTH)
        return spread_slow(jnp.concatenate([w1[:, :, :WIDTH], w1[:, :, WIDTH:], w2], axis=1), zs)

    def fill(ins, held):
        f_ref, gi_ref, a_ref, go_ref = ins
        held[0][...] = t_mm(f_ref[...], gi_ref[...]).astype(BF16)
        held[1][...] = t_mm(a_ref[...], go_ref[...]).astype(BF16)

        def write(out, n, chip):
            at = rows_at(chip, rows)
            out[n, :rows, :] = held[0][at, :WIDTH]
            out[n, rows : 2 * rows, :] = held[0][at, WIDTH:]
            out[n, 2 * rows :, :] = held[1][rows_at(chip, hidden), :]

        return write

    return spread(
        zs,
        2 * rows + hidden,
        WIDTH,
        (first2, grad_inner, active, grad_outer2),
        fill,
        "spread_rest",
        ((WIDTH, units), (units, WIDTH)),
    )


def spread_qkv(zs, x_own, x_got, dq, qv, mid, top, unit, g_kv, ctx, ctx_got, low, low_got):
    tokens = x_own.shape[0]
    rows = WIDTH // (4 * zs)
    cols = WIDE + WIDTH + HALF

    def fill(ins, held):
        part_s = held[0]
        xo, xg, dq_r, qv_r, mid_r, top_r, unit_r, c_r, cg_r, l_r, lg_r, *kv_rs = ins
        core = place()[3]
        part_s[:, :HALF] = (
            t_mm(xo[...], dq_r[:tokens, :]) + t_mm(xg[...], dq_r[tokens:, :])
        ).astype(BF16)
        zero = jnp.zeros((2, HALF), F32)
        sums = jnp.concatenate(
            [
                jnp.concatenate(halves(core, qv_r[0:2, :], zero), axis=1),
                mid_r[0:3, :],
                top_r[0:4, :],
                unit_r[...],
                jnp.zeros((AUX - 17, WIDTH), F32),
            ],
            axis=0,
        )
        part_s[:, HALF:WIDE] = jnp.transpose(sums).astype(BF16)
        if len(kv_rs) == 1:
            part_s[:, WIDE : WIDE + WIDTH] = kv_rs[0][...]
        else:
            xk, dk, xl, dl = kv_rs
            part_s[:, WIDE : WIDE + WIDTH] = (t_mm(xk[...], dk[...]) + t_mm(xl[...], dl[...])).astype(
                BF16
            )
        lows = (l_r[:, HALF:], lg_r[:, HALF:])
        part_s[pl.ds(pl.multiple_of(core * HALF, HALF), HALF), WIDE + WIDTH :] = (
            t_mm(c_r[:tokens, :], lows[0]) + t_mm(c_r[tokens:, :], lows[1])
        ).astype(BF16)
        part_s[pl.ds(pl.multiple_of((1 - core) * HALF, HALF), HALF), WIDE + WIDTH :] = (
            t_mm(cg_r[tokens:, :], lows[0]) + t_mm(cg_r[:tokens, :], lows[1])
        ).astype(BF16)

        def write(out, n, chip):
            out[n] = part_s[rows_at(chip, rows), :]

        return write

    args = (x_own, x_got, dq, qv, mid, top, unit, ctx, ctx_got, low, low_got, *g_kv)
    if rows % 16 == 0:
        return spread(zs, rows, cols, args, fill, "spread_qkv", ((WIDTH, cols),), 24)

    def body(*refs):
        fill(refs[:12], refs[12:])

    full = kernel(body, args, [shape((WIDTH, cols), BF16)], "fill_qkv")[0]
    return spread_slow(full.reshape(4 * zs, rows, cols), zs)


def finish_sums(qkv, rest, rows):
    count, cols = len(qkv), qkv[0].shape[1]
    hidden = rest[0].shape[0] - 4 * rows
    wide = cols + 2 * WIDTH

    def body(*refs):
        ins, (own_ref, send_ref, outer_ref, both_s) = refs[:-4], refs[-4:]
        core = place()[3]
        both_s[:, :cols] = sum(ref[...].astype(F32) for ref in ins[:count])
        low = sum(ref[...].astype(F32) for ref in ins[count:])
        both_s[:, cols : cols + WIDTH] = low[: 2 * rows]
        both_s[:, cols + WIDTH :] = low[2 * rows : 4 * rows]
        outer_ref[...] = low[4 * rows :]
        halves_of = (both_s[:rows, :], both_s[rows:, :])
        own_ref[...] = jnp.where(core == 0, *halves_of)
        send_ref[...] = jnp.where(core == 1, *halves_of)

    return kernel(
        body,
        (*qkv, *rest),
        [shape((rows, wide), F32)] * 2 + [shape((hidden, WIDTH), F32)],
        "finish_sums",
        limit=8,
        scratch=[pltpu.VMEM((2 * rows, wide), F32)],
    )


def finish_rows(own, got, hidden, per):
    rows = own.shape[0]
    base = WIDE + WIDTH + HALF
    chips = (own.shape[1] - base) // hidden

    def body(own_ref, got_ref, *outs):
        core = place()[3]
        left = jnp.where(core == 0, own_ref[...], got_ref[...])
        right = jnp.where(core == 0, got_ref[...], own_ref[...])
        for out, lo in zip(outs, (0, WIDE, WIDE + HALF, WIDE + WIDTH)):
            out[:, :HALF] = left[:, lo : lo + HALF]
            out[:, HALF:] = right[:, lo : lo + HALF]
        outs[4][...] = jnp.concatenate(
            [
                side[:, base + i * hidden : base + (i + 1) * hidden]
                for i in range(chips)
                for side in (left, right)
            ],
            axis=1,
        )
        small = left[:, HALF:WIDE] + right[:, HALF:WIDE]
        if rows < AUX:
            small = jnp.concatenate([small, jnp.zeros((AUX - rows, AUX), F32)], axis=0)
        small = jnp.transpose(small)
        for j in range(9):
            outs[5 + j][...] = small[j, :rows]
        for j in range(per):
            outs[14][pl.ds(j * rows, rows)] = small[9 + j, :rows]

    outs = kernel(
        body,
        (own, got),
        [shape((rows, WIDTH), F32)] * 4
        + [shape((rows, 2 * chips * hidden), F32)]
        + [shape((rows,), F32)] * 9
        + [shape((hidden,), F32)],
        "finish_rows",
        limit=8,
    )
    return (*outs[:5], outs[5:])


def shards(
    layer_input,
    query_weight,
    query_bias,
    key_weight,
    value_weight,
    value_bias,
    mixer_weight,
    mixer_bias,
    first_gain,
    first_shift,
    inner_weight,
    inner_bias,
    outer_weight,
    outer_bias,
    second_gain,
    second_shift,
    head_weight,
    out_cotangent,
    term_cotangent,
):
    core = place()[3]
    chips = lax.axis_size("ctx")
    zs = chips // 4
    inputs = layer_input[0]
    tokens = inputs.shape[0]
    rows = query_weight.shape[0]
    hidden = outer_weight.shape[0]
    ff = inner_weight.shape[1]
    units = ff // 2
    per = hidden // rows

    def in_order(own, other, axis):
        return jnp.stack(halves(core, own, other), axis=axis)

    own, send = pack(
        (query_weight, key_weight, value_weight, mixer_weight),
        inner_weight,
        (
            query_bias,
            value_bias,
            mixer_bias,
            first_gain,
            first_shift,
            outer_bias,
            second_gain,
            second_shift,
            head_weight,
            inner_bias,
        ),
    )
    block, rest = join(own, swap_core(send), outer_weight)
    x_got = swap_core(inputs)
    first = 2 * rows * (units // HALF)
    every = tuple(range(zs))
    barrier = lax.optimization_barrier
    part_row = 2 * rows // 3
    if zs == 4:
        near_y, near_x = swap_y(rest[None]), swap_x(rest[None])
        near_y, near_x, qkv = barrier((near_y, near_x, along_z_pieces(block)))
        x_own, first_piece = barrier((inputs, qkv[1]))
        qkv = jnp.stack([qkv[0], first_piece, *qkv[2:]])
        flat = qkv.reshape(first, -1)
        sent_y = swap_y(jnp.concatenate([flat, near_x[0, first:]], axis=1))
        sent_x = swap_x(jnp.concatenate([flat, near_y[0, :first]], axis=1))
        sent_y, sent_x, x_along = barrier((sent_y, sent_x, along_z_pieces(x_own)))
        x_along = jnp.stack(x_along)
        cols = flat.shape[1]
        qkv_y, qkv_x = (sent[:, :cols].reshape(qkv.shape) for sent in (sent_y, sent_x))
        near_far = [sent[None, :, cols:] for sent in (sent_x, sent_y)]
        rest_sent, x_along = barrier((rest, x_along))
        x_y, qkv_far, pieces = barrier(
            (swap_y(x_along), far_out(qkv_y, qkv_x, part_row), along_z_pieces(rest_sent))
        )
        pieces = jnp.stack(pieces[1:])
        rest_y, rest_x = swap_y(pieces), swap_x(pieces)
    else:
        qkv, x_along, pieces = (along_z_pieces(v) for v in (block, inputs, rest))
        x_y, rest_y, rest_x = swap_y(x_along), swap_y(pieces), swap_x(pieces)
        qkv_y, qkv_x = swap_y(qkv), swap_x(qkv)
        qkv_far = far_out(qkv_y, qkv_x, part_row)
    wq, wkv, mixer_own = build_qkv(
        *sources([(every, qkv, qkv_y, qkv_x, *qkv_far)], part_row), part_row
    )
    mixer_got = swap_core(mixer_own)
    xo = jnp.concatenate([x_along, x_y]).reshape(2 * zs * tokens, WIDTH)
    xc = swap_core(xo)

    q_scaled, kvo, vecs, bias, top, total, weighted = attend_first(inputs, x_got, xo, wq, wkv)
    kvc, o_exact, ctx, lse = attend_last(q_scaled, xc, wkv, bias, top, total, weighted)
    rest_y, rest_x, ctx = barrier((rest_y, rest_x, ctx))
    away = (pieces, rest_y, rest_x, *far_out(rest_y, rest_x, first))
    if zs == 4:
        away = [((0,), rest[None], near_y, near_x, *near_far), ((1, 2, 3), *away)]
    else:
        away = [(every, *away)]
    w_inner, w_outer = build_rest(*sources(away, first), 2 * rows, hidden)
    ctx_got = swap_core(ctx)
    i_bias = unit_bias(vecs, chips, per, rows)
    first_low, first_rows, first_normed, first_scale = mix(
        ctx, ctx_got, mixer_own, mixer_got, vecs, inputs
    )

    first2, active, slope, mine, away = feed(
        first_low, swap_core(first_low), w_inner, i_bias, w_outer
    )
    final_low, term, grad_second, grad_outer, top_sums = crown(
        mine, swap_core(away), first_rows, vecs, out_cotangent[0], term_cotangent
    )
    grad_outer2, grad_inner, mine, away, inner_sums = feed_back(
        grad_outer, swap_core(grad_outer), slope, w_inner, w_outer
    )
    got = swap_core(away)
    keep, rest_y, rest_x, far = spread_rest(first2, grad_inner, active, grad_outer2, zs)
    mine, keep, rest_y, rest_x, far = barrier((mine, keep, rest_y, rest_x, far))
    over_x, over_y = swap_x(far[:, : 4 * rows]), swap_y(far[:, 4 * rows :])

    grad_residual, low, low_send, mid_sums = mix_back(
        mine, got, grad_second, first_normed, first_scale, vecs, mixer_own, mixer_got
    )
    low_got = swap_core(low_send)
    dkvc, g_both, delta, acc, qv_sums = attend_back_first(
        q_scaled, low, low_got, o_exact, lse, kvc
    )
    over_x, over_y, dkvc, kvo = barrier((over_x, over_y, dkvc, kvo))
    away = swap_core(input_part_other(dkvc, wkv))
    rest_y = jnp.concatenate([rest_y[:, : 4 * rows] + over_x, rest_y[:, 4 * rows :]], axis=1)
    rest_x = jnp.concatenate([rest_x[:, : 4 * rows], rest_x[:, 4 * rows :] + over_y], axis=1)
    at = 1 if zs == 4 else 0
    got_y, got_x = swap_y(rest_y[at:]), swap_x(rest_x[at:])
    dkvo, dq, qv_sums, q_away = attend_back_last(
        q_scaled, g_both, lse, delta, acc, qv_sums, kvo, wq
    )

    part, part_y = input_part_own(dkvo, wkv, away, dq, wq, swap_core(q_away))
    dq, dkvo, part, part_y = barrier((dq, dkvo, part, part_y))
    if zs == 4:
        g_kv = (xo, dkvo, xc, dkvc)
    else:
        g_kv = ((t_mm(xo, dkvo) + t_mm(xc, dkvc)).astype(BF16),)
    g_qkv, qkv_y, qkv_x, qkv_far = spread_qkv(
        zs,
        inputs,
        x_got,
        dq,
        qv_sums,
        mid_sums,
        top_sums,
        unit_rows(inner_sums, chips, per, rows),
        g_kv,
        ctx,
        ctx_got,
        low,
        low_got,
    )
    part, part_y = part.reshape(zs, tokens, WIDTH), part_y.reshape(zs, tokens, WIDTH)
    if zs == 4:
        got_y, got_x, part_y, qkv_far = barrier((got_y, got_x, part_y, qkv_far))
        g_rest = keep[1:] + got_y + got_x
        qkv_far, got_part, g_rest = barrier(
            (
                swap_x(qkv_far),
                swap_y(part_y),
                [shift_z(g_rest[k - 1], k) for k in range(1, zs)],
            )
        )
        part = part + got_part
        qkv_x, qkv_far = barrier((qkv_x, qkv_far))
        got_y, got_x, parts = barrier(
            (
                swap_y(qkv_y + qkv_far),
                swap_x(qkv_x),
                [shift_z(part[k], zs - k) for k in range(1, zs)],
            )
        )
        near_y, near_x, parts = barrier((rest_y[:1], rest_x[:1], parts))
        total = part[0].astype(F32)
        for value in parts:
            total = total + value.astype(F32)
        g_qkv = g_qkv + got_y + got_x
        near_y, near_x, pieces = barrier(
            (
                swap_y(near_y),
                swap_x(near_x),
                [shift_z(g_qkv[k], k) for k in range(1, zs)],
            )
        )
        g_qkv = [g_qkv[0], *pieces]
        g_rest = [keep[0], near_y[0], near_x[0], *g_rest]
    else:
        g_rest = [sum_z([(every, keep + got_y + got_x)])]
        part = part + swap_y(part_y)
        total = sum_z([(every, jnp.concatenate([part[:1], jnp.flip(part[1:], 0)]))])
        qkv_y, qkv_x = fan_far(qkv_y, qkv_x, qkv_far, 2 * rows)
        g_qkv = [sum_z([(every, g_qkv + swap_y(qkv_y) + swap_x(qkv_x))])]
    input_grad = (grad_residual + total).astype(BF16)

    own, send, g_outer = finish_sums(g_qkv, g_rest, rows)
    g_query, g_key, g_value, g_mixer, g_inner, vectors = finish_rows(
        own, swap_core(send), hidden, per
    )
    return (
        final_low[None],
        term,
        input_grad[None],
        g_query,
        vectors[0],
        g_key,
        g_value,
        vectors[1],
        g_mixer,
        vectors[2],
        vectors[3],
        vectors[4],
        g_inner,
        vectors[9],
        g_outer,
        vectors[5],
        vectors[6],
        vectors[7],
        vectors[8],
    )


def pick(value, index, axis):
    return lax.dynamic_index_in_dim(value, index, axis, keepdims=False)


def solution(mesh):
    both = ("seq", "ctx")
    tok, mat, vec = P("seq", "ctx", None), P(both, None), P(both)
    term = P("seq", "ctx")
    in_specs = (
        tok, mat, vec, mat, mat, vec, mat, vec, vec, vec,
        mat, vec, mat, vec, vec, vec, vec, tok, term,
    )
    out_specs = (
        tok, term, tok, mat, vec, mat, mat, vec, mat, vec,
        vec, vec, mat, vec, mat, vec, vec, vec, vec,
    )
    return jax.shard_map(
        shards, mesh=mesh, in_specs=in_specs, out_specs=out_specs, check_vma=False
    )
```

```python
import math

import jax
import jax.numpy as jnp
from jax import lax
from jax.experimental import pallas as pl
from jax.experimental.pallas import tpu as pltpu
from jax.sharding import PartitionSpec as P

HEADS = 12
HD = 64
WIDTH = HEADS * HD
HALF = WIDTH // 2
NH = HEADS // 2
EPSILON = 1e-12
ROOT_HALF = 0.7071067811865476
GAUSS_FACTOR = 0.3989422804014327
F32 = jnp.float32
BF16 = jnp.bfloat16
AUX = 128
WIDE = HALF + AUX
MIB = 2**20


def mm(a, b):
    return lax.dot_general(a, b, (((1,), (0,)), ((), ())), preferred_element_type=F32)


def mm_t(a, b):
    return lax.dot_general(a, b, (((1,), (1,)), ((), ())), preferred_element_type=F32)


def t_mm(a, b):
    return lax.dot_general(a, b, (((0,), (0,)), ((), ())), preferred_element_type=F32)


def shape(dims, dtype):
    return jax.ShapeDtypeStruct(dims, dtype)


def swap_ctx(value, bit):
    n = lax.axis_size("ctx")
    return lax.ppermute(value, "ctx", [(i, i ^ bit) for i in range(n)])


def swap_core(value):
    return swap_ctx(value, 1)


def swap_y(value):
    return swap_ctx(value, 2)


def swap_x(value):
    return lax.ppermute(value, "seq", [(0, 1), (1, 0)])


def swap_z(value, k):
    return swap_ctx(value, 4 * k)


def place():
    at = lax.axis_index("ctx")
    return lax.axis_index("seq"), at // 4, (at // 2) % 2, at % 2


def z_groups():
    n = lax.axis_size("ctx")
    return [[i + 4 * j for j in range(n // 4)] for i in range(4)]


def turned(blocks, z, axis=0):
    zs = blocks.shape[axis]
    lead = blocks.shape[:axis]
    rest = blocks.shape[axis + 1 :]
    bit = 1
    while bit < zs:
        pairs = blocks.reshape(*lead, zs // (2 * bit), 2, bit, *rest)
        flipped = jnp.flip(pairs, len(lead) + 1)
        blocks = jnp.where((z & bit) == 0, pairs, flipped).reshape(*lead, zs, *rest)
        bit *= 2
    return blocks


def along_z_pieces(block):
    zs = lax.axis_size("ctx") // 4
    if zs > 4:
        every = lax.all_gather(block, "ctx", axis_index_groups=z_groups())
        return turned(every, lax.axis_index("ctx") // 4)
    return [block] + [swap_z(block, k) for k in range(1, zs)]


def far_out(by_y, by_x, row):
    return swap_x(by_y[:, :row]), swap_y(by_x[:, row:])


def sources(groups, row):
    arrays, where = [], {}
    for ks, *blocks in groups:
        at = len(arrays)
        arrays += blocks
        for i, k in enumerate(ks):
            last = ((at + 3, i), (at + 4, i, row))
            where[k] = (*(((at + j, i), (at + j, i, 0)) for j in range(3)), last)
    return arrays, where


def by_distance(arrays, where, row=0):
    def whole(first, rest):
        top = arrays[first[0]][first[1]][:row]
        return jnp.concatenate([top, arrays[rest[0]][rest[1]][row - rest[2] :]])

    blocks = [[whole(*side) for side in where[k]] for k in sorted(where)]
    full = jnp.stack([jnp.stack(four) for four in blocks], axis=1)
    return full.reshape(2, 2, *full.shape[1:])


def fan_far(by_y, by_x, far, row):
    if row == far.shape[1]:
        return by_y + swap_x(far), by_x
    over_x, over_y = swap_x(far[:, :row]), swap_y(far[:, row:])
    by_y = jnp.concatenate([by_y[:, :row] + over_x, by_y[:, row:]], axis=1)
    by_x = jnp.concatenate([by_x[:, :row], by_x[:, row:] + over_y], axis=1)
    return by_y, by_x


def sum_z(groups):
    zs = lax.axis_size("ctx") // 4
    if zs > 4:
        ((_, along),) = groups
        every = turned(along, lax.axis_index("ctx") // 4)
        every = lax.all_to_all(every, "ctx", 0, 0, axis_index_groups=z_groups())
        return jnp.sum(every.astype(F32), axis=0)
    total = None
    for ks, blocks in groups:
        for i, k in enumerate(ks):
            part = (blocks[i] if k == 0 else swap_z(blocks[i], k)).astype(F32)
            total = part if total is None else total + part
    return total


def to_mesh_order(blocks):
    x, z, y, _ = place()
    blocks = turned(blocks, z, 2)
    for axis, bit in enumerate((x, y)):
        blocks = jnp.where(bit == 0, blocks, jnp.flip(blocks, axis))
    return jnp.swapaxes(blocks, 1, 2)


def to_distance(blocks):
    x, z, y, _ = place()
    blocks = turned(jnp.swapaxes(blocks, 1, 2), z, 2)
    for axis, bit in enumerate((x, y)):
        blocks = jnp.where(bit == 0, blocks, jnp.flip(blocks, axis))
    return blocks


def chip_of(here, xr, yr, k, zs):
    x, z, y, _ = here
    return ((x ^ xr) * zs + (z ^ k)) * 2 + (y ^ yr)


def rows_at(chip, rows):
    return pl.ds(pl.multiple_of(chip * rows, 16), rows)


def kernel(body, args, outs, name, limit=14, scratch=(), flops=0, bytes_accessed=0):
    return pl.pallas_call(
        body,
        in_specs=[pl.BlockSpec(memory_space=pltpu.VMEM) for _ in args],
        out_specs=[pl.BlockSpec(memory_space=pltpu.VMEM) for _ in outs],
        out_shape=list(outs),
        scratch_shapes=list(scratch),
        compiler_params=pltpu.CompilerParams(vmem_limit_bytes=limit * MIB),
        cost_estimate=pl.CostEstimate(flops=1, bytes_accessed=1, transcendentals=0),
        name=name,
    )(*args)


def pack(weights, inner, vectors):
    rows, hidden = inner.shape[0], vectors[-1].shape[0]
    count = len(weights)
    every = (*weights, inner, *vectors)
    base = WIDE + WIDTH + HALF
    chips = inner.shape[1] // (2 * hidden)
    cols = base + chips * hidden

    def body(*refs):
        n = len(every)
        ins, (own_ref, send_ref), held = refs[:n], refs[n : n + 2], refs[n + 2 : 2 * n + 2]
        flat_s, sems = refs[-2:]
        copies = [pltpu.make_async_copy(i, h, sems.at[j]) for j, (i, h) in enumerate(zip(ins, held))]
        for copy in copies:
            copy.start()
        flat_s[...] = jnp.zeros(flat_s.shape, F32)
        for copy in copies:
            copy.wait()
        ws, inner_ref, vs = held[:count], held[count], held[count + 1 :]
        core = place()[3]
        at = 0
        for v in vs:
            for j in range(v.shape[0] // rows):
                flat_s[at : at + 1, :rows] = v[pl.ds(j * rows, rows)].astype(F32).reshape(1, rows)
                at += 1
        aux = jnp.transpose(flat_s[...])[:rows, :].astype(BF16)
        places = (0, WIDE, WIDE + HALF, WIDE + WIDTH)
        whole = inner_ref[...]
        units = [
            jnp.concatenate(
                [
                    whole[:, (2 * i + side) * hidden : (2 * i + side + 1) * hidden]
                    for i in range(chips)
                ],
                axis=1,
            )
            for side in range(2)
        ]
        for out, side in ((own_ref, core), (send_ref, 1 - core)):
            out[:, HALF:WIDE] = aux
            for w, lo in zip(ws, places):
                out[:, lo : lo + HALF] = jnp.where(side == 0, w[:, :HALF], w[:, HALF:])
            out[:, base:] = jnp.where(side == 0, units[0], units[1])

    return pl.pallas_call(
        body,
        in_specs=[pl.BlockSpec(memory_space=pl.ANY) for _ in every],
        out_specs=[pl.BlockSpec(memory_space=pltpu.VMEM)] * 2,
        out_shape=[shape((rows, cols), BF16)] * 2,
        scratch_shapes=[pltpu.VMEM(a.shape, BF16) for a in every]
        + [pltpu.VMEM((AUX, AUX), F32), pltpu.SemaphoreType.DMA((len(every),))],
        compiler_params=pltpu.CompilerParams(vmem_limit_bytes=56 * MIB),
        name="pack",
    )(*every)


def join(own, got, outer):
    rows, hidden = own.shape[0], outer.shape[0]
    base = WIDE + WIDTH + HALF
    quarters = (own.shape[1] - base) // HALF
    core = place()[3]
    both = jnp.concatenate(halves(core, own, got))
    return both[:, :base], jnp.concatenate(
        [both[:, base + j * HALF : base + (j + 1) * HALF] for j in range(quarters)]
        + [outer[:, :HALF], outer[:, HALF:]]
    )


def build_qkv(arrays, where, row):
    zs, rows = len(where), arrays[0].shape[1]
    ends = (0, WIDE, WIDE + WIDTH, WIDE + WIDTH + HALF)
    if rows % 16:
        full = to_mesh_order(by_distance(arrays, where, row)).reshape(WIDTH, -1)
        return [full[:, lo:hi] for lo, hi in zip(ends, ends[1:])]

    def body(*refs):
        outs = refs[len(arrays) :]
        here = place()
        for k in range(zs):
            for side, ((a, i), (b, n, back)) in enumerate(where[k]):
                at = chip_of(here, side // 2, side % 2, k, zs) * rows
                top = pl.ds(pl.multiple_of(at, 16), row)
                low = pl.ds(pl.multiple_of(at + row, 16), rows - row)
                for out, lo, hi in zip(outs, ends, ends[1:]):
                    out[top, :] = refs[a][i, :row, lo:hi]
                    out[low, :] = refs[b][n, row - back : rows - back, lo:hi]

    return kernel(
        body,
        arrays,
        [shape((WIDTH, hi - lo), BF16) for lo, hi in zip(ends, ends[1:])],
        "build_qkv",
        flops=10**6,
        bytes_accessed=4 * 10**6,
    )


def build_rest(arrays, where, rows, hidden):
    zs = len(where)
    units = zs * 4 * hidden
    quarters = units // HALF
    first = quarters * rows
    if rows % 16:
        full = to_mesh_order(by_distance(arrays, where, first)).reshape(4 * zs, -1, HALF)
        w1 = jnp.swapaxes(full[:, :first].reshape(4 * zs, quarters, rows, HALF), 1, 2)
        w2 = jnp.swapaxes(full[:, first:].reshape(4 * zs, 2, hidden, HALF), 1, 2)
        return w1.reshape(WIDTH, units), w2.reshape(units, WIDTH)

    def body(*refs):
        w1_ref, w2_ref = refs[len(arrays) :]
        here = place()
        for k in range(zs):
            for side, ((a, i), (b, n, back)) in enumerate(where[k]):
                chip = chip_of(here, side // 2, side % 2, k, zs)
                to, down = rows_at(chip, rows), rows_at(chip, hidden)
                for j in range(quarters):
                    w1_ref[to, j * HALF : (j + 1) * HALF] = refs[a][i, j * rows : (j + 1) * rows, :]
                for j in range(2):
                    lo = first + j * hidden - back
                    w2_ref[down, j * HALF : (j + 1) * HALF] = refs[b][n, lo : lo + hidden, :]

    return kernel(
        body,
        arrays,
        (shape((WIDTH, units), BF16), shape((units, WIDTH), BF16)),
        "build_rest",
        flops=10**6,
        bytes_accessed=10**7,
    )


def whole_spec(*dims):
    return pl.BlockSpec(dims, lambda i: (0,) * len(dims))


def attend_step(q_ref, kv_ref, m_ref, l_ref, acc_ref):
    for h in range(NH):
        lo = h * HD
        qh = q_ref[:, lo : lo + HD]
        kh = kv_ref[:, lo : lo + HD]
        vh = kv_ref[:, HALF + lo : HALF + lo + HD]
        s = mm_t(kh, qh)
        before = m_ref[h : h + 1, :]
        top = jnp.maximum(before, jnp.max(s, axis=0, keepdims=True))
        p = jnp.exp(s - top)
        factor = jnp.exp(before - top)
        m_ref[h : h + 1, :] = top
        l_ref[h : h + 1, :] = l_ref[h : h + 1, :] * factor + jnp.sum(p, axis=0, keepdims=True)
        acc_ref[lo : lo + HD, :] = acc_ref[lo : lo + HD, :] * factor + t_mm(vh, p.astype(BF16))


def keys_values(x_ref, w_ref, v_bias, kv_ref):
    kv_ref[:, :HALF] = mm(x_ref[...], w_ref[:, :HALF]).astype(BF16)
    kv_ref[:, HALF:] = (mm(x_ref[...], w_ref[:, HALF:]) + v_bias).astype(BF16)


def attend_cost(tokens, keys):
    return pl.CostEstimate(flops=1, bytes_accessed=1, transcendentals=0)


def attend_first(own, got, xo, wq, wkv):
    tokens, keys = own.shape[0], xo.shape[0]
    block = math.gcd(keys, 1024)
    rows = pl.BlockSpec((block, WIDTH), lambda i: (i, 0))

    def body(o_ref, g_ref, x_ref, wq_ref, wkv_ref, q_ref, kv_ref, vec_ref, b_ref, m_ref, l_ref, acc_ref):
        @pl.when(pl.program_id(0) == 0)
        def _():
            core = place()[3]
            vecs = jnp.transpose(wq_ref[:, HALF:].astype(F32))
            vec_ref[...] = vecs[:16]
            b_ref[...] = jnp.where(core == 0, vecs[:8, :HALF], vecs[:8, HALF:])
            for i, ref in enumerate((o_ref, g_ref)):
                part = mm(ref[...], wq_ref[:, :HALF]) + b_ref[0:1, :]
                q_ref[i * tokens : (i + 1) * tokens, :] = part.astype(BF16) * BF16(0.125)
            m_ref[...] = jnp.full(m_ref.shape, -1e30, F32)
            l_ref[...] = jnp.zeros(l_ref.shape, F32)
            acc_ref[...] = jnp.zeros(acc_ref.shape, F32)

        keys_values(x_ref, wkv_ref, b_ref[1:2, :], kv_ref)
        attend_step(q_ref, kv_ref, m_ref, l_ref, acc_ref)

    return pl.pallas_call(
        body,
        grid=(keys // block,),
        in_specs=[
            whole_spec(tokens, WIDTH),
            whole_spec(tokens, WIDTH),
            rows,
            whole_spec(*wq.shape),
            whole_spec(*wkv.shape),
        ],
        out_specs=[
            whole_spec(2 * tokens, HALF),
            rows,
            whole_spec(16, WIDTH),
            whole_spec(8, HALF),
            whole_spec(8, 2 * tokens),
            whole_spec(8, 2 * tokens),
            whole_spec(HALF, 2 * tokens),
        ],
        out_shape=[
            shape((2 * tokens, HALF), BF16),
            shape((keys, WIDTH), BF16),
            shape((16, WIDTH), F32),
            shape((8, HALF), F32),
            shape((8, 2 * tokens), F32),
            shape((8, 2 * tokens), F32),
            shape((HALF, 2 * tokens), F32),
        ],
        compiler_params=pltpu.CompilerParams(vmem_limit_bytes=20 * MIB),
        cost_estimate=attend_cost(tokens, keys),
        name="attend_first",
    )(own, got, xo, wq, wkv)


def attend_last(q, xc, wkv, bias, top, total, weighted):
    tokens, keys = q.shape[0], xc.shape[0]
    block = math.gcd(keys, 1024)
    rows = pl.BlockSpec((block, WIDTH), lambda i: (i, 0))

    def body(q_ref, x_ref, w_ref, b_ref, mi_ref, li_ref, ai_ref, kv_ref, o_ref, ctx_ref, lse_ref, m_s, l_s, acc_s):
        @pl.when(pl.program_id(0) == 0)
        def _():
            m_s[...] = mi_ref[...]
            l_s[...] = li_ref[...]
            acc_s[...] = ai_ref[...]

        keys_values(x_ref, w_ref, b_ref[1:2, :], kv_ref)
        attend_step(q_ref, kv_ref, m_s, l_s, acc_s)

        @pl.when(pl.program_id(0) == pl.num_programs(0) - 1)
        def _():
            lse_ref[...] = m_s[...] + jnp.log(l_s[...])
            for h in range(NH):
                lo = h * HD
                o_ref[lo : lo + HD, :] = acc_s[lo : lo + HD, :] / l_s[h : h + 1, :]
            ctx_ref[...] = jnp.transpose(o_ref[...]).astype(BF16)

    return pl.pallas_call(
        body,
        grid=(keys // block,),
        in_specs=[
            whole_spec(tokens, HALF),
            rows,
            whole_spec(*wkv.shape),
            whole_spec(8, HALF),
            whole_spec(8, tokens),
            whole_spec(8, tokens),
            whole_spec(HALF, tokens),
        ],
        out_specs=[
            rows,
            whole_spec(HALF, tokens),
            whole_spec(tokens, HALF),
            whole_spec(8, tokens),
        ],
        out_shape=[
            shape((keys, WIDTH), BF16),
            shape((HALF, tokens), F32),
            shape((tokens, HALF), BF16),
            shape((8, tokens), F32),
        ],
        scratch_shapes=[
            pltpu.VMEM((8, tokens), F32),
            pltpu.VMEM((8, tokens), F32),
            pltpu.VMEM((HALF, tokens), F32),
        ],
        compiler_params=pltpu.CompilerParams(vmem_limit_bytes=20 * MIB),
        cost_estimate=attend_cost(tokens // 2, keys),
        name="attend_last",
    )(q, xc, wkv, bias, top, total, weighted)


def unit_places(chips, per, rows, core):
    units = chips * per * rows
    unit = lax.broadcasted_iota(jnp.int32, (WIDTH, units), 1)
    at = lax.broadcasted_iota(jnp.int32, (WIDTH, units), 0)
    chip, inside = unit // (per * rows), lax.rem(unit, rows)
    return (at == chip * (2 * rows) + core * rows + inside).astype(BF16)


def unit_bias(vecs, chips, per, rows):
    units = chips * per * rows

    def body(v_ref, out_ref):
        every = mm(v_ref[...].astype(BF16), unit_places(chips, per, rows, place()[3]))
        turn = lax.rem(lax.broadcasted_iota(jnp.int32, (16, units), 1) // rows, per)
        row = lax.broadcasted_iota(jnp.int32, (16, units), 0)
        out_ref[...] = column_sum(jnp.where(row == 9 + turn, every, 0.0))

    return kernel(body, (vecs,), (shape((1, units), F32),), "unit_bias", flops=10**8)[0]


def unit_rows(sums, chips, per, rows):
    units = chips * per * rows

    def body(s_ref, out_ref):
        turn = lax.rem(lax.broadcasted_iota(jnp.int32, (8, units), 1) // rows, per)
        row = lax.broadcasted_iota(jnp.int32, (8, units), 0)
        spread_out = jnp.where(row == turn, s_ref[...], 0.0).astype(BF16)
        out_ref[...] = mm_t(spread_out, unit_places(chips, per, rows, place()[3]))

    return kernel(body, (sums,), (shape((8, WIDTH), F32),), "unit_rows", flops=10**8)[0]


def norm_forward(residual, gain, shift):
    center = residual - jnp.mean(residual, axis=-1, keepdims=True)
    scale = lax.rsqrt(jnp.mean(center * center, axis=-1, keepdims=True) + EPSILON)
    normed = center * scale
    return normed * gain + shift, normed, scale


def norm_backward(grad_out, normed, scale, gain):
    grad_normed = grad_out * gain
    return scale * (
        grad_normed
        - jnp.mean(grad_normed, axis=-1, keepdims=True)
        - normed * jnp.mean(grad_normed * normed, axis=-1, keepdims=True)
    )


def column_sum(value):
    return jnp.sum(value, axis=0, keepdims=True)


def halves(core, own, other):
    left = jnp.where(core == 0, own, other)
    right = jnp.where(core == 0, other, own)
    return left, right


def mix(ctx, ctx_got, mixer_own, mixer_got, vecs, inputs):
    tokens = inputs.shape[0]

    def body(o_ref, g_ref, mo_ref, mg_ref, v_ref, x_ref, low_ref, row_ref, n_ref, s_ref):
        core = place()[3]
        mine = pl.ds(pl.multiple_of(core * HALF, HALF), HALF)
        others = pl.ds(pl.multiple_of((1 - core) * HALF, HALF), HALF)
        parts = [
            mm(o_ref[:tokens, :], ref[mine, :]) + mm(g_ref[tokens:, :], ref[others, :])
            for ref in (mo_ref, mg_ref)
        ]
        attended = jnp.concatenate(halves(core, *parts), axis=1) + v_ref[2:3, :]
        rows, normed, scale = norm_forward(
            x_ref[...].astype(F32) + attended, v_ref[3:4, :], v_ref[4:5, :]
        )
        low_ref[...] = rows.astype(BF16)
        row_ref[...] = rows
        n_ref[...] = normed
        s_ref[...] = scale

    return kernel(
        body,
        (ctx, ctx_got, mixer_own, mixer_got, vecs, inputs),
        (
            shape((tokens, WIDTH), BF16),
            shape((tokens, WIDTH), F32),
            shape((tokens, WIDTH), F32),
            shape((tokens, 1), F32),
        ),
        "mix",
        flops=10**9,
        bytes_accessed=3 * 10**6,
    )


def feed(own, got, w_inner, i_bias, w_outer):
    tokens = own.shape[0]
    units = w_inner.shape[1]

    def body(o_ref, g_ref, w1_ref, b_ref, w2_ref, two_ref, act_ref, slope_ref, mine_ref, send_ref):
        two_ref[:tokens, :] = o_ref[...]
        two_ref[tokens:, :] = g_ref[...]
        u = mm(two_ref[...], w1_ref[...]) + b_ref[...]
        cdf = 0.5 * (1.0 + lax.erf(u * ROOT_HALF))
        slope_ref[...] = cdf + u * jnp.exp(-0.5 * u * u) * GAUSS_FACTOR
        act_ref[...] = (u * cdf).astype(BF16)
        part = mm(act_ref[...], w2_ref[...])
        mine_ref[...] = part[:tokens]
        send_ref[...] = part[tokens:]

    return kernel(
        body,
        (own, got, w_inner, i_bias, w_outer),
        (
            shape((2 * tokens, WIDTH), BF16),
            shape((2 * tokens, units), BF16),
            shape((2 * tokens, units), F32),
            shape((tokens, WIDTH), F32),
            shape((tokens, WIDTH), F32),
        ),
        "feed",
        flops=3 * 10**9,
        bytes_accessed=8 * 10**6,
    )


def crown(mine, got, first_rows, vecs, out_cot, term_cot):
    tokens = mine.shape[0]

    def body(
        m_ref, g_ref, f_ref, v_ref, oc_ref, tc_ref, out_ref, term_ref, gs_ref, go_ref, sum_ref
    ):
        gain = v_ref[6:7, :]
        head = v_ref[8:9, :]
        outer = m_ref[...] + g_ref[...] + v_ref[5:6, :]
        rows, normed, scale = norm_forward(f_ref[...] + outer, gain, v_ref[7:8, :])
        out_ref[...] = rows.astype(BF16)
        logits = jnp.sum(rows * head, axis=-1, keepdims=True)
        small = jnp.exp(-jnp.abs(logits))
        term = jnp.maximum(logits, 0.0) + jnp.log1p(small)
        term_ref[...] = jnp.transpose(jnp.broadcast_to(term, (tokens, 128)))[0:1, :]
        sig = jnp.where(logits >= 0.0, 1.0, small) / (1.0 + small)
        cot = jnp.transpose(jnp.broadcast_to(tc_ref[...], (128, tokens)))[:, 0:1]
        slope = cot * sig
        grad_final = oc_ref[...].astype(F32) + slope * head
        grad = norm_backward(grad_final, normed, scale, gain)
        low = grad.astype(BF16)
        gs_ref[...] = grad
        go_ref[...] = low
        sum_ref[...] = jnp.concatenate(
            [
                column_sum(low.astype(F32)),
                column_sum(grad_final * normed),
                column_sum(grad_final),
                column_sum(slope * rows),
                jnp.zeros((4, WIDTH), F32),
            ],
            axis=0,
        )

    return kernel(
        body,
        (mine, got, first_rows, vecs, out_cot, term_cot),
        (
            shape((tokens, WIDTH), BF16),
            shape((1, tokens), F32),
            shape((tokens, WIDTH), F32),
            shape((tokens, WIDTH), BF16),
            shape((8, WIDTH), F32),
        ),
        "crown",
        flops=10**8,
        bytes_accessed=3 * 10**6,
    )


def feed_back(own, got, slope, w_inner, w_outer):
    tokens = own.shape[0]
    units = w_inner.shape[1]

    def body(o_ref, g_ref, s_ref, w1_ref, w2_ref, two_ref, gi_ref, mine_ref, send_ref, sum_ref):
        two_ref[:tokens, :] = o_ref[...]
        two_ref[tokens:, :] = g_ref[...]
        low = (mm_t(two_ref[...], w2_ref[...]) * s_ref[...]).astype(BF16)
        gi_ref[...] = low
        sum_ref[...] = column_sum(low.astype(F32))
        part = mm_t(gi_ref[...], w1_ref[...])
        mine_ref[...] = part[:tokens]
        send_ref[...] = part[tokens:]

    return kernel(
        body,
        (own, got, slope, w_inner, w_outer),
        (
            shape((2 * tokens, WIDTH), BF16),
            shape((2 * tokens, units), BF16),
            shape((tokens, WIDTH), F32),
            shape((tokens, WIDTH), F32),
            shape((1, units), F32),
        ),
        "feed_back",
        flops=3 * 10**9,
        bytes_accessed=8 * 10**6,
    )


def mix_back(mine, got, grad_second, normed, scale, vecs, mixer_own, mixer_got):
    tokens = mine.shape[0]

    def body(
        m_ref, g_ref, gs_ref, n_ref, s_ref, v_ref, mo_ref, mg_ref, res_ref, keep_ref, send_ref, sum_ref
    ):
        core = place()[3]
        first = gs_ref[...] + m_ref[...] + g_ref[...]
        normal = n_ref[...]
        grad = norm_backward(first, normal, s_ref[...], v_ref[3:4, :])
        res_ref[...] = grad
        low = grad.astype(BF16)
        sum_ref[...] = jnp.concatenate(
            [
                column_sum(low.astype(F32)),
                column_sum(first * normal),
                column_sum(first),
                jnp.zeros((5, WIDTH), F32),
            ],
            axis=0,
        )
        mine_low, other_low = halves(core, low[:, :HALF], low[:, HALF:])
        ctx = (mm_t(mine_low, mo_ref[...]) + mm_t(other_low, mg_ref[...])).astype(BF16)
        mine_ctx, other_ctx = halves(core, ctx[:, :HALF], ctx[:, HALF:])
        keep_ref[:, :HALF] = mine_ctx
        keep_ref[:, HALF:] = mine_low
        send_ref[:, :HALF] = other_ctx
        send_ref[:, HALF:] = other_low

    return kernel(
        body,
        (mine, got, grad_second, normed, scale, vecs, mixer_own, mixer_got),
        (
            shape((tokens, WIDTH), F32),
            shape((tokens, WIDTH), BF16),
            shape((tokens, WIDTH), BF16),
            shape((8, WIDTH), F32),
        ),
        "mix_back",
        flops=10**9,
        bytes_accessed=4 * 10**6,
    )


def attend_back_step(q_ref, g_ref, lse_ref, delta_ref, kv_ref, out_ref, acc_ref, sum_ref):
    held = []
    for h in range(NH):
        lo = h * HD
        qh = q_ref[:, lo : lo + HD]
        gh = g_ref[:, lo : lo + HD]
        kh = kv_ref[:, lo : lo + HD]
        vh = kv_ref[:, HALF + lo : HALF + lo + HD]
        p = jnp.exp(mm_t(kh, qh) - lse_ref[h : h + 1, :])
        dp = mm_t(vh, gh)
        ds = (p * (dp - delta_ref[h : h + 1, :])).astype(BF16)
        acc_ref[lo : lo + HD, :] += t_mm(kh, ds)
        held.append((mm(ds, qh).astype(BF16), mm(p.astype(BF16), gh).astype(BF16)))
        if h % 2 == 1:
            (dk0, dv0), (dk1, dv1) = held
            held = []
            at = lo - HD
            dv = jnp.concatenate([dv0, dv1], axis=1)
            out_ref[:, at : at + 2 * HD] = jnp.concatenate([dk0, dk1], axis=1)
            out_ref[:, HALF + at : HALF + at + 2 * HD] = dv
            sum_ref[1:2, at : at + 2 * HD] += column_sum(dv.astype(F32))


def attend_back_cost(tokens, keys):
    return pl.CostEstimate(flops=1, bytes_accessed=1, transcendentals=0)


def attend_back_first(q, low, low_got, o, lse, kv):
    tokens, keys = q.shape[0], kv.shape[0]
    block = math.gcd(keys, 1024)
    rows = pl.BlockSpec((block, WIDTH), lambda i: (i, 0))

    def body(q_ref, go_ref, gc_ref, o_ref, lse_ref, kv_ref, d_ref, g_ref, delta_ref, acc_ref, sum_ref):
        @pl.when(pl.program_id(0) == 0)
        def _():
            acc_ref[...] = jnp.zeros(acc_ref.shape, F32)
            sum_ref[...] = jnp.zeros(sum_ref.shape, F32)
            g_ref[: tokens // 2, :] = go_ref[:, :HALF]
            g_ref[tokens // 2 :, :] = gc_ref[:, :HALF]
            prod = jnp.transpose(g_ref[...].astype(F32)) * o_ref[...]
            for h in range(NH):
                delta_ref[h : h + 1, :] = column_sum(prod[h * HD : (h + 1) * HD, :])

        attend_back_step(q_ref, g_ref, lse_ref, delta_ref, kv_ref, d_ref, acc_ref, sum_ref)

    return pl.pallas_call(
        body,
        grid=(keys // block,),
        in_specs=[
            whole_spec(tokens, HALF),
            whole_spec(tokens // 2, WIDTH),
            whole_spec(tokens // 2, WIDTH),
            whole_spec(HALF, tokens),
            whole_spec(8, tokens),
            rows,
        ],
        out_specs=[
            rows,
            whole_spec(tokens, HALF),
            whole_spec(8, tokens),
            whole_spec(HALF, tokens),
            whole_spec(8, HALF),
        ],
        out_shape=[
            shape((keys, WIDTH), BF16),
            shape((tokens, HALF), BF16),
            shape((8, tokens), F32),
            shape((HALF, tokens), F32),
            shape((8, HALF), F32),
        ],
        compiler_params=pltpu.CompilerParams(vmem_limit_bytes=20 * MIB),
        cost_estimate=attend_back_cost(tokens, keys),
        name="attend_back_first",
    )(q, low, low_got, o, lse, kv)


def attend_back_last(q, g, lse, delta, acc, sums, kv, wq):
    tokens, keys = q.shape[0], kv.shape[0]
    block = math.gcd(keys, 1024)
    rows = pl.BlockSpec((block, WIDTH), lambda i: (i, 0))

    def body(q_ref, g_ref, lse_ref, delta_ref, ai_ref, si_ref, kv_ref, w_ref, d_ref, dq_ref, sum_ref, send_ref, acc_s):
        @pl.when(pl.program_id(0) == 0)
        def _():
            acc_s[...] = ai_ref[...]
            sum_ref[...] = si_ref[...]

        attend_back_step(q_ref, g_ref, lse_ref, delta_ref, kv_ref, d_ref, acc_s, sum_ref)

        @pl.when(pl.program_id(0) == pl.num_programs(0) - 1)
        def _():
            dq = jnp.transpose(acc_s[...] * 0.125).astype(BF16)
            dq_ref[...] = dq
            sum_ref[0:1, :] = column_sum(dq.astype(F32))
            send_ref[...] = mm_t(dq[tokens // 2 :], w_ref[:, :HALF]).astype(BF16)

    return pl.pallas_call(
        body,
        grid=(keys // block,),
        in_specs=[
            whole_spec(tokens, HALF),
            whole_spec(tokens, HALF),
            whole_spec(8, tokens),
            whole_spec(8, tokens),
            whole_spec(HALF, tokens),
            whole_spec(8, HALF),
            rows,
            whole_spec(*wq.shape),
        ],
        out_specs=[
            rows,
            whole_spec(tokens, HALF),
            whole_spec(8, HALF),
            whole_spec(tokens // 2, WIDTH),
        ],
        out_shape=[
            shape((keys, WIDTH), BF16),
            shape((tokens, HALF), BF16),
            shape((8, HALF), F32),
            shape((tokens // 2, WIDTH), BF16),
        ],
        scratch_shapes=[pltpu.VMEM((HALF, tokens), F32)],
        compiler_params=pltpu.CompilerParams(vmem_limit_bytes=20 * MIB),
        cost_estimate=attend_back_cost(tokens, keys),
        name="attend_back_last",
    )(q, g, lse, delta, acc, sums, kv, wq)


def input_part_other(dkv, wkv):
    keys = dkv.shape[0]
    block = math.gcd(keys, 1024)
    rows = pl.BlockSpec((block, WIDTH), lambda i: (i, 0))

    def body(d_ref, w_ref, out_ref):
        out_ref[...] = mm_t(d_ref[...], w_ref[...]).astype(BF16)

    return pl.pallas_call(
        body,
        grid=(keys // block,),
        in_specs=[rows, whole_spec(*wkv.shape)],
        out_specs=rows,
        out_shape=shape((keys, WIDTH), BF16),
        compiler_params=pltpu.CompilerParams(vmem_limit_bytes=12 * MIB),
        cost_estimate=pl.CostEstimate(flops=1, bytes_accessed=1, transcendentals=0),
        name="input_part_other",
    )(dkv, wkv)


def input_part_own(dkv, wkv, got, dq, wq, q_got):
    keys = dkv.shape[0]
    tokens = q_got.shape[0]
    block = math.gcd(keys // 2, 512)
    half = keys // 2 // block
    rows = pl.BlockSpec((block, WIDTH), lambda i: (i, 0))

    def body(d_ref, w_ref, g_ref, dq_ref, wq_ref, qg_ref, keep_ref, send_ref, part_s):
        step = pl.program_id(0)
        part_s[...] = mm_t(d_ref[...], w_ref[...]) + g_ref[...].astype(F32)

        @pl.when(step == 0)
        def _():
            part_s[:tokens, :] += mm_t(dq_ref[:tokens, :], wq_ref[:, :HALF]) + qg_ref[...].astype(
                F32
            )

        @pl.when(step < half)
        def _():
            keep_ref[...] = part_s[...].astype(BF16)

        @pl.when(step >= half)
        def _():
            send_ref[...] = part_s[...].astype(BF16)

    return pl.pallas_call(
        body,
        grid=(2 * half,),
        in_specs=[
            rows,
            whole_spec(*wkv.shape),
            rows,
            whole_spec(*dq.shape),
            whole_spec(*wq.shape),
            whole_spec(*q_got.shape),
        ],
        out_specs=[
            pl.BlockSpec((block, WIDTH), lambda i: (jnp.minimum(i, half - 1), 0)),
            pl.BlockSpec((block, WIDTH), lambda i: (jnp.maximum(i - half, 0), 0)),
        ],
        out_shape=[shape((keys // 2, WIDTH), BF16)] * 2,
        scratch_shapes=[pltpu.VMEM((block, WIDTH), F32)],
        compiler_params=pltpu.CompilerParams(vmem_limit_bytes=12 * MIB),
        cost_estimate=pl.CostEstimate(flops=1, bytes_accessed=1, transcendentals=0),
        name="input_part_own",
    )(dkv, wkv, got, dq, wq, q_got)


def spread(zs, rows, cols, args, fill, name, scratch, limit=14):
    count = len(args)

    def body(*refs):
        ins, outs, held = refs[:count], refs[count : count + 4], refs[count + 4 :]
        write = fill(ins, held)
        here = place()
        for k in range(zs):
            for side in range(4):
                write(outs[side], k, chip_of(here, side // 2, side % 2, k, zs))

    return kernel(
        body,
        args,
        [shape((zs, rows, cols), BF16)] * 4,
        name,
        limit=limit,
        scratch=[pltpu.VMEM(dims, BF16) for dims in scratch],
        flops=2 * 10**9,
        bytes_accessed=6 * 10**6,
    )


def spread_slow(full, zs):
    full = to_distance(full.reshape(2, zs, 2, *full.shape[1:]))
    full = full.reshape(4, zs, *full.shape[3:])
    return full[0], full[1], full[2], full[3]


def spread_rest(first2, grad_inner, active, grad_outer2, zs):
    units = active.shape[1]
    rows, hidden = WIDTH // (4 * zs), units // (4 * zs)
    if rows % 16:
        w1 = t_mm(first2, grad_inner).astype(BF16).reshape(4 * zs, rows, units)
        w2 = t_mm(active, grad_outer2).astype(BF16).reshape(4 * zs, hidden, WIDTH)
        return spread_slow(jnp.concatenate([w1[:, :, :WIDTH], w1[:, :, WIDTH:], w2], axis=1), zs)

    def fill(ins, held):
        f_ref, gi_ref, a_ref, go_ref = ins
        held[0][...] = t_mm(f_ref[...], gi_ref[...]).astype(BF16)
        held[1][...] = t_mm(a_ref[...], go_ref[...]).astype(BF16)

        def write(out, n, chip):
            at = rows_at(chip, rows)
            out[n, :rows, :] = held[0][at, :WIDTH]
            out[n, rows : 2 * rows, :] = held[0][at, WIDTH:]
            out[n, 2 * rows :, :] = held[1][rows_at(chip, hidden), :]

        return write

    return spread(
        zs,
        2 * rows + hidden,
        WIDTH,
        (first2, grad_inner, active, grad_outer2),
        fill,
        "spread_rest",
        ((WIDTH, units), (units, WIDTH)),
    )


def spread_qkv(zs, x_own, x_got, dq, qv, mid, top, unit, g_kv, ctx, ctx_got, low, low_got):
    tokens = x_own.shape[0]
    rows = WIDTH // (4 * zs)
    cols = WIDE + WIDTH + HALF

    def fill(ins, held):
        part_s = held[0]
        xo, xg, dq_r, qv_r, mid_r, top_r, unit_r, c_r, cg_r, l_r, lg_r, *kv_rs = ins
        core = place()[3]
        part_s[:, :HALF] = (
            t_mm(xo[...], dq_r[:tokens, :]) + t_mm(xg[...], dq_r[tokens:, :])
        ).astype(BF16)
        zero = jnp.zeros((2, HALF), F32)
        sums = jnp.concatenate(
            [
                jnp.concatenate(halves(core, qv_r[0:2, :], zero), axis=1),
                mid_r[0:3, :],
                top_r[0:4, :],
                unit_r[...],
                jnp.zeros((AUX - 17, WIDTH), F32),
            ],
            axis=0,
        )
        part_s[:, HALF:WIDE] = jnp.transpose(sums).astype(BF16)
        if len(kv_rs) == 1:
            part_s[:, WIDE : WIDE + WIDTH] = kv_rs[0][...]
        else:
            xk, dk, xl, dl = kv_rs
            part_s[:, WIDE : WIDE + WIDTH] = (t_mm(xk[...], dk[...]) + t_mm(xl[...], dl[...])).astype(
                BF16
            )
        lows = (l_r[:, HALF:], lg_r[:, HALF:])
        part_s[pl.ds(pl.multiple_of(core * HALF, HALF), HALF), WIDE + WIDTH :] = (
            t_mm(c_r[:tokens, :], lows[0]) + t_mm(c_r[tokens:, :], lows[1])
        ).astype(BF16)
        part_s[pl.ds(pl.multiple_of((1 - core) * HALF, HALF), HALF), WIDE + WIDTH :] = (
            t_mm(cg_r[tokens:, :], lows[0]) + t_mm(cg_r[:tokens, :], lows[1])
        ).astype(BF16)

        def write(out, n, chip):
            out[n] = part_s[rows_at(chip, rows), :]

        return write

    args = (x_own, x_got, dq, qv, mid, top, unit, ctx, ctx_got, low, low_got, *g_kv)
    if rows % 16 == 0:
        return spread(zs, rows, cols, args, fill, "spread_qkv", ((WIDTH, cols),), 24)

    def body(*refs):
        fill(refs[:12], refs[12:])

    full = kernel(body, args, [shape((WIDTH, cols), BF16)], "fill_qkv")[0]
    return spread_slow(full.reshape(4 * zs, rows, cols), zs)


def finish_sums(qkv, rest, rows):
    count, cols = len(qkv), qkv[0].shape[1]
    hidden = rest[0].shape[0] - 4 * rows
    wide = cols + 2 * WIDTH

    def body(*refs):
        ins, (own_ref, send_ref, outer_ref, both_s) = refs[:-4], refs[-4:]
        core = place()[3]
        both_s[:, :cols] = sum(ref[...].astype(F32) for ref in ins[:count])
        low = sum(ref[...].astype(F32) for ref in ins[count:])
        both_s[:, cols : cols + WIDTH] = low[: 2 * rows]
        both_s[:, cols + WIDTH :] = low[2 * rows : 4 * rows]
        outer_ref[...] = low[4 * rows :]
        halves_of = (both_s[:rows, :], both_s[rows:, :])
        own_ref[...] = jnp.where(core == 0, *halves_of)
        send_ref[...] = jnp.where(core == 1, *halves_of)

    return kernel(
        body,
        (*qkv, *rest),
        [shape((rows, wide), F32)] * 2 + [shape((hidden, WIDTH), F32)],
        "finish_sums",
        limit=8,
        scratch=[pltpu.VMEM((2 * rows, wide), F32)],
    )


def finish_rows(own, got, hidden, per):
    rows = own.shape[0]
    base = WIDE + WIDTH + HALF
    chips = (own.shape[1] - base) // hidden

    def body(own_ref, got_ref, *outs):
        core = place()[3]
        left = jnp.where(core == 0, own_ref[...], got_ref[...])
        right = jnp.where(core == 0, got_ref[...], own_ref[...])
        for out, lo in zip(outs, (0, WIDE, WIDE + HALF, WIDE + WIDTH)):
            out[:, :HALF] = left[:, lo : lo + HALF]
            out[:, HALF:] = right[:, lo : lo + HALF]
        outs[4][...] = jnp.concatenate(
            [
                side[:, base + i * hidden : base + (i + 1) * hidden]
                for i in range(chips)
                for side in (left, right)
            ],
            axis=1,
        )
        small = left[:, HALF:WIDE] + right[:, HALF:WIDE]
        if rows < AUX:
            small = jnp.concatenate([small, jnp.zeros((AUX - rows, AUX), F32)], axis=0)
        small = jnp.transpose(small)
        for j in range(9):
            outs[5 + j][...] = small[j, :rows]
        for j in range(per):
            outs[14][pl.ds(j * rows, rows)] = small[9 + j, :rows]

    outs = kernel(
        body,
        (own, got),
        [shape((rows, WIDTH), F32)] * 4
        + [shape((rows, 2 * chips * hidden), F32)]
        + [shape((rows,), F32)] * 9
        + [shape((hidden,), F32)],
        "finish_rows",
        limit=8,
    )
    return (*outs[:5], outs[5:])


def shards(
    layer_input,
    query_weight,
    query_bias,
    key_weight,
    value_weight,
    value_bias,
    mixer_weight,
    mixer_bias,
    first_gain,
    first_shift,
    inner_weight,
    inner_bias,
    outer_weight,
    outer_bias,
    second_gain,
    second_shift,
    head_weight,
    out_cotangent,
    term_cotangent,
):
    core = place()[3]
    chips = lax.axis_size("ctx")
    zs = chips // 4
    inputs = layer_input[0]
    tokens = inputs.shape[0]
    rows = query_weight.shape[0]
    hidden = outer_weight.shape[0]
    ff = inner_weight.shape[1]
    units = ff // 2
    per = hidden // rows

    def in_order(own, other, axis):
        return jnp.stack(halves(core, own, other), axis=axis)

    own, send = pack(
        (query_weight, key_weight, value_weight, mixer_weight),
        inner_weight,
        (
            query_bias,
            value_bias,
            mixer_bias,
            first_gain,
            first_shift,
            outer_bias,
            second_gain,
            second_shift,
            head_weight,
            inner_bias,
        ),
    )
    block, rest = join(own, swap_core(send), outer_weight)
    x_got = swap_core(inputs)
    first = 2 * rows * (units // HALF)
    every = tuple(range(zs))
    barrier = lax.optimization_barrier
    part_row = 2 * rows // 3
    if zs == 4:
        near_y, near_x = swap_y(rest[None]), swap_x(rest[None])
        near_y, near_x, qkv = barrier((near_y, near_x, along_z_pieces(block)))
        x_own, first_piece = barrier((inputs, qkv[1]))
        qkv = jnp.stack([qkv[0], first_piece, *qkv[2:]])
        flat = qkv.reshape(first, -1)
        sent_y = swap_y(jnp.concatenate([flat, near_x[0, first:]], axis=1))
        sent_x = swap_x(jnp.concatenate([flat, near_y[0, :first]], axis=1))
        sent_y, sent_x, x_along = barrier((sent_y, sent_x, along_z_pieces(x_own)))
        x_along = jnp.stack(x_along)
        cols = flat.shape[1]
        qkv_y, qkv_x = (sent[:, :cols].reshape(qkv.shape) for sent in (sent_y, sent_x))
        near_far = [sent[None, :, cols:] for sent in (sent_x, sent_y)]
        rest_sent, x_along = barrier((rest, x_along))
        x_y, qkv_far, pieces = barrier(
            (swap_y(x_along), far_out(qkv_y, qkv_x, part_row), along_z_pieces(rest_sent))
        )
        pieces = jnp.stack(pieces[1:])
        rest_y, rest_x = swap_y(pieces), swap_x(pieces)
    else:
        qkv, x_along, pieces = (along_z_pieces(v) for v in (block, inputs, rest))
        x_y, rest_y, rest_x = swap_y(x_along), swap_y(pieces), swap_x(pieces)
        qkv_y, qkv_x = swap_y(qkv), swap_x(qkv)
        qkv_far = far_out(qkv_y, qkv_x, part_row)
    wq, wkv, mixer_own = build_qkv(
        *sources([(every, qkv, qkv_y, qkv_x, *qkv_far)], part_row), part_row
    )
    mixer_got = swap_core(mixer_own)
    xo = jnp.concatenate([x_along, x_y]).reshape(2 * zs * tokens, WIDTH)
    xc = swap_core(xo)

    q_scaled, kvo, vecs, bias, top, total, weighted = attend_first(inputs, x_got, xo, wq, wkv)
    kvc, o_exact, ctx, lse = attend_last(q_scaled, xc, wkv, bias, top, total, weighted)
    rest_y, rest_x, ctx = barrier((rest_y, rest_x, ctx))
    away = (pieces, rest_y, rest_x, *far_out(rest_y, rest_x, first))
    if zs == 4:
        away = [((0,), rest[None], near_y, near_x, *near_far), ((1, 2, 3), *away)]
    else:
        away = [(every, *away)]
    w_inner, w_outer = build_rest(*sources(away, first), 2 * rows, hidden)
    ctx_got = swap_core(ctx)
    i_bias = unit_bias(vecs, chips, per, rows)
    first_low, first_rows, first_normed, first_scale = mix(
        ctx, ctx_got, mixer_own, mixer_got, vecs, inputs
    )

    first2, active, slope, mine, away = feed(
        first_low, swap_core(first_low), w_inner, i_bias, w_outer
    )
    final_low, term, grad_second, grad_outer, top_sums = crown(
        mine, swap_core(away), first_rows, vecs, out_cotangent[0], term_cotangent
    )
    grad_outer2, grad_inner, mine, away, inner_sums = feed_back(
        grad_outer, swap_core(grad_outer), slope, w_inner, w_outer
    )
    got = swap_core(away)
    keep, rest_y, rest_x, far = spread_rest(first2, grad_inner, active, grad_outer2, zs)
    mine, keep, rest_y, rest_x, far = barrier((mine, keep, rest_y, rest_x, far))
    over_x, over_y = swap_x(far[:, : 4 * rows]), swap_y(far[:, 4 * rows :])

    grad_residual, low, low_send, mid_sums = mix_back(
        mine, got, grad_second, first_normed, first_scale, vecs, mixer_own, mixer_got
    )
    low_got = swap_core(low_send)
    dkvc, g_both, delta, acc, qv_sums = attend_back_first(
        q_scaled, low, low_got, o_exact, lse, kvc
    )
    over_x, over_y, dkvc, kvo = barrier((over_x, over_y, dkvc, kvo))
    away = swap_core(input_part_other(dkvc, wkv))
    rest_y = jnp.concatenate([rest_y[:, : 4 * rows] + over_x, rest_y[:, 4 * rows :]], axis=1)
    rest_x = jnp.concatenate([rest_x[:, : 4 * rows], rest_x[:, 4 * rows :] + over_y], axis=1)
    at = 1 if zs == 4 else 0
    got_y, got_x = swap_y(rest_y[at:]), swap_x(rest_x[at:])
    dkvo, dq, qv_sums, q_away = attend_back_last(
        q_scaled, g_both, lse, delta, acc, qv_sums, kvo, wq
    )

    part, part_y = input_part_own(dkvo, wkv, away, dq, wq, swap_core(q_away))
    dq, dkvo, part, part_y = barrier((dq, dkvo, part, part_y))
    if zs == 4:
        g_kv = (xo, dkvo, xc, dkvc)
    else:
        g_kv = ((t_mm(xo, dkvo) + t_mm(xc, dkvc)).astype(BF16),)
    g_qkv, qkv_y, qkv_x, qkv_far = spread_qkv(
        zs,
        inputs,
        x_got,
        dq,
        qv_sums,
        mid_sums,
        top_sums,
        unit_rows(inner_sums, chips, per, rows),
        g_kv,
        ctx,
        ctx_got,
        low,
        low_got,
    )
    part, part_y = part.reshape(zs, tokens, WIDTH), part_y.reshape(zs, tokens, WIDTH)
    if zs == 4:
        got_y, got_x, part_y, qkv_far = barrier((got_y, got_x, part_y, qkv_far))
        g_rest = keep[1:] + got_y + got_x
        qkv_far, got_part, g_rest = barrier(
            (
                swap_x(qkv_far),
                swap_y(part_y),
                [swap_z(g_rest[k - 1], k) for k in range(1, zs)],
            )
        )
        part = part + got_part
        qkv_x, qkv_far = barrier((qkv_x, qkv_far))
        got_y, got_x, parts = barrier(
            (
                swap_y(qkv_y + qkv_far),
                swap_x(qkv_x),
                [swap_z(part[k], k) for k in range(1, zs)],
            )
        )
        near_y, near_x, parts = barrier((rest_y[:1], rest_x[:1], parts))
        total = part[0].astype(F32)
        for value in parts:
            total = total + value.astype(F32)
        g_qkv = g_qkv + got_y + got_x
        near_y, near_x, pieces = barrier(
            (
                swap_y(near_y),
                swap_x(near_x),
                [swap_z(g_qkv[k], k) for k in range(1, zs)],
            )
        )
        g_qkv = [g_qkv[0], *pieces]
        g_rest = [keep[0], near_y[0], near_x[0], *g_rest]
    else:
        g_rest = [sum_z([(every, keep + got_y + got_x)])]
        part = part + swap_y(part_y)
        total = sum_z([(every, part)])
        qkv_y, qkv_x = fan_far(qkv_y, qkv_x, qkv_far, 2 * rows)
        g_qkv = [sum_z([(every, g_qkv + swap_y(qkv_y) + swap_x(qkv_x))])]
    input_grad = (grad_residual + total).astype(BF16)

    own, send, g_outer = finish_sums(g_qkv, g_rest, rows)
    g_query, g_key, g_value, g_mixer, g_inner, vectors = finish_rows(
        own, swap_core(send), hidden, per
    )
    return (
        final_low[None],
        term,
        input_grad[None],
        g_query,
        vectors[0],
        g_key,
        g_value,
        vectors[1],
        g_mixer,
        vectors[2],
        vectors[3],
        vectors[4],
        g_inner,
        vectors[9],
        g_outer,
        vectors[5],
        vectors[6],
        vectors[7],
        vectors[8],
    )


def pick(value, index, axis):
    return lax.dynamic_index_in_dim(value, index, axis, keepdims=False)


def solution(mesh):
    both = ("seq", "ctx")
    tok, mat, vec = P("seq", "ctx", None), P(both, None), P(both)
    term = P("seq", "ctx")
    in_specs = (
        tok, mat, vec, mat, mat, vec, mat, vec, vec, vec,
        mat, vec, mat, vec, vec, vec, vec, tok, term,
    )
    out_specs = (
        tok, term, tok, mat, vec, mat, mat, vec, mat, vec,
        vec, vec, mat, vec, mat, vec, vec, vec, vec,
    )
    return jax.shard_map(
        shards, mesh=mesh, in_specs=in_specs, out_specs=out_specs, check_vma=False
    )
```

```python
import math

import jax
import jax.numpy as jnp
from jax import lax
from jax.experimental import pallas as pl
from jax.experimental.pallas import tpu as pltpu
from jax.sharding import PartitionSpec as P

HEADS = 12
HD = 64
WIDTH = HEADS * HD
HALF = WIDTH // 2
NH = HEADS // 2
EPSILON = 1e-12
ROOT_HALF = 0.7071067811865476
GAUSS_FACTOR = 0.3989422804014327
F32 = jnp.float32
BF16 = jnp.bfloat16
AUX = 128
WIDE = HALF + AUX
MIB = 2**20


def mm(a, b):
    return lax.dot_general(a, b, (((1,), (0,)), ((), ())), preferred_element_type=F32)


def mm_t(a, b):
    return lax.dot_general(a, b, (((1,), (1,)), ((), ())), preferred_element_type=F32)


def t_mm(a, b):
    return lax.dot_general(a, b, (((0,), (0,)), ((), ())), preferred_element_type=F32)


def shape(dims, dtype):
    return jax.ShapeDtypeStruct(dims, dtype)


def swap_ctx(value, bit):
    n = lax.axis_size("ctx")
    return lax.ppermute(value, "ctx", [(i, i ^ bit) for i in range(n)])


def swap_core(value):
    return swap_ctx(value, 1)


def swap_y(value):
    return swap_ctx(value, 2)


def swap_x(value):
    return lax.ppermute(value, "seq", [(0, 1), (1, 0)])


def swap_z(value, k):
    return swap_ctx(value, 4 * k)


def place():
    at = lax.axis_index("ctx")
    return lax.axis_index("seq"), at // 4, (at // 2) % 2, at % 2


def z_groups():
    n = lax.axis_size("ctx")
    return [[i + 4 * j for j in range(n // 4)] for i in range(4)]


def turned(blocks, z, axis=0):
    zs = blocks.shape[axis]
    lead = blocks.shape[:axis]
    rest = blocks.shape[axis + 1 :]
    bit = 1
    while bit < zs:
        pairs = blocks.reshape(*lead, zs // (2 * bit), 2, bit, *rest)
        flipped = jnp.flip(pairs, len(lead) + 1)
        blocks = jnp.where((z & bit) == 0, pairs, flipped).reshape(*lead, zs, *rest)
        bit *= 2
    return blocks


def along_z_pieces(block):
    zs = lax.axis_size("ctx") // 4
    if zs > 4:
        every = lax.all_gather(block, "ctx", axis_index_groups=z_groups())
        return turned(every, lax.axis_index("ctx") // 4)
    return [block] + [swap_z(block, k) for k in range(1, zs)]


def far_out(by_y, by_x, row):
    if row == by_y.shape[1]:
        return (swap_x(by_y),)
    return swap_x(by_y[:, :row]), swap_y(by_x[:, row:])


def sources(groups, row):
    arrays, where = [], {}
    for ks, *blocks in groups:
        at = len(arrays)
        arrays += blocks
        for i, k in enumerate(ks):
            last = ((at + 3, i), (at + 4, i, row)) if len(blocks) > 4 else ((at + 3, i), (at + 3, i, 0))
            where[k] = (*(((at + j, i), (at + j, i, 0)) for j in range(3)), last)
    return arrays, where


def by_distance(arrays, where, row=0):
    def whole(first, rest):
        top = arrays[first[0]][first[1]][:row]
        return jnp.concatenate([top, arrays[rest[0]][rest[1]][row - rest[2] :]])

    blocks = [[whole(*side) for side in where[k]] for k in sorted(where)]
    full = jnp.stack([jnp.stack(four) for four in blocks], axis=1)
    return full.reshape(2, 2, *full.shape[1:])


def fan_far(by_y, by_x, far, row):
    if row == far.shape[1]:
        return by_y + swap_x(far), by_x
    over_x, over_y = swap_x(far[:, :row]), swap_y(far[:, row:])
    by_y = jnp.concatenate([by_y[:, :row] + over_x, by_y[:, row:]], axis=1)
    by_x = jnp.concatenate([by_x[:, :row], by_x[:, row:] + over_y], axis=1)
    return by_y, by_x


def sum_z(groups):
    zs = lax.axis_size("ctx") // 4
    if zs > 4:
        ((_, along),) = groups
        every = turned(along, lax.axis_index("ctx") // 4)
        every = lax.all_to_all(every, "ctx", 0, 0, axis_index_groups=z_groups())
        return jnp.sum(every.astype(F32), axis=0)
    total = None
    for ks, blocks in groups:
        for i, k in enumerate(ks):
            part = (blocks[i] if k == 0 else swap_z(blocks[i], k)).astype(F32)
            total = part if total is None else total + part
    return total


def to_mesh_order(blocks):
    x, z, y, _ = place()
    blocks = turned(blocks, z, 2)
    for axis, bit in enumerate((x, y)):
        blocks = jnp.where(bit == 0, blocks, jnp.flip(blocks, axis))
    return jnp.swapaxes(blocks, 1, 2)


def to_distance(blocks):
    x, z, y, _ = place()
    blocks = turned(jnp.swapaxes(blocks, 1, 2), z, 2)
    for axis, bit in enumerate((x, y)):
        blocks = jnp.where(bit == 0, blocks, jnp.flip(blocks, axis))
    return blocks


def chip_of(here, xr, yr, k, zs):
    x, z, y, _ = here
    return ((x ^ xr) * zs + (z ^ k)) * 2 + (y ^ yr)


def rows_at(chip, rows):
    return pl.ds(pl.multiple_of(chip * rows, 16), rows)


def kernel(body, args, outs, name, limit=14, scratch=(), flops=0, bytes_accessed=0):
    return pl.pallas_call(
        body,
        in_specs=[pl.BlockSpec(memory_space=pltpu.VMEM) for _ in args],
        out_specs=[pl.BlockSpec(memory_space=pltpu.VMEM) for _ in outs],
        out_shape=list(outs),
        scratch_shapes=list(scratch),
        compiler_params=pltpu.CompilerParams(vmem_limit_bytes=limit * MIB),
        cost_estimate=pl.CostEstimate(flops=1, bytes_accessed=1, transcendentals=0),
        name=name,
    )(*args)


def pack(weights, inner, vectors):
    rows, hidden = inner.shape[0], vectors[-1].shape[0]
    count = len(weights)
    every = (*weights, inner, *vectors)
    base = WIDE + WIDTH + HALF
    chips = inner.shape[1] // (2 * hidden)
    cols = base + chips * hidden

    def body(*refs):
        n = len(every)
        ins, (own_ref, send_ref), held = refs[:n], refs[n : n + 2], refs[n + 2 : 2 * n + 2]
        flat_s, sems = refs[-2:]
        copies = [pltpu.make_async_copy(i, h, sems.at[j]) for j, (i, h) in enumerate(zip(ins, held))]
        for copy in copies:
            copy.start()
        flat_s[...] = jnp.zeros(flat_s.shape, F32)
        for copy in copies:
            copy.wait()
        ws, inner_ref, vs = held[:count], held[count], held[count + 1 :]
        core = place()[3]
        at = 0
        for v in vs:
            for j in range(v.shape[0] // rows):
                flat_s[at : at + 1, :rows] = v[pl.ds(j * rows, rows)].astype(F32).reshape(1, rows)
                at += 1
        aux = jnp.transpose(flat_s[...])[:rows, :].astype(BF16)
        places = (0, WIDE, WIDE + HALF, WIDE + WIDTH)
        whole = inner_ref[...]
        units = [
            jnp.concatenate(
                [
                    whole[:, (2 * i + side) * hidden : (2 * i + side + 1) * hidden]
                    for i in range(chips)
                ],
                axis=1,
            )
            for side in range(2)
        ]
        for out, side in ((own_ref, core), (send_ref, 1 - core)):
            out[:, HALF:WIDE] = aux
            for w, lo in zip(ws, places):
                out[:, lo : lo + HALF] = jnp.where(side == 0, w[:, :HALF], w[:, HALF:])
            out[:, base:] = jnp.where(side == 0, units[0], units[1])

    return pl.pallas_call(
        body,
        in_specs=[pl.BlockSpec(memory_space=pl.ANY) for _ in every],
        out_specs=[pl.BlockSpec(memory_space=pltpu.VMEM)] * 2,
        out_shape=[shape((rows, cols), BF16)] * 2,
        scratch_shapes=[pltpu.VMEM(a.shape, BF16) for a in every]
        + [pltpu.VMEM((AUX, AUX), F32), pltpu.SemaphoreType.DMA((len(every),))],
        compiler_params=pltpu.CompilerParams(vmem_limit_bytes=56 * MIB),
        name="pack",
    )(*every)


def join(own, got, outer):
    rows, hidden = own.shape[0], outer.shape[0]
    base = WIDE + WIDTH + HALF
    quarters = (own.shape[1] - base) // HALF
    core = place()[3]
    both = jnp.concatenate(halves(core, own, got))
    return both[:, :base], jnp.concatenate(
        [both[:, base + j * HALF : base + (j + 1) * HALF] for j in range(quarters)]
        + [outer[:, :HALF], outer[:, HALF:]]
    )


def build_qkv(arrays, where, row):
    zs, rows = len(where), arrays[0].shape[1]
    ends = (0, WIDE, WIDE + WIDTH, WIDE + WIDTH + HALF)
    if rows % 16:
        full = to_mesh_order(by_distance(arrays, where, row)).reshape(WIDTH, -1)
        return [full[:, lo:hi] for lo, hi in zip(ends, ends[1:])]

    def body(*refs):
        outs = refs[len(arrays) :]
        here = place()
        for k in range(zs):
            for side, ((a, i), (b, n, back)) in enumerate(where[k]):
                at = chip_of(here, side // 2, side % 2, k, zs) * rows
                top = pl.ds(pl.multiple_of(at, 16), row)
                for out, lo, hi in zip(outs, ends, ends[1:]):
                    out[top, :] = refs[a][i, :row, lo:hi]

    return kernel(
        body,
        arrays,
        [shape((WIDTH, hi - lo), BF16) for lo, hi in zip(ends, ends[1:])],
        "build_qkv",
        flops=10**6,
        bytes_accessed=4 * 10**6,
    )


def build_split(near, far, late, rows, hidden, cuts):
    zs = len(late) + 1
    quarters = zs * 4 * hidden // HALF
    count = len(near) + len(far)

    def body(*refs):
        nears, fars, lates = refs[: len(near)], refs[len(near) : count], refs[count:-2]
        w1_ref, w2_ref = refs[-2:]
        here = place()

        def read(k, side, lo, n):
            if k > 0 and lo >= cuts[2]:
                return lates[k - 1][side, lo - cuts[2] : lo - cuts[2] + n, :]
            refs_of, at, row = (nears, 0, cuts[1]) if k == 0 else (fars, k - 1, cuts[0])
            if side < 3:
                return refs_of[side][at, lo : lo + n, :]
            if lo < row:
                return refs_of[3][at, lo : lo + n, :]
            return refs_of[4][at, lo - row : lo - row + n, :]

        for k in range(zs):
            for side in range(4):
                chip = chip_of(here, side // 2, side % 2, k, zs)
                to, down = rows_at(chip, rows), rows_at(chip, hidden)
                for j in range(quarters):
                    w1_ref[to, j * HALF : (j + 1) * HALF] = read(k, side, j * rows, rows)
                for j in range(2):
                    w2_ref[down, j * HALF : (j + 1) * HALF] = read(
                        k, side, quarters * rows + j * hidden, hidden
                    )

    return kernel(
        body,
        (*near, *far, *late),
        (shape((WIDTH, zs * 4 * hidden), BF16), shape((zs * 4 * hidden, WIDTH), BF16)),
        "build_split",
    )


def build_rest(arrays, where, rows, hidden):
    zs = len(where)
    units = zs * 4 * hidden
    quarters = units // HALF
    first = quarters * rows
    if rows % 16:
        full = to_mesh_order(by_distance(arrays, where, first)).reshape(4 * zs, -1, HALF)
        w1 = jnp.swapaxes(full[:, :first].reshape(4 * zs, quarters, rows, HALF), 1, 2)
        w2 = jnp.swapaxes(full[:, first:].reshape(4 * zs, 2, hidden, HALF), 1, 2)
        return w1.reshape(WIDTH, units), w2.reshape(units, WIDTH)

    def body(*refs):
        w1_ref, w2_ref = refs[len(arrays) :]
        here = place()
        for k in range(zs):
            for side, ((a, i), (b, n, back)) in enumerate(where[k]):
                chip = chip_of(here, side // 2, side % 2, k, zs)
                to, down = rows_at(chip, rows), rows_at(chip, hidden)
                for j in range(quarters):
                    w1_ref[to, j * HALF : (j + 1) * HALF] = refs[a][i, j * rows : (j + 1) * rows, :]
                for j in range(2):
                    lo = first + j * hidden - back
                    w2_ref[down, j * HALF : (j + 1) * HALF] = refs[b][n, lo : lo + hidden, :]

    return kernel(
        body,
        arrays,
        (shape((WIDTH, units), BF16), shape((units, WIDTH), BF16)),
        "build_rest",
        flops=10**6,
        bytes_accessed=10**7,
    )


def whole_spec(*dims):
    return pl.BlockSpec(dims, lambda i: (0,) * len(dims))


def attend_step(q_ref, kv_ref, m_ref, l_ref, acc_ref):
    for h in range(NH):
        lo = h * HD
        qh = q_ref[:, lo : lo + HD]
        kh = kv_ref[:, lo : lo + HD]
        vh = kv_ref[:, HALF + lo : HALF + lo + HD]
        s = mm_t(kh, qh)
        before = m_ref[h : h + 1, :]
        top = jnp.maximum(before, jnp.max(s, axis=0, keepdims=True))
        p = jnp.exp(s - top)
        factor = jnp.exp(before - top)
        m_ref[h : h + 1, :] = top
        l_ref[h : h + 1, :] = l_ref[h : h + 1, :] * factor + jnp.sum(p, axis=0, keepdims=True)
        acc_ref[lo : lo + HD, :] = acc_ref[lo : lo + HD, :] * factor + t_mm(vh, p.astype(BF16))


def keys_values(x_ref, w_ref, v_bias, kv_ref):
    kv_ref[:, :HALF] = mm(x_ref[...], w_ref[:, :HALF]).astype(BF16)
    kv_ref[:, HALF:] = (mm(x_ref[...], w_ref[:, HALF:]) + v_bias).astype(BF16)


def attend_cost(tokens, keys):
    return pl.CostEstimate(flops=1, bytes_accessed=1, transcendentals=0)


def attend_first(own, got, xo, wq, wkv):
    tokens, keys = own.shape[0], xo.shape[0]
    block = math.gcd(keys, 1024)
    rows = pl.BlockSpec((block, WIDTH), lambda i: (i, 0))

    def body(o_ref, g_ref, x_ref, wq_ref, wkv_ref, q_ref, kv_ref, vec_ref, b_ref, m_ref, l_ref, acc_ref):
        @pl.when(pl.program_id(0) == 0)
        def _():
            core = place()[3]
            vecs = jnp.transpose(wq_ref[:, HALF:].astype(F32))
            vec_ref[...] = vecs[:16]
            b_ref[...] = jnp.where(core == 0, vecs[:8, :HALF], vecs[:8, HALF:])
            for i, ref in enumerate((o_ref, g_ref)):
                part = mm(ref[...], wq_ref[:, :HALF]) + b_ref[0:1, :]
                q_ref[i * tokens : (i + 1) * tokens, :] = part.astype(BF16) * BF16(0.125)
            m_ref[...] = jnp.full(m_ref.shape, -1e30, F32)
            l_ref[...] = jnp.zeros(l_ref.shape, F32)
            acc_ref[...] = jnp.zeros(acc_ref.shape, F32)

        keys_values(x_ref, wkv_ref, b_ref[1:2, :], kv_ref)
        attend_step(q_ref, kv_ref, m_ref, l_ref, acc_ref)

    return pl.pallas_call(
        body,
        grid=(keys // block,),
        in_specs=[
            whole_spec(tokens, WIDTH),
            whole_spec(tokens, WIDTH),
            rows,
            whole_spec(*wq.shape),
            whole_spec(*wkv.shape),
        ],
        out_specs=[
            whole_spec(2 * tokens, HALF),
            rows,
            whole_spec(16, WIDTH),
            whole_spec(8, HALF),
            whole_spec(8, 2 * tokens),
            whole_spec(8, 2 * tokens),
            whole_spec(HALF, 2 * tokens),
        ],
        out_shape=[
            shape((2 * tokens, HALF), BF16),
            shape((keys, WIDTH), BF16),
            shape((16, WIDTH), F32),
            shape((8, HALF), F32),
            shape((8, 2 * tokens), F32),
            shape((8, 2 * tokens), F32),
            shape((HALF, 2 * tokens), F32),
        ],
        compiler_params=pltpu.CompilerParams(vmem_limit_bytes=20 * MIB),
        cost_estimate=attend_cost(tokens, keys),
        name="attend_first",
    )(own, got, xo, wq, wkv)


def attend_last(q, xc, wkv, bias, top, total, weighted):
    tokens, keys = q.shape[0], xc.shape[0]
    block = math.gcd(keys, 1024)
    rows = pl.BlockSpec((block, WIDTH), lambda i: (i, 0))

    def body(q_ref, x_ref, w_ref, b_ref, mi_ref, li_ref, ai_ref, kv_ref, o_ref, ctx_ref, lse_ref, m_s, l_s, acc_s):
        @pl.when(pl.program_id(0) == 0)
        def _():
            m_s[...] = mi_ref[...]
            l_s[...] = li_ref[...]
            acc_s[...] = ai_ref[...]

        keys_values(x_ref, w_ref, b_ref[1:2, :], kv_ref)
        attend_step(q_ref, kv_ref, m_s, l_s, acc_s)

        @pl.when(pl.program_id(0) == pl.num_programs(0) - 1)
        def _():
            lse_ref[...] = m_s[...] + jnp.log(l_s[...])
            for h in range(NH):
                lo = h * HD
                o_ref[lo : lo + HD, :] = acc_s[lo : lo + HD, :] / l_s[h : h + 1, :]
            ctx_ref[...] = jnp.transpose(o_ref[...]).astype(BF16)

    return pl.pallas_call(
        body,
        grid=(keys // block,),
        in_specs=[
            whole_spec(tokens, HALF),
            rows,
            whole_spec(*wkv.shape),
            whole_spec(8, HALF),
            whole_spec(8, tokens),
            whole_spec(8, tokens),
            whole_spec(HALF, tokens),
        ],
        out_specs=[
            rows,
            whole_spec(HALF, tokens),
            whole_spec(tokens, HALF),
            whole_spec(8, tokens),
        ],
        out_shape=[
            shape((keys, WIDTH), BF16),
            shape((HALF, tokens), F32),
            shape((tokens, HALF), BF16),
            shape((8, tokens), F32),
        ],
        scratch_shapes=[
            pltpu.VMEM((8, tokens), F32),
            pltpu.VMEM((8, tokens), F32),
            pltpu.VMEM((HALF, tokens), F32),
        ],
        compiler_params=pltpu.CompilerParams(vmem_limit_bytes=20 * MIB),
        cost_estimate=attend_cost(tokens // 2, keys),
        name="attend_last",
    )(q, xc, wkv, bias, top, total, weighted)


def unit_places(chips, per, rows, core):
    units = chips * per * rows
    unit = lax.broadcasted_iota(jnp.int32, (WIDTH, units), 1)
    at = lax.broadcasted_iota(jnp.int32, (WIDTH, units), 0)
    chip, inside = unit // (per * rows), lax.rem(unit, rows)
    return (at == chip * (2 * rows) + core * rows + inside).astype(BF16)


def unit_bias(vecs, chips, per, rows):
    units = chips * per * rows

    def body(v_ref, out_ref):
        every = mm(v_ref[...].astype(BF16), unit_places(chips, per, rows, place()[3]))
        turn = lax.rem(lax.broadcasted_iota(jnp.int32, (16, units), 1) // rows, per)
        row = lax.broadcasted_iota(jnp.int32, (16, units), 0)
        out_ref[...] = column_sum(jnp.where(row == 9 + turn, every, 0.0))

    return kernel(body, (vecs,), (shape((1, units), F32),), "unit_bias", flops=10**8)[0]


def unit_rows(sums, chips, per, rows):
    units = chips * per * rows

    def body(s_ref, out_ref):
        turn = lax.rem(lax.broadcasted_iota(jnp.int32, (8, units), 1) // rows, per)
        row = lax.broadcasted_iota(jnp.int32, (8, units), 0)
        spread_out = jnp.where(row == turn, s_ref[...], 0.0).astype(BF16)
        out_ref[...] = mm_t(spread_out, unit_places(chips, per, rows, place()[3]))

    return kernel(body, (sums,), (shape((8, WIDTH), F32),), "unit_rows", flops=10**8)[0]


def norm_forward(residual, gain, shift):
    center = residual - jnp.mean(residual, axis=-1, keepdims=True)
    scale = lax.rsqrt(jnp.mean(center * center, axis=-1, keepdims=True) + EPSILON)
    normed = center * scale
    return normed * gain + shift, normed, scale


def norm_backward(grad_out, normed, scale, gain):
    grad_normed = grad_out * gain
    return scale * (
        grad_normed
        - jnp.mean(grad_normed, axis=-1, keepdims=True)
        - normed * jnp.mean(grad_normed * normed, axis=-1, keepdims=True)
    )


def column_sum(value):
    return jnp.sum(value, axis=0, keepdims=True)


def halves(core, own, other):
    left = jnp.where(core == 0, own, other)
    right = jnp.where(core == 0, other, own)
    return left, right


def mix(ctx, ctx_got, mixer_own, mixer_got, vecs, inputs):
    tokens = inputs.shape[0]

    def body(o_ref, g_ref, mo_ref, mg_ref, v_ref, x_ref, low_ref, row_ref, n_ref, s_ref):
        core = place()[3]
        mine = pl.ds(pl.multiple_of(core * HALF, HALF), HALF)
        others = pl.ds(pl.multiple_of((1 - core) * HALF, HALF), HALF)
        parts = [
            mm(o_ref[:tokens, :], ref[mine, :]) + mm(g_ref[tokens:, :], ref[others, :])
            for ref in (mo_ref, mg_ref)
        ]
        attended = jnp.concatenate(halves(core, *parts), axis=1) + v_ref[2:3, :]
        rows, normed, scale = norm_forward(
            x_ref[...].astype(F32) + attended, v_ref[3:4, :], v_ref[4:5, :]
        )
        low_ref[...] = rows.astype(BF16)
        row_ref[...] = rows
        n_ref[...] = normed
        s_ref[...] = scale

    return kernel(
        body,
        (ctx, ctx_got, mixer_own, mixer_got, vecs, inputs),
        (
            shape((tokens, WIDTH), BF16),
            shape((tokens, WIDTH), F32),
            shape((tokens, WIDTH), F32),
            shape((tokens, 1), F32),
        ),
        "mix",
        flops=10**9,
        bytes_accessed=3 * 10**6,
    )


def feed(own, got, w_inner, i_bias, w_outer):
    tokens = own.shape[0]
    units = w_inner.shape[1]

    def body(o_ref, g_ref, w1_ref, b_ref, w2_ref, two_ref, act_ref, slope_ref, mine_ref, send_ref):
        two_ref[:tokens, :] = o_ref[...]
        two_ref[tokens:, :] = g_ref[...]
        u = mm(two_ref[...], w1_ref[...]) + b_ref[...]
        cdf = 0.5 * (1.0 + lax.erf(u * ROOT_HALF))
        slope_ref[...] = cdf + u * jnp.exp(-0.5 * u * u) * GAUSS_FACTOR
        act_ref[...] = (u * cdf).astype(BF16)
        part = mm(act_ref[...], w2_ref[...])
        mine_ref[...] = part[:tokens]
        send_ref[...] = part[tokens:]

    return kernel(
        body,
        (own, got, w_inner, i_bias, w_outer),
        (
            shape((2 * tokens, WIDTH), BF16),
            shape((2 * tokens, units), BF16),
            shape((2 * tokens, units), F32),
            shape((tokens, WIDTH), F32),
            shape((tokens, WIDTH), F32),
        ),
        "feed",
        flops=3 * 10**9,
        bytes_accessed=8 * 10**6,
    )


def crown(mine, got, first_rows, vecs, out_cot, term_cot):
    tokens = mine.shape[0]

    def body(
        m_ref, g_ref, f_ref, v_ref, oc_ref, tc_ref, out_ref, term_ref, gs_ref, go_ref, sum_ref
    ):
        gain = v_ref[6:7, :]
        head = v_ref[8:9, :]
        outer = m_ref[...] + g_ref[...] + v_ref[5:6, :]
        rows, normed, scale = norm_forward(f_ref[...] + outer, gain, v_ref[7:8, :])
        out_ref[...] = rows.astype(BF16)
        logits = jnp.sum(rows * head, axis=-1, keepdims=True)
        small = jnp.exp(-jnp.abs(logits))
        term = jnp.maximum(logits, 0.0) + jnp.log1p(small)
        term_ref[...] = jnp.transpose(jnp.broadcast_to(term, (tokens, 128)))[0:1, :]
        sig = jnp.where(logits >= 0.0, 1.0, small) / (1.0 + small)
        cot = jnp.transpose(jnp.broadcast_to(tc_ref[...], (128, tokens)))[:, 0:1]
        slope = cot * sig
        grad_final = oc_ref[...].astype(F32) + slope * head
        grad = norm_backward(grad_final, normed, scale, gain)
        low = grad.astype(BF16)
        gs_ref[...] = grad
        go_ref[...] = low
        sum_ref[...] = jnp.concatenate(
            [
                column_sum(low.astype(F32)),
                column_sum(grad_final * normed),
                column_sum(grad_final),
                column_sum(slope * rows),
                jnp.zeros((4, WIDTH), F32),
            ],
            axis=0,
        )

    return kernel(
        body,
        (mine, got, first_rows, vecs, out_cot, term_cot),
        (
            shape((tokens, WIDTH), BF16),
            shape((1, tokens), F32),
            shape((tokens, WIDTH), F32),
            shape((tokens, WIDTH), BF16),
            shape((8, WIDTH), F32),
        ),
        "crown",
        flops=10**8,
        bytes_accessed=3 * 10**6,
    )


def feed_back(own, got, slope, w_inner, w_outer):
    tokens = own.shape[0]
    units = w_inner.shape[1]

    def body(o_ref, g_ref, s_ref, w1_ref, w2_ref, two_ref, gi_ref, mine_ref, send_ref, sum_ref):
        two_ref[:tokens, :] = o_ref[...]
        two_ref[tokens:, :] = g_ref[...]
        low = (mm_t(two_ref[...], w2_ref[...]) * s_ref[...]).astype(BF16)
        gi_ref[...] = low
        sum_ref[...] = column_sum(low.astype(F32))
        part = mm_t(gi_ref[...], w1_ref[...])
        mine_ref[...] = part[:tokens]
        send_ref[...] = part[tokens:]

    return kernel(
        body,
        (own, got, slope, w_inner, w_outer),
        (
            shape((2 * tokens, WIDTH), BF16),
            shape((2 * tokens, units), BF16),
            shape((tokens, WIDTH), F32),
            shape((tokens, WIDTH), F32),
            shape((1, units), F32),
        ),
        "feed_back",
        flops=3 * 10**9,
        bytes_accessed=8 * 10**6,
    )


def mix_back(mine, got, grad_second, normed, scale, vecs, mixer_own, mixer_got):
    tokens = mine.shape[0]

    def body(
        m_ref, g_ref, gs_ref, n_ref, s_ref, v_ref, mo_ref, mg_ref, res_ref, keep_ref, send_ref, sum_ref
    ):
        core = place()[3]
        first = gs_ref[...] + m_ref[...] + g_ref[...]
        normal = n_ref[...]
        grad = norm_backward(first, normal, s_ref[...], v_ref[3:4, :])
        res_ref[...] = grad
        low = grad.astype(BF16)
        sum_ref[...] = jnp.concatenate(
            [
                column_sum(low.astype(F32)),
                column_sum(first * normal),
                column_sum(first),
                jnp.zeros((5, WIDTH), F32),
            ],
            axis=0,
        )
        mine_low, other_low = halves(core, low[:, :HALF], low[:, HALF:])
        ctx = (mm_t(mine_low, mo_ref[...]) + mm_t(other_low, mg_ref[...])).astype(BF16)
        mine_ctx, other_ctx = halves(core, ctx[:, :HALF], ctx[:, HALF:])
        keep_ref[:, :HALF] = mine_ctx
        keep_ref[:, HALF:] = mine_low
        send_ref[:, :HALF] = other_ctx
        send_ref[:, HALF:] = other_low

    return kernel(
        body,
        (mine, got, grad_second, normed, scale, vecs, mixer_own, mixer_got),
        (
            shape((tokens, WIDTH), F32),
            shape((tokens, WIDTH), BF16),
            shape((tokens, WIDTH), BF16),
            shape((8, WIDTH), F32),
        ),
        "mix_back",
        flops=10**9,
        bytes_accessed=4 * 10**6,
    )


def attend_back_step(q_ref, g_ref, lse_ref, delta_ref, kv_ref, out_ref, acc_ref, sum_ref):
    held = []
    for h in range(NH):
        lo = h * HD
        qh = q_ref[:, lo : lo + HD]
        gh = g_ref[:, lo : lo + HD]
        kh = kv_ref[:, lo : lo + HD]
        vh = kv_ref[:, HALF + lo : HALF + lo + HD]
        p = jnp.exp(mm_t(kh, qh) - lse_ref[h : h + 1, :])
        dp = mm_t(vh, gh)
        ds = (p * (dp - delta_ref[h : h + 1, :])).astype(BF16)
        acc_ref[lo : lo + HD, :] += t_mm(kh, ds)
        held.append((mm(ds, qh).astype(BF16), mm(p.astype(BF16), gh).astype(BF16)))
        if h % 2 == 1:
            (dk0, dv0), (dk1, dv1) = held
            held = []
            at = lo - HD
            dv = jnp.concatenate([dv0, dv1], axis=1)
            out_ref[:, at : at + 2 * HD] = jnp.concatenate([dk0, dk1], axis=1)
            out_ref[:, HALF + at : HALF + at + 2 * HD] = dv
            sum_ref[1:2, at : at + 2 * HD] += column_sum(dv.astype(F32))


def attend_back_cost(tokens, keys):
    return pl.CostEstimate(flops=1, bytes_accessed=1, transcendentals=0)


def attend_back_first(q, low, low_got, o, lse, kv):
    tokens, keys = q.shape[0], kv.shape[0]
    block = math.gcd(keys, 1024)
    rows = pl.BlockSpec((block, WIDTH), lambda i: (i, 0))

    def body(q_ref, go_ref, gc_ref, o_ref, lse_ref, kv_ref, d_ref, g_ref, delta_ref, acc_ref, sum_ref):
        @pl.when(pl.program_id(0) == 0)
        def _():
            acc_ref[...] = jnp.zeros(acc_ref.shape, F32)
            sum_ref[...] = jnp.zeros(sum_ref.shape, F32)
            g_ref[: tokens // 2, :] = go_ref[:, :HALF]
            g_ref[tokens // 2 :, :] = gc_ref[:, :HALF]
            prod = jnp.transpose(g_ref[...].astype(F32)) * o_ref[...]
            for h in range(NH):
                delta_ref[h : h + 1, :] = column_sum(prod[h * HD : (h + 1) * HD, :])

        attend_back_step(q_ref, g_ref, lse_ref, delta_ref, kv_ref, d_ref, acc_ref, sum_ref)

    return pl.pallas_call(
        body,
        grid=(keys // block,),
        in_specs=[
            whole_spec(tokens, HALF),
            whole_spec(tokens // 2, WIDTH),
            whole_spec(tokens // 2, WIDTH),
            whole_spec(HALF, tokens),
            whole_spec(8, tokens),
            rows,
        ],
        out_specs=[
            rows,
            whole_spec(tokens, HALF),
            whole_spec(8, tokens),
            whole_spec(HALF, tokens),
            whole_spec(8, HALF),
        ],
        out_shape=[
            shape((keys, WIDTH), BF16),
            shape((tokens, HALF), BF16),
            shape((8, tokens), F32),
            shape((HALF, tokens), F32),
            shape((8, HALF), F32),
        ],
        compiler_params=pltpu.CompilerParams(vmem_limit_bytes=20 * MIB),
        cost_estimate=attend_back_cost(tokens, keys),
        name="attend_back_first",
    )(q, low, low_got, o, lse, kv)


def attend_back_last(q, g, lse, delta, acc, sums, kv, wq):
    tokens, keys = q.shape[0], kv.shape[0]
    block = math.gcd(keys, 1024)
    rows = pl.BlockSpec((block, WIDTH), lambda i: (i, 0))

    def body(q_ref, g_ref, lse_ref, delta_ref, ai_ref, si_ref, kv_ref, w_ref, d_ref, dq_ref, sum_ref, send_ref, acc_s):
        @pl.when(pl.program_id(0) == 0)
        def _():
            acc_s[...] = ai_ref[...]
            sum_ref[...] = si_ref[...]

        attend_back_step(q_ref, g_ref, lse_ref, delta_ref, kv_ref, d_ref, acc_s, sum_ref)

        @pl.when(pl.program_id(0) == pl.num_programs(0) - 1)
        def _():
            dq = jnp.transpose(acc_s[...] * 0.125).astype(BF16)
            dq_ref[...] = dq
            sum_ref[0:1, :] = column_sum(dq.astype(F32))
            send_ref[...] = mm_t(dq[tokens // 2 :], w_ref[:, :HALF]).astype(BF16)

    return pl.pallas_call(
        body,
        grid=(keys // block,),
        in_specs=[
            whole_spec(tokens, HALF),
            whole_spec(tokens, HALF),
            whole_spec(8, tokens),
            whole_spec(8, tokens),
            whole_spec(HALF, tokens),
            whole_spec(8, HALF),
            rows,
            whole_spec(*wq.shape),
        ],
        out_specs=[
            rows,
            whole_spec(tokens, HALF),
            whole_spec(8, HALF),
            whole_spec(tokens // 2, WIDTH),
        ],
        out_shape=[
            shape((keys, WIDTH), BF16),
            shape((tokens, HALF), BF16),
            shape((8, HALF), F32),
            shape((tokens // 2, WIDTH), BF16),
        ],
        scratch_shapes=[pltpu.VMEM((HALF, tokens), F32)],
        compiler_params=pltpu.CompilerParams(vmem_limit_bytes=20 * MIB),
        cost_estimate=attend_back_cost(tokens, keys),
        name="attend_back_last",
    )(q, g, lse, delta, acc, sums, kv, wq)


def input_part_other(dkv, wkv):
    keys = dkv.shape[0]
    block = math.gcd(keys, 1024)
    rows = pl.BlockSpec((block, WIDTH), lambda i: (i, 0))

    def body(d_ref, w_ref, out_ref):
        out_ref[...] = mm_t(d_ref[...], w_ref[...]).astype(BF16)

    return pl.pallas_call(
        body,
        grid=(keys // block,),
        in_specs=[rows, whole_spec(*wkv.shape)],
        out_specs=rows,
        out_shape=shape((keys, WIDTH), BF16),
        compiler_params=pltpu.CompilerParams(vmem_limit_bytes=12 * MIB),
        cost_estimate=pl.CostEstimate(flops=1, bytes_accessed=1, transcendentals=0),
        name="input_part_other",
    )(dkv, wkv)


def input_part_own(dkv, wkv, got, dq, wq, q_got):
    keys = dkv.shape[0]
    tokens = q_got.shape[0]
    block = math.gcd(keys // 2, 512)
    half = keys // 2 // block
    rows = pl.BlockSpec((block, WIDTH), lambda i: (i, 0))

    def body(d_ref, w_ref, g_ref, dq_ref, wq_ref, qg_ref, keep_ref, send_ref, part_s):
        step = pl.program_id(0)
        part_s[...] = mm_t(d_ref[...], w_ref[...]) + g_ref[...].astype(F32)

        @pl.when(step == 0)
        def _():
            part_s[:tokens, :] += mm_t(dq_ref[:tokens, :], wq_ref[:, :HALF]) + qg_ref[...].astype(
                F32
            )

        @pl.when(step < half)
        def _():
            keep_ref[...] = part_s[...].astype(BF16)

        @pl.when(step >= half)
        def _():
            send_ref[...] = part_s[...].astype(BF16)

    return pl.pallas_call(
        body,
        grid=(2 * half,),
        in_specs=[
            rows,
            whole_spec(*wkv.shape),
            rows,
            whole_spec(*dq.shape),
            whole_spec(*wq.shape),
            whole_spec(*q_got.shape),
        ],
        out_specs=[
            pl.BlockSpec((block, WIDTH), lambda i: (jnp.minimum(i, half - 1), 0)),
            pl.BlockSpec((block, WIDTH), lambda i: (jnp.maximum(i - half, 0), 0)),
        ],
        out_shape=[shape((keys // 2, WIDTH), BF16)] * 2,
        scratch_shapes=[pltpu.VMEM((block, WIDTH), F32)],
        compiler_params=pltpu.CompilerParams(vmem_limit_bytes=12 * MIB),
        cost_estimate=pl.CostEstimate(flops=1, bytes_accessed=1, transcendentals=0),
        name="input_part_own",
    )(dkv, wkv, got, dq, wq, q_got)


def spread(zs, rows, cols, args, fill, name, scratch, limit=14):
    count = len(args)

    def body(*refs):
        ins, outs, held = refs[:count], refs[count : count + 4], refs[count + 4 :]
        write = fill(ins, held)
        here = place()
        for k in range(zs):
            for side in range(4):
                write(outs[side], k, chip_of(here, side // 2, side % 2, k, zs))

    return kernel(
        body,
        args,
        [shape((zs, rows, cols), BF16)] * 4,
        name,
        limit=limit,
        scratch=[pltpu.VMEM(dims, BF16) for dims in scratch],
        flops=2 * 10**9,
        bytes_accessed=6 * 10**6,
    )


def spread_slow(full, zs):
    full = to_distance(full.reshape(2, zs, 2, *full.shape[1:]))
    full = full.reshape(4, zs, *full.shape[3:])
    return full[0], full[1], full[2], full[3]


def spread_rest(first2, grad_inner, active, grad_outer2, zs):
    units = active.shape[1]
    rows, hidden = WIDTH // (4 * zs), units // (4 * zs)
    if rows % 16:
        w1 = t_mm(first2, grad_inner).astype(BF16).reshape(4 * zs, rows, units)
        w2 = t_mm(active, grad_outer2).astype(BF16).reshape(4 * zs, hidden, WIDTH)
        return spread_slow(jnp.concatenate([w1[:, :, :WIDTH], w1[:, :, WIDTH:], w2], axis=1), zs)

    late = hidden // 2
    most = 2 * rows + hidden - late

    def body(f_ref, gi_ref, a_ref, go_ref, *outs):
        outs, late_ref, (w1_s, w2_s) = outs[:4], outs[4], outs[5:]
        w1_s[...] = t_mm(f_ref[...], gi_ref[...]).astype(BF16)
        w2_s[...] = t_mm(a_ref[...], go_ref[...]).astype(BF16)
        here = place()
        for k in range(zs):
            for side in range(4):
                chip = chip_of(here, side // 2, side % 2, k, zs)
                at, down = rows_at(chip, rows), chip * hidden
                outs[side][k, :rows, :] = w1_s[at, :WIDTH]
                outs[side][k, rows : 2 * rows, :] = w1_s[at, WIDTH:]
                outs[side][k, 2 * rows :, :] = w2_s[pl.ds(pl.multiple_of(down, 16), hidden - late), :]
                late_ref[k, side] = w2_s[pl.ds(pl.multiple_of(down + hidden - late, 16), late), :]

    return kernel(
        body,
        (first2, grad_inner, active, grad_outer2),
        [shape((zs, most, WIDTH), BF16)] * 4 + [shape((zs, 4, late, WIDTH), BF16)],
        "spread_rest",
        scratch=[pltpu.VMEM((WIDTH, units), BF16), pltpu.VMEM((units, WIDTH), BF16)],
    )


def spread_qkv(zs, x_own, x_got, dq, qv, mid, top, unit, g_kv, ctx, ctx_got, low, low_got):
    tokens = x_own.shape[0]
    rows = WIDTH // (4 * zs)
    cols = WIDE + WIDTH + HALF

    def fill(ins, held):
        part_s = held[0]
        xo, xg, dq_r, qv_r, mid_r, top_r, unit_r, c_r, cg_r, l_r, lg_r, *kv_rs = ins
        core = place()[3]
        part_s[:, :HALF] = (
            t_mm(xo[...], dq_r[:tokens, :]) + t_mm(xg[...], dq_r[tokens:, :])
        ).astype(BF16)
        zero = jnp.zeros((2, HALF), F32)
        sums = jnp.concatenate(
            [
                jnp.concatenate(halves(core, qv_r[0:2, :], zero), axis=1),
                mid_r[0:3, :],
                top_r[0:4, :],
                unit_r[...],
                jnp.zeros((AUX - 17, WIDTH), F32),
            ],
            axis=0,
        )
        part_s[:, HALF:WIDE] = jnp.transpose(sums).astype(BF16)
        if len(kv_rs) == 1:
            part_s[:, WIDE : WIDE + WIDTH] = kv_rs[0][...]
        else:
            xk, dk, xl, dl = kv_rs
            part_s[:, WIDE : WIDE + WIDTH] = (t_mm(xk[...], dk[...]) + t_mm(xl[...], dl[...])).astype(
                BF16
            )
        lows = (l_r[:, HALF:], lg_r[:, HALF:])
        part_s[pl.ds(pl.multiple_of(core * HALF, HALF), HALF), WIDE + WIDTH :] = (
            t_mm(c_r[:tokens, :], lows[0]) + t_mm(c_r[tokens:, :], lows[1])
        ).astype(BF16)
        part_s[pl.ds(pl.multiple_of((1 - core) * HALF, HALF), HALF), WIDE + WIDTH :] = (
            t_mm(cg_r[tokens:, :], lows[0]) + t_mm(cg_r[:tokens, :], lows[1])
        ).astype(BF16)

        def write(out, n, chip):
            out[n] = part_s[rows_at(chip, rows), :]

        return write

    args = (x_own, x_got, dq, qv, mid, top, unit, ctx, ctx_got, low, low_got, *g_kv)
    if rows % 16 == 0:
        return spread(zs, rows, cols, args, fill, "spread_qkv", ((WIDTH, cols),), 24)

    def body(*refs):
        fill(refs[:12], refs[12:])

    full = kernel(body, args, [shape((WIDTH, cols), BF16)], "fill_qkv")[0]
    return spread_slow(full.reshape(4 * zs, rows, cols), zs)


def finish_sums(qkv, rest, more, rows):
    count, cols = len(qkv), qkv[0].shape[1]
    hidden = rest[0].shape[0] - 4 * rows
    wide = cols + 2 * WIDTH

    def body(*refs):
        ins, (own_ref, send_ref, outer_ref, both_s) = refs[:-4], refs[-4:]
        core = place()[3]
        both_s[:, :cols] = sum(ref[...].astype(F32) for ref in ins[:count])
        low = sum(ref[...].astype(F32) for ref in ins[count : count + len(rest)])
        if more:
            top = sum(ref[...].astype(F32) for ref in ins[count + len(rest) :])
            most = top.shape[0]
            low = jnp.concatenate([low[:most] + top, low[most:]], axis=0)
        both_s[:, cols : cols + WIDTH] = low[: 2 * rows]
        both_s[:, cols + WIDTH :] = low[2 * rows : 4 * rows]
        outer_ref[...] = low[4 * rows :]
        halves_of = (both_s[:rows, :], both_s[rows:, :])
        own_ref[...] = jnp.where(core == 0, *halves_of)
        send_ref[...] = jnp.where(core == 1, *halves_of)

    return kernel(
        body,
        (*qkv, *rest, *more),
        [shape((rows, wide), F32)] * 2 + [shape((hidden, WIDTH), F32)],
        "finish_sums",
        limit=8,
        scratch=[pltpu.VMEM((2 * rows, wide), F32)],
    )


def finish_rows(own, got, hidden, per):
    rows = own.shape[0]
    base = WIDE + WIDTH + HALF
    chips = (own.shape[1] - base) // hidden

    def body(own_ref, got_ref, *outs):
        core = place()[3]
        left = jnp.where(core == 0, own_ref[...], got_ref[...])
        right = jnp.where(core == 0, got_ref[...], own_ref[...])
        for out, lo in zip(outs, (0, WIDE, WIDE + HALF, WIDE + WIDTH)):
            out[:, :HALF] = left[:, lo : lo + HALF]
            out[:, HALF:] = right[:, lo : lo + HALF]
        outs[4][...] = jnp.concatenate(
            [
                side[:, base + i * hidden : base + (i + 1) * hidden]
                for i in range(chips)
                for side in (left, right)
            ],
            axis=1,
        )
        small = left[:, HALF:WIDE] + right[:, HALF:WIDE]
        if rows < AUX:
            small = jnp.concatenate([small, jnp.zeros((AUX - rows, AUX), F32)], axis=0)
        small = jnp.transpose(small)
        for j in range(9):
            outs[5 + j][...] = small[j, :rows]
        for j in range(per):
            outs[14][pl.ds(j * rows, rows)] = small[9 + j, :rows]

    outs = kernel(
        body,
        (own, got),
        [shape((rows, WIDTH), F32)] * 4
        + [shape((rows, 2 * chips * hidden), F32)]
        + [shape((rows,), F32)] * 9
        + [shape((hidden,), F32)],
        "finish_rows",
        limit=8,
    )
    return (*outs[:5], outs[5:])


def shards(
    layer_input,
    query_weight,
    query_bias,
    key_weight,
    value_weight,
    value_bias,
    mixer_weight,
    mixer_bias,
    first_gain,
    first_shift,
    inner_weight,
    inner_bias,
    outer_weight,
    outer_bias,
    second_gain,
    second_shift,
    head_weight,
    out_cotangent,
    term_cotangent,
):
    core = place()[3]
    chips = lax.axis_size("ctx")
    zs = chips // 4
    inputs = layer_input[0]
    tokens = inputs.shape[0]
    rows = query_weight.shape[0]
    hidden = outer_weight.shape[0]
    ff = inner_weight.shape[1]
    units = ff // 2
    per = hidden // rows

    def in_order(own, other, axis):
        return jnp.stack(halves(core, own, other), axis=axis)

    own, send = pack(
        (query_weight, key_weight, value_weight, mixer_weight),
        inner_weight,
        (
            query_bias,
            value_bias,
            mixer_bias,
            first_gain,
            first_shift,
            outer_bias,
            second_gain,
            second_shift,
            head_weight,
            inner_bias,
        ),
    )
    block, rest = join(own, swap_core(send), outer_weight)
    x_got = swap_core(inputs)
    first = 2 * rows * (units // HALF)
    most, part_far = first + hidden, 3 * first // 4
    every = tuple(range(zs))
    barrier = lax.optimization_barrier
    part_row = 2 * rows
    if zs == 4:
        near_y, near_x = swap_y(rest[None]), swap_x(rest[None])
        near_y, near_x, qkv = barrier((near_y, near_x, along_z_pieces(block)))
        x_own, first_piece = barrier((inputs, qkv[1]))
        qkv = jnp.stack([qkv[0], first_piece, *qkv[2:]])
        flat = qkv.reshape(first, -1)
        sent_y = swap_y(jnp.concatenate([flat, near_x[0, first:]], axis=1))
        sent_x = swap_x(jnp.concatenate([flat, near_y[0, :first]], axis=1))
        sent_y, sent_x, x_along = barrier((sent_y, sent_x, along_z_pieces(x_own)))
        x_along = jnp.stack(x_along)
        cols = flat.shape[1]
        qkv_y, qkv_x = (sent[:, :cols].reshape(qkv.shape) for sent in (sent_y, sent_x))
        near_far = [sent[None, :, cols:] for sent in (sent_x, sent_y)]
        rest_sent, x_along = barrier((rest[:most], x_along))
        x_y, qkv_far, pieces = barrier(
            (swap_y(x_along), far_out(qkv_y, qkv_x, part_row), along_z_pieces(rest_sent))
        )
        square = jnp.stack(
            [rest[most:], near_y[0, most:], near_x[0, most:], near_far[1][0, most - first :]]
        )
        pieces, square = barrier((jnp.stack(pieces[1:]), square))
        rest_y, rest_x = swap_y(pieces), swap_x(pieces)
    else:
        qkv, x_along, pieces = (along_z_pieces(v) for v in (block, inputs, rest))
        x_y, rest_y, rest_x = swap_y(x_along), swap_y(pieces), swap_x(pieces)
        qkv_y, qkv_x = swap_y(qkv), swap_x(qkv)
        qkv_far = far_out(qkv_y, qkv_x, part_row)
    wq, wkv, mixer_own = build_qkv(
        *sources([(every, qkv, qkv_y, qkv_x, *qkv_far)], part_row), part_row
    )
    mixer_got = swap_core(mixer_own)
    xo = jnp.concatenate([x_along, x_y]).reshape(2 * zs * tokens, WIDTH)
    xc = swap_core(xo)

    q_scaled, kvo, vecs, bias, top, total, weighted = attend_first(inputs, x_got, xo, wq, wkv)
    kvc, o_exact, ctx, lse = attend_last(q_scaled, xc, wkv, bias, top, total, weighted)
    if zs == 4:
        rest_y, rest_x, ctx, *late = barrier(
            (rest_y, rest_x, ctx, swap_z(square, 1), swap_z(square, 2))
        )
        w_inner, w_outer = build_split(
            (rest[None], near_y, near_x, *near_far),
            (pieces, rest_y, rest_x, *far_out(rest_y, rest_x, part_far)),
            (*late, swap_z(square, 3)),
            2 * rows,
            hidden,
            (part_far, first, most),
        )
    else:
        away = [(every, pieces, rest_y, rest_x, *far_out(rest_y, rest_x, first))]
        w_inner, w_outer = build_rest(*sources(away, first), 2 * rows, hidden)
    ctx_got = swap_core(ctx)
    i_bias = unit_bias(vecs, chips, per, rows)
    first_low, first_rows, first_normed, first_scale = mix(
        ctx, ctx_got, mixer_own, mixer_got, vecs, inputs
    )

    first2, active, slope, mine, away = feed(
        first_low, swap_core(first_low), w_inner, i_bias, w_outer
    )
    final_low, term, grad_second, grad_outer, top_sums = crown(
        mine, swap_core(away), first_rows, vecs, out_cotangent[0], term_cotangent
    )
    grad_outer2, grad_inner, mine, away, inner_sums = feed_back(
        grad_outer, swap_core(grad_outer), slope, w_inner, w_outer
    )
    got = swap_core(away)
    keep, rest_y, rest_x, far, *late = spread_rest(first2, grad_inner, active, grad_outer2, zs)
    mine, keep, rest_y, rest_x, far, *late = barrier((mine, keep, rest_y, rest_x, far, *late))
    part_far = far.shape[1] // 2
    over_x, over_y = swap_x(far[:, :part_far]), swap_y(far[:, part_far:])

    grad_residual, low, low_send, mid_sums = mix_back(
        mine, got, grad_second, first_normed, first_scale, vecs, mixer_own, mixer_got
    )
    low_got = swap_core(low_send)
    dkvc, g_both, delta, acc, qv_sums = attend_back_first(
        q_scaled, low, low_got, o_exact, lse, kvc
    )
    if zs == 4:
        (late,) = late
        over_x, over_y, dkvc, kvo, late_1, late_2, late_3, square = barrier(
            (over_x, over_y, dkvc, kvo, swap_z(late[1], 1), swap_z(late[2], 2), late[3], late[0])
        )
        late_3 = swap_z(late_3, 3)
    else:
        over_x, over_y, dkvc, kvo = barrier((over_x, over_y, dkvc, kvo))
    away = swap_core(input_part_other(dkvc, wkv))
    rest_y = jnp.concatenate([rest_y[:, : part_far] + over_x, rest_y[:, part_far :]], axis=1)
    rest_x = jnp.concatenate([rest_x[:, : part_far], rest_x[:, part_far :] + over_y], axis=1)
    at = 1 if zs == 4 else 0
    got_y, got_x = swap_y(rest_y[at:]), swap_x(rest_x[at:])
    dkvo, dq, qv_sums, q_away = attend_back_last(
        q_scaled, g_both, lse, delta, acc, qv_sums, kvo, wq
    )

    part, part_y = input_part_own(dkvo, wkv, away, dq, wq, swap_core(q_away))
    dq, dkvo, part, part_y = barrier((dq, dkvo, part, part_y))
    if zs == 4:
        g_kv = (xo, dkvo, xc, dkvc)
    else:
        g_kv = ((t_mm(xo, dkvo) + t_mm(xc, dkvc)).astype(BF16),)
    g_qkv, qkv_y, qkv_x, qkv_far = spread_qkv(
        zs,
        inputs,
        x_got,
        dq,
        qv_sums,
        mid_sums,
        top_sums,
        unit_rows(inner_sums, chips, per, rows),
        g_kv,
        ctx,
        ctx_got,
        low,
        low_got,
    )
    part, part_y = part.reshape(zs, tokens, WIDTH), part_y.reshape(zs, tokens, WIDTH)
    if zs == 4:
        got_y, got_x, part_y, qkv_far, late_3 = barrier((got_y, got_x, part_y, qkv_far, late_3))
        square = square + late_1 + late_2 + late_3
        g_rest = keep[1:] + got_y + got_x
        qkv_far, got_part, far, g_rest = barrier(
            (
                swap_x(qkv_far),
                swap_y(part_y),
                swap_x(square[3]),
                [swap_z(g_rest[k - 1], k) for k in range(1, zs)],
            )
        )
        part = part + got_part
        qkv_x, qkv_far = barrier((qkv_x, qkv_far))
        got_y, got_x, parts = barrier(
            (
                swap_y(qkv_y + qkv_far),
                swap_x(qkv_x),
                [swap_z(part[k], k) for k in range(1, zs)],
            )
        )
        near_y = jnp.concatenate([rest_y[0], square[1] + far])
        near_x = jnp.concatenate([rest_x[0], square[2]])
        near_y, near_x, parts = barrier((near_y, near_x, parts))
        total = part[0].astype(F32)
        for value in parts:
            total = total + value.astype(F32)
        g_qkv = g_qkv + got_y + got_x
        near_y, near_x, pieces = barrier(
            (
                swap_y(near_y),
                swap_x(near_x),
                [swap_z(g_qkv[k], k) for k in range(1, zs)],
            )
        )
        g_qkv = [g_qkv[0], *pieces]
        g_whole = [jnp.concatenate([keep[0], square[0]]), near_y, near_x]
    else:
        g_whole, g_rest = [sum_z([(every, keep + got_y + got_x)])], []
        part = part + swap_y(part_y)
        total = sum_z([(every, part)])
        qkv_y, qkv_x = fan_far(qkv_y, qkv_x, qkv_far, 2 * rows)
        g_qkv = [sum_z([(every, g_qkv + swap_y(qkv_y) + swap_x(qkv_x))])]
    input_grad = (grad_residual + total).astype(BF16)

    own, send, g_outer = finish_sums(g_qkv, g_whole, g_rest, rows)
    g_query, g_key, g_value, g_mixer, g_inner, vectors = finish_rows(
        own, swap_core(send), hidden, per
    )
    return (
        final_low[None],
        term,
        input_grad[None],
        g_query,
        vectors[0],
        g_key,
        g_value,
        vectors[1],
        g_mixer,
        vectors[2],
        vectors[3],
        vectors[4],
        g_inner,
        vectors[9],
        g_outer,
        vectors[5],
        vectors[6],
        vectors[7],
        vectors[8],
    )


def pick(value, index, axis):
    return lax.dynamic_index_in_dim(value, index, axis, keepdims=False)


def solution(mesh):
    both = ("seq", "ctx")
    tok, mat, vec = P("seq", "ctx", None), P(both, None), P(both)
    term = P("seq", "ctx")
    in_specs = (
        tok, mat, vec, mat, mat, vec, mat, vec, vec, vec,
        mat, vec, mat, vec, vec, vec, vec, tok, term,
    )
    out_specs = (
        tok, term, tok, mat, vec, mat, mat, vec, mat, vec,
        vec, vec, mat, vec, mat, vec, vec, vec, vec,
    )
    return jax.shard_map(
        shards, mesh=mesh, in_specs=in_specs, out_specs=out_specs, check_vma=False
    )
```

```python
import math

import jax
import jax.numpy as jnp
from jax import lax
from jax.experimental import pallas as pl
from jax.experimental.pallas import tpu as pltpu
from jax.sharding import PartitionSpec as P

HEADS = 12
HD = 64
WIDTH = HEADS * HD
HALF = WIDTH // 2
NH = HEADS // 2
EPSILON = 1e-12
ROOT_HALF = 0.7071067811865476
GAUSS_FACTOR = 0.3989422804014327
F32 = jnp.float32
BF16 = jnp.bfloat16
AUX = 128
WIDE = HALF + AUX
MIB = 2**20


def mm(a, b):
    return lax.dot_general(a, b, (((1,), (0,)), ((), ())), preferred_element_type=F32)


def mm_t(a, b):
    return lax.dot_general(a, b, (((1,), (1,)), ((), ())), preferred_element_type=F32)


def t_mm(a, b):
    return lax.dot_general(a, b, (((0,), (0,)), ((), ())), preferred_element_type=F32)


def shape(dims, dtype):
    return jax.ShapeDtypeStruct(dims, dtype)


def swap_ctx(value, bit):
    n = lax.axis_size("ctx")
    return lax.ppermute(value, "ctx", [(i, i ^ bit) for i in range(n)])


def swap_core(value):
    return swap_ctx(value, 1)


def swap_y(value):
    return swap_ctx(value, 2)


def swap_x(value):
    return lax.ppermute(value, "seq", [(0, 1), (1, 0)])


def swap_z(value, k):
    return swap_ctx(value, 4 * k)


def place():
    at = lax.axis_index("ctx")
    return lax.axis_index("seq"), at // 4, (at // 2) % 2, at % 2


def z_groups():
    n = lax.axis_size("ctx")
    return [[i + 4 * j for j in range(n // 4)] for i in range(4)]


def turned(blocks, z, axis=0):
    zs = blocks.shape[axis]
    lead = blocks.shape[:axis]
    rest = blocks.shape[axis + 1 :]
    bit = 1
    while bit < zs:
        pairs = blocks.reshape(*lead, zs // (2 * bit), 2, bit, *rest)
        flipped = jnp.flip(pairs, len(lead) + 1)
        blocks = jnp.where((z & bit) == 0, pairs, flipped).reshape(*lead, zs, *rest)
        bit *= 2
    return blocks


def along_z_pieces(block):
    zs = lax.axis_size("ctx") // 4
    if zs > 4:
        every = lax.all_gather(block, "ctx", axis_index_groups=z_groups())
        return turned(every, lax.axis_index("ctx") // 4)
    return [block] + [swap_z(block, k) for k in range(1, zs)]


def far_out(by_y, by_x, row):
    if row == by_y.shape[1]:
        return (swap_x(by_y),)
    return swap_x(by_y[:, :row]), swap_y(by_x[:, row:])


def sources(groups, row):
    arrays, where = [], {}
    for ks, *blocks in groups:
        at = len(arrays)
        arrays += blocks
        for i, k in enumerate(ks):
            last = ((at + 3, i), (at + 4, i, row)) if len(blocks) > 4 else ((at + 3, i), (at + 3, i, 0))
            where[k] = (*(((at + j, i), (at + j, i, 0)) for j in range(3)), last)
    return arrays, where


def by_distance(arrays, where, row=0):
    def whole(first, rest):
        top = arrays[first[0]][first[1]][:row]
        return jnp.concatenate([top, arrays[rest[0]][rest[1]][row - rest[2] :]])

    blocks = [[whole(*side) for side in where[k]] for k in sorted(where)]
    full = jnp.stack([jnp.stack(four) for four in blocks], axis=1)
    return full.reshape(2, 2, *full.shape[1:])


def fan_far(by_y, by_x, far, row):
    if row == far.shape[1]:
        return by_y + swap_x(far), by_x
    over_x, over_y = swap_x(far[:, :row]), swap_y(far[:, row:])
    by_y = jnp.concatenate([by_y[:, :row] + over_x, by_y[:, row:]], axis=1)
    by_x = jnp.concatenate([by_x[:, :row], by_x[:, row:] + over_y], axis=1)
    return by_y, by_x


def sum_z(groups):
    zs = lax.axis_size("ctx") // 4
    if zs > 4:
        ((_, along),) = groups
        every = turned(along, lax.axis_index("ctx") // 4)
        every = lax.all_to_all(every, "ctx", 0, 0, axis_index_groups=z_groups())
        return jnp.sum(every.astype(F32), axis=0)
    total = None
    for ks, blocks in groups:
        for i, k in enumerate(ks):
            part = (blocks[i] if k == 0 else swap_z(blocks[i], k)).astype(F32)
            total = part if total is None else total + part
    return total


def to_mesh_order(blocks):
    x, z, y, _ = place()
    blocks = turned(blocks, z, 2)
    for axis, bit in enumerate((x, y)):
        blocks = jnp.where(bit == 0, blocks, jnp.flip(blocks, axis))
    return jnp.swapaxes(blocks, 1, 2)


def to_distance(blocks):
    x, z, y, _ = place()
    blocks = turned(jnp.swapaxes(blocks, 1, 2), z, 2)
    for axis, bit in enumerate((x, y)):
        blocks = jnp.where(bit == 0, blocks, jnp.flip(blocks, axis))
    return blocks


def chip_of(here, xr, yr, k, zs):
    x, z, y, _ = here
    return ((x ^ xr) * zs + (z ^ k)) * 2 + (y ^ yr)


def rows_at(chip, rows):
    return pl.ds(pl.multiple_of(chip * rows, 16), rows)


def kernel(body, args, outs, name, limit=14, scratch=(), flops=0, bytes_accessed=0):
    return pl.pallas_call(
        body,
        in_specs=[pl.BlockSpec(memory_space=pltpu.VMEM) for _ in args],
        out_specs=[pl.BlockSpec(memory_space=pltpu.VMEM) for _ in outs],
        out_shape=list(outs),
        scratch_shapes=list(scratch),
        compiler_params=pltpu.CompilerParams(vmem_limit_bytes=limit * MIB),
        cost_estimate=pl.CostEstimate(flops=1, bytes_accessed=1, transcendentals=0),
        name=name,
    )(*args)


def pack(weights, inner, vectors):
    rows, hidden = inner.shape[0], vectors[-1].shape[0]
    count = len(weights)
    every = (*weights, inner, *vectors)
    base = WIDE + WIDTH + HALF
    chips = inner.shape[1] // (2 * hidden)
    cols = base + chips * hidden

    def body(*refs):
        n = len(every)
        ins, (own_ref, send_ref), held = refs[:n], refs[n : n + 2], refs[n + 2 : 2 * n + 2]
        flat_s, sems = refs[-2:]
        copies = [pltpu.make_async_copy(i, h, sems.at[j]) for j, (i, h) in enumerate(zip(ins, held))]
        for copy in copies:
            copy.start()
        flat_s[...] = jnp.zeros(flat_s.shape, F32)
        for copy in copies:
            copy.wait()
        ws, inner_ref, vs = held[:count], held[count], held[count + 1 :]
        core = place()[3]
        at = 0
        for v in vs:
            for j in range(v.shape[0] // rows):
                flat_s[at : at + 1, :rows] = v[pl.ds(j * rows, rows)].astype(F32).reshape(1, rows)
                at += 1
        aux = jnp.transpose(flat_s[...])[:rows, :].astype(BF16)
        places = (0, WIDE, WIDE + HALF, WIDE + WIDTH)
        whole = inner_ref[...]
        units = [
            jnp.concatenate(
                [
                    whole[:, (2 * i + side) * hidden : (2 * i + side + 1) * hidden]
                    for i in range(chips)
                ],
                axis=1,
            )
            for side in range(2)
        ]
        for out, side in ((own_ref, core), (send_ref, 1 - core)):
            out[:, HALF:WIDE] = aux
            for w, lo in zip(ws, places):
                out[:, lo : lo + HALF] = jnp.where(side == 0, w[:, :HALF], w[:, HALF:])
            out[:, base:] = jnp.where(side == 0, units[0], units[1])

    return pl.pallas_call(
        body,
        in_specs=[pl.BlockSpec(memory_space=pl.ANY) for _ in every],
        out_specs=[pl.BlockSpec(memory_space=pltpu.VMEM)] * 2,
        out_shape=[shape((rows, cols), BF16)] * 2,
        scratch_shapes=[pltpu.VMEM(a.shape, BF16) for a in every]
        + [pltpu.VMEM((AUX, AUX), F32), pltpu.SemaphoreType.DMA((len(every),))],
        compiler_params=pltpu.CompilerParams(vmem_limit_bytes=56 * MIB),
        name="pack",
    )(*every)


def join(own, got, outer):
    rows, hidden = own.shape[0], outer.shape[0]
    base = WIDE + WIDTH + HALF
    quarters = (own.shape[1] - base) // HALF
    core = place()[3]
    both = jnp.concatenate(halves(core, own, got))
    return both[:, :base], jnp.concatenate(
        [both[:, base + j * HALF : base + (j + 1) * HALF] for j in range(quarters)]
        + [outer[:, :HALF], outer[:, HALF:]]
    )


def build_qkv(arrays, where, row):
    zs, rows = len(where), arrays[0].shape[1]
    ends = (0, WIDE, WIDE + WIDTH, WIDE + WIDTH + HALF)
    if rows % 16:
        full = to_mesh_order(by_distance(arrays, where, row)).reshape(WIDTH, -1)
        return [full[:, lo:hi] for lo, hi in zip(ends, ends[1:])]

    def body(*refs):
        outs = refs[len(arrays) :]
        here = place()
        for k in range(zs):
            for side, ((a, i), (b, n, back)) in enumerate(where[k]):
                at = chip_of(here, side // 2, side % 2, k, zs) * rows
                top = pl.ds(pl.multiple_of(at, 16), row)
                for out, lo, hi in zip(outs, ends, ends[1:]):
                    out[top, :] = refs[a][i, :row, lo:hi]

    return kernel(
        body,
        arrays,
        [shape((WIDTH, hi - lo), BF16) for lo, hi in zip(ends, ends[1:])],
        "build_qkv",
        flops=10**6,
        bytes_accessed=4 * 10**6,
    )


def build_split(near, far, late, rows, hidden, cuts):
    zs = len(late) + 1
    quarters = zs * 4 * hidden // HALF
    count = len(near) + len(far)

    def body(*refs):
        nears, fars, lates = refs[: len(near)], refs[len(near) : count], refs[count:-2]
        w1_ref, w2_ref = refs[-2:]
        here = place()

        def read(k, side, lo, n):
            if k > 0 and lo >= cuts[2]:
                return lates[k - 1][side, lo - cuts[2] : lo - cuts[2] + n, :]
            refs_of, at, row = (nears, 0, cuts[1]) if k == 0 else (fars, k - 1, cuts[0])
            if side < 3:
                return refs_of[side][at, lo : lo + n, :]
            if lo < row:
                return refs_of[3][at, lo : lo + n, :]
            return refs_of[4][at, lo - row : lo - row + n, :]

        for k in range(zs):
            for side in range(4):
                chip = chip_of(here, side // 2, side % 2, k, zs)
                to, down = rows_at(chip, rows), rows_at(chip, hidden)
                for j in range(quarters):
                    w1_ref[to, j * HALF : (j + 1) * HALF] = read(k, side, j * rows, rows)
                lo = quarters * rows
                w2_ref[down, :HALF] = read(k, side, lo, hidden)
                lo += hidden
                part = cuts[2] - lo
                down = pl.ds(pl.multiple_of(chip * hidden, 16), part)
                w2_ref[down, HALF:] = read(k, side, lo, part)
                down = pl.ds(pl.multiple_of(chip * hidden + part, 16), hidden - part)
                w2_ref[down, HALF:] = read(k, side, lo + part, hidden - part)

    return kernel(
        body,
        (*near, *far, *late),
        (shape((WIDTH, zs * 4 * hidden), BF16), shape((zs * 4 * hidden, WIDTH), BF16)),
        "build_split",
    )


def build_rest(arrays, where, rows, hidden):
    zs = len(where)
    units = zs * 4 * hidden
    quarters = units // HALF
    first = quarters * rows
    if rows % 16:
        full = to_mesh_order(by_distance(arrays, where, first)).reshape(4 * zs, -1, HALF)
        w1 = jnp.swapaxes(full[:, :first].reshape(4 * zs, quarters, rows, HALF), 1, 2)
        w2 = jnp.swapaxes(full[:, first:].reshape(4 * zs, 2, hidden, HALF), 1, 2)
        return w1.reshape(WIDTH, units), w2.reshape(units, WIDTH)

    def body(*refs):
        w1_ref, w2_ref = refs[len(arrays) :]
        here = place()
        for k in range(zs):
            for side, ((a, i), (b, n, back)) in enumerate(where[k]):
                chip = chip_of(here, side // 2, side % 2, k, zs)
                to, down = rows_at(chip, rows), rows_at(chip, hidden)
                for j in range(quarters):
                    w1_ref[to, j * HALF : (j + 1) * HALF] = refs[a][i, j * rows : (j + 1) * rows, :]
                for j in range(2):
                    lo = first + j * hidden - back
                    w2_ref[down, j * HALF : (j + 1) * HALF] = refs[b][n, lo : lo + hidden, :]

    return kernel(
        body,
        arrays,
        (shape((WIDTH, units), BF16), shape((units, WIDTH), BF16)),
        "build_rest",
        flops=10**6,
        bytes_accessed=10**7,
    )


def whole_spec(*dims):
    return pl.BlockSpec(dims, lambda i: (0,) * len(dims))


def attend_step(q_ref, kv_ref, m_ref, l_ref, acc_ref):
    for h in range(NH):
        lo = h * HD
        qh = q_ref[:, lo : lo + HD]
        kh = kv_ref[:, lo : lo + HD]
        vh = kv_ref[:, HALF + lo : HALF + lo + HD]
        s = mm_t(kh, qh)
        before = m_ref[h : h + 1, :]
        top = jnp.maximum(before, jnp.max(s, axis=0, keepdims=True))
        p = jnp.exp(s - top)
        factor = jnp.exp(before - top)
        m_ref[h : h + 1, :] = top
        l_ref[h : h + 1, :] = l_ref[h : h + 1, :] * factor + jnp.sum(p, axis=0, keepdims=True)
        acc_ref[lo : lo + HD, :] = acc_ref[lo : lo + HD, :] * factor + t_mm(vh, p.astype(BF16))


def keys_values(x_ref, w_ref, v_bias, kv_ref):
    kv_ref[:, :HALF] = mm(x_ref[...], w_ref[:, :HALF]).astype(BF16)
    kv_ref[:, HALF:] = (mm(x_ref[...], w_ref[:, HALF:]) + v_bias).astype(BF16)


def attend_cost(tokens, keys):
    return pl.CostEstimate(flops=1, bytes_accessed=1, transcendentals=0)


def attend_first(own, got, xo, wq, wkv):
    tokens, keys = own.shape[0], xo.shape[0]
    block = math.gcd(keys, 1024)
    rows = pl.BlockSpec((block, WIDTH), lambda i: (i, 0))

    def body(o_ref, g_ref, x_ref, wq_ref, wkv_ref, q_ref, kv_ref, vec_ref, b_ref, m_ref, l_ref, acc_ref):
        @pl.when(pl.program_id(0) == 0)
        def _():
            core = place()[3]
            vecs = jnp.transpose(wq_ref[:, HALF:].astype(F32))
            vec_ref[...] = vecs[:16]
            b_ref[...] = jnp.where(core == 0, vecs[:8, :HALF], vecs[:8, HALF:])
            for i, ref in enumerate((o_ref, g_ref)):
                part = mm(ref[...], wq_ref[:, :HALF]) + b_ref[0:1, :]
                q_ref[i * tokens : (i + 1) * tokens, :] = part.astype(BF16) * BF16(0.125)
            m_ref[...] = jnp.full(m_ref.shape, -1e30, F32)
            l_ref[...] = jnp.zeros(l_ref.shape, F32)
            acc_ref[...] = jnp.zeros(acc_ref.shape, F32)

        keys_values(x_ref, wkv_ref, b_ref[1:2, :], kv_ref)
        attend_step(q_ref, kv_ref, m_ref, l_ref, acc_ref)

    return pl.pallas_call(
        body,
        grid=(keys // block,),
        in_specs=[
            whole_spec(tokens, WIDTH),
            whole_spec(tokens, WIDTH),
            rows,
            whole_spec(*wq.shape),
            whole_spec(*wkv.shape),
        ],
        out_specs=[
            whole_spec(2 * tokens, HALF),
            rows,
            whole_spec(16, WIDTH),
            whole_spec(8, HALF),
            whole_spec(8, 2 * tokens),
            whole_spec(8, 2 * tokens),
            whole_spec(HALF, 2 * tokens),
        ],
        out_shape=[
            shape((2 * tokens, HALF), BF16),
            shape((keys, WIDTH), BF16),
            shape((16, WIDTH), F32),
            shape((8, HALF), F32),
            shape((8, 2 * tokens), F32),
            shape((8, 2 * tokens), F32),
            shape((HALF, 2 * tokens), F32),
        ],
        compiler_params=pltpu.CompilerParams(vmem_limit_bytes=20 * MIB),
        cost_estimate=attend_cost(tokens, keys),
        name="attend_first",
    )(own, got, xo, wq, wkv)


def attend_last(q, xc, wkv, bias, top, total, weighted):
    tokens, keys = q.shape[0], xc.shape[0]
    block = math.gcd(keys, 1024)
    rows = pl.BlockSpec((block, WIDTH), lambda i: (i, 0))

    def body(q_ref, x_ref, w_ref, b_ref, mi_ref, li_ref, ai_ref, kv_ref, o_ref, ctx_ref, lse_ref, m_s, l_s, acc_s):
        @pl.when(pl.program_id(0) == 0)
        def _():
            m_s[...] = mi_ref[...]
            l_s[...] = li_ref[...]
            acc_s[...] = ai_ref[...]

        keys_values(x_ref, w_ref, b_ref[1:2, :], kv_ref)
        attend_step(q_ref, kv_ref, m_s, l_s, acc_s)

        @pl.when(pl.program_id(0) == pl.num_programs(0) - 1)
        def _():
            lse_ref[...] = m_s[...] + jnp.log(l_s[...])
            for h in range(NH):
                lo = h * HD
                o_ref[lo : lo + HD, :] = acc_s[lo : lo + HD, :] / l_s[h : h + 1, :]
            ctx_ref[...] = jnp.transpose(o_ref[...]).astype(BF16)

    return pl.pallas_call(
        body,
        grid=(keys // block,),
        in_specs=[
            whole_spec(tokens, HALF),
            rows,
            whole_spec(*wkv.shape),
            whole_spec(8, HALF),
            whole_spec(8, tokens),
            whole_spec(8, tokens),
            whole_spec(HALF, tokens),
        ],
        out_specs=[
            rows,
            whole_spec(HALF, tokens),
            whole_spec(tokens, HALF),
            whole_spec(8, tokens),
        ],
        out_shape=[
            shape((keys, WIDTH), BF16),
            shape((HALF, tokens), F32),
            shape((tokens, HALF), BF16),
            shape((8, tokens), F32),
        ],
        scratch_shapes=[
            pltpu.VMEM((8, tokens), F32),
            pltpu.VMEM((8, tokens), F32),
            pltpu.VMEM((HALF, tokens), F32),
        ],
        compiler_params=pltpu.CompilerParams(vmem_limit_bytes=20 * MIB),
        cost_estimate=attend_cost(tokens // 2, keys),
        name="attend_last",
    )(q, xc, wkv, bias, top, total, weighted)


def unit_places(chips, per, rows, core):
    units = chips * per * rows
    unit = lax.broadcasted_iota(jnp.int32, (WIDTH, units), 1)
    at = lax.broadcasted_iota(jnp.int32, (WIDTH, units), 0)
    chip, inside = unit // (per * rows), lax.rem(unit, rows)
    return (at == chip * (2 * rows) + core * rows + inside).astype(BF16)


def unit_bias(vecs, chips, per, rows):
    units = chips * per * rows

    def body(v_ref, out_ref):
        every = mm(v_ref[...].astype(BF16), unit_places(chips, per, rows, place()[3]))
        turn = lax.rem(lax.broadcasted_iota(jnp.int32, (16, units), 1) // rows, per)
        row = lax.broadcasted_iota(jnp.int32, (16, units), 0)
        out_ref[...] = column_sum(jnp.where(row == 9 + turn, every, 0.0))

    return kernel(body, (vecs,), (shape((1, units), F32),), "unit_bias", flops=10**8)[0]


def unit_rows(sums, chips, per, rows):
    units = chips * per * rows

    def body(s_ref, out_ref):
        turn = lax.rem(lax.broadcasted_iota(jnp.int32, (8, units), 1) // rows, per)
        row = lax.broadcasted_iota(jnp.int32, (8, units), 0)
        spread_out = jnp.where(row == turn, s_ref[...], 0.0).astype(BF16)
        out_ref[...] = mm_t(spread_out, unit_places(chips, per, rows, place()[3]))

    return kernel(body, (sums,), (shape((8, WIDTH), F32),), "unit_rows", flops=10**8)[0]


def norm_forward(residual, gain, shift):
    center = residual - jnp.mean(residual, axis=-1, keepdims=True)
    scale = lax.rsqrt(jnp.mean(center * center, axis=-1, keepdims=True) + EPSILON)
    normed = center * scale
    return normed * gain + shift, normed, scale


def norm_backward(grad_out, normed, scale, gain):
    grad_normed = grad_out * gain
    return scale * (
        grad_normed
        - jnp.mean(grad_normed, axis=-1, keepdims=True)
        - normed * jnp.mean(grad_normed * normed, axis=-1, keepdims=True)
    )


def column_sum(value):
    return jnp.sum(value, axis=0, keepdims=True)


def halves(core, own, other):
    left = jnp.where(core == 0, own, other)
    right = jnp.where(core == 0, other, own)
    return left, right


def mix(ctx, ctx_got, mixer_own, mixer_got, vecs, inputs):
    tokens = inputs.shape[0]

    def body(o_ref, g_ref, mo_ref, mg_ref, v_ref, x_ref, low_ref, row_ref, n_ref, s_ref):
        core = place()[3]
        mine = pl.ds(pl.multiple_of(core * HALF, HALF), HALF)
        others = pl.ds(pl.multiple_of((1 - core) * HALF, HALF), HALF)
        parts = [
            mm(o_ref[:tokens, :], ref[mine, :]) + mm(g_ref[tokens:, :], ref[others, :])
            for ref in (mo_ref, mg_ref)
        ]
        attended = jnp.concatenate(halves(core, *parts), axis=1) + v_ref[2:3, :]
        rows, normed, scale = norm_forward(
            x_ref[...].astype(F32) + attended, v_ref[3:4, :], v_ref[4:5, :]
        )
        low_ref[...] = rows.astype(BF16)
        row_ref[...] = rows
        n_ref[...] = normed
        s_ref[...] = scale

    return kernel(
        body,
        (ctx, ctx_got, mixer_own, mixer_got, vecs, inputs),
        (
            shape((tokens, WIDTH), BF16),
            shape((tokens, WIDTH), F32),
            shape((tokens, WIDTH), F32),
            shape((tokens, 1), F32),
        ),
        "mix",
        flops=10**9,
        bytes_accessed=3 * 10**6,
    )


def feed(own, got, w_inner, i_bias, w_outer):
    tokens = own.shape[0]
    units = w_inner.shape[1]

    def body(o_ref, g_ref, w1_ref, b_ref, w2_ref, two_ref, act_ref, slope_ref, mine_ref, send_ref):
        two_ref[:tokens, :] = o_ref[...]
        two_ref[tokens:, :] = g_ref[...]
        u = mm(two_ref[...], w1_ref[...]) + b_ref[...]
        cdf = 0.5 * (1.0 + lax.erf(u * ROOT_HALF))
        slope_ref[...] = cdf + u * jnp.exp(-0.5 * u * u) * GAUSS_FACTOR
        act_ref[...] = (u * cdf).astype(BF16)
        part = mm(act_ref[...], w2_ref[...])
        mine_ref[...] = part[:tokens]
        send_ref[...] = part[tokens:]

    return kernel(
        body,
        (own, got, w_inner, i_bias, w_outer),
        (
            shape((2 * tokens, WIDTH), BF16),
            shape((2 * tokens, units), BF16),
            shape((2 * tokens, units), F32),
            shape((tokens, WIDTH), F32),
            shape((tokens, WIDTH), F32),
        ),
        "feed",
        flops=3 * 10**9,
        bytes_accessed=8 * 10**6,
    )


def crown(mine, got, first_rows, vecs, out_cot, term_cot):
    tokens = mine.shape[0]

    def body(
        m_ref, g_ref, f_ref, v_ref, oc_ref, tc_ref, out_ref, term_ref, gs_ref, go_ref, sum_ref
    ):
        gain = v_ref[6:7, :]
        head = v_ref[8:9, :]
        outer = m_ref[...] + g_ref[...] + v_ref[5:6, :]
        rows, normed, scale = norm_forward(f_ref[...] + outer, gain, v_ref[7:8, :])
        out_ref[...] = rows.astype(BF16)
        logits = jnp.sum(rows * head, axis=-1, keepdims=True)
        small = jnp.exp(-jnp.abs(logits))
        term = jnp.maximum(logits, 0.0) + jnp.log1p(small)
        term_ref[...] = jnp.transpose(jnp.broadcast_to(term, (tokens, 128)))[0:1, :]
        sig = jnp.where(logits >= 0.0, 1.0, small) / (1.0 + small)
        cot = jnp.transpose(jnp.broadcast_to(tc_ref[...], (128, tokens)))[:, 0:1]
        slope = cot * sig
        grad_final = oc_ref[...].astype(F32) + slope * head
        grad = norm_backward(grad_final, normed, scale, gain)
        low = grad.astype(BF16)
        gs_ref[...] = grad
        go_ref[...] = low
        sum_ref[...] = jnp.concatenate(
            [
                column_sum(low.astype(F32)),
                column_sum(grad_final * normed),
                column_sum(grad_final),
                column_sum(slope * rows),
                jnp.zeros((4, WIDTH), F32),
            ],
            axis=0,
        )

    return kernel(
        body,
        (mine, got, first_rows, vecs, out_cot, term_cot),
        (
            shape((tokens, WIDTH), BF16),
            shape((1, tokens), F32),
            shape((tokens, WIDTH), F32),
            shape((tokens, WIDTH), BF16),
            shape((8, WIDTH), F32),
        ),
        "crown",
        flops=10**8,
        bytes_accessed=3 * 10**6,
    )


def feed_back(own, got, slope, w_inner, w_outer):
    tokens = own.shape[0]
    units = w_inner.shape[1]

    def body(o_ref, g_ref, s_ref, w1_ref, w2_ref, two_ref, gi_ref, mine_ref, send_ref, sum_ref):
        two_ref[:tokens, :] = o_ref[...]
        two_ref[tokens:, :] = g_ref[...]
        low = (mm_t(two_ref[...], w2_ref[...]) * s_ref[...]).astype(BF16)
        gi_ref[...] = low
        sum_ref[...] = column_sum(low.astype(F32))
        part = mm_t(gi_ref[...], w1_ref[...])
        mine_ref[...] = part[:tokens]
        send_ref[...] = part[tokens:]

    return kernel(
        body,
        (own, got, slope, w_inner, w_outer),
        (
            shape((2 * tokens, WIDTH), BF16),
            shape((2 * tokens, units), BF16),
            shape((tokens, WIDTH), F32),
            shape((tokens, WIDTH), F32),
            shape((1, units), F32),
        ),
        "feed_back",
        flops=3 * 10**9,
        bytes_accessed=8 * 10**6,
    )


def mix_back(mine, got, grad_second, normed, scale, vecs, mixer_own, mixer_got):
    tokens = mine.shape[0]

    def body(
        m_ref, g_ref, gs_ref, n_ref, s_ref, v_ref, mo_ref, mg_ref, res_ref, keep_ref, send_ref, sum_ref
    ):
        core = place()[3]
        first = gs_ref[...] + m_ref[...] + g_ref[...]
        normal = n_ref[...]
        grad = norm_backward(first, normal, s_ref[...], v_ref[3:4, :])
        res_ref[...] = grad
        low = grad.astype(BF16)
        sum_ref[...] = jnp.concatenate(
            [
                column_sum(low.astype(F32)),
                column_sum(first * normal),
                column_sum(first),
                jnp.zeros((5, WIDTH), F32),
            ],
            axis=0,
        )
        mine_low, other_low = halves(core, low[:, :HALF], low[:, HALF:])
        ctx = (mm_t(mine_low, mo_ref[...]) + mm_t(other_low, mg_ref[...])).astype(BF16)
        mine_ctx, other_ctx = halves(core, ctx[:, :HALF], ctx[:, HALF:])
        keep_ref[:, :HALF] = mine_ctx
        keep_ref[:, HALF:] = mine_low
        send_ref[:, :HALF] = other_ctx
        send_ref[:, HALF:] = other_low

    return kernel(
        body,
        (mine, got, grad_second, normed, scale, vecs, mixer_own, mixer_got),
        (
            shape((tokens, WIDTH), F32),
            shape((tokens, WIDTH), BF16),
            shape((tokens, WIDTH), BF16),
            shape((8, WIDTH), F32),
        ),
        "mix_back",
        flops=10**9,
        bytes_accessed=4 * 10**6,
    )


def attend_back_step(q_ref, g_ref, lse_ref, delta_ref, kv_ref, out_ref, acc_ref, sum_ref):
    held = []
    for h in range(NH):
        lo = h * HD
        qh = q_ref[:, lo : lo + HD]
        gh = g_ref[:, lo : lo + HD]
        kh = kv_ref[:, lo : lo + HD]
        vh = kv_ref[:, HALF + lo : HALF + lo + HD]
        p = jnp.exp(mm_t(kh, qh) - lse_ref[h : h + 1, :])
        dp = mm_t(vh, gh)
        ds = (p * (dp - delta_ref[h : h + 1, :])).astype(BF16)
        acc_ref[lo : lo + HD, :] += t_mm(kh, ds)
        held.append((mm(ds, qh).astype(BF16), mm(p.astype(BF16), gh).astype(BF16)))
        if h % 2 == 1:
            (dk0, dv0), (dk1, dv1) = held
            held = []
            at = lo - HD
            dv = jnp.concatenate([dv0, dv1], axis=1)
            out_ref[:, at : at + 2 * HD] = jnp.concatenate([dk0, dk1], axis=1)
            out_ref[:, HALF + at : HALF + at + 2 * HD] = dv
            sum_ref[1:2, at : at + 2 * HD] += column_sum(dv.astype(F32))


def attend_back_cost(tokens, keys):
    return pl.CostEstimate(flops=1, bytes_accessed=1, transcendentals=0)


def attend_back_first(q, low, low_got, o, lse, kv):
    tokens, keys = q.shape[0], kv.shape[0]
    block = math.gcd(keys, 1024)
    rows = pl.BlockSpec((block, WIDTH), lambda i: (i, 0))

    def body(q_ref, go_ref, gc_ref, o_ref, lse_ref, kv_ref, d_ref, g_ref, delta_ref, acc_ref, sum_ref):
        @pl.when(pl.program_id(0) == 0)
        def _():
            acc_ref[...] = jnp.zeros(acc_ref.shape, F32)
            sum_ref[...] = jnp.zeros(sum_ref.shape, F32)
            g_ref[: tokens // 2, :] = go_ref[:, :HALF]
            g_ref[tokens // 2 :, :] = gc_ref[:, :HALF]
            prod = jnp.transpose(g_ref[...].astype(F32)) * o_ref[...]
            for h in range(NH):
                delta_ref[h : h + 1, :] = column_sum(prod[h * HD : (h + 1) * HD, :])

        attend_back_step(q_ref, g_ref, lse_ref, delta_ref, kv_ref, d_ref, acc_ref, sum_ref)

    return pl.pallas_call(
        body,
        grid=(keys // block,),
        in_specs=[
            whole_spec(tokens, HALF),
            whole_spec(tokens // 2, WIDTH),
            whole_spec(tokens // 2, WIDTH),
            whole_spec(HALF, tokens),
            whole_spec(8, tokens),
            rows,
        ],
        out_specs=[
            rows,
            whole_spec(tokens, HALF),
            whole_spec(8, tokens),
            whole_spec(HALF, tokens),
            whole_spec(8, HALF),
        ],
        out_shape=[
            shape((keys, WIDTH), BF16),
            shape((tokens, HALF), BF16),
            shape((8, tokens), F32),
            shape((HALF, tokens), F32),
            shape((8, HALF), F32),
        ],
        compiler_params=pltpu.CompilerParams(vmem_limit_bytes=20 * MIB),
        cost_estimate=attend_back_cost(tokens, keys),
        name="attend_back_first",
    )(q, low, low_got, o, lse, kv)


def attend_back_last(q, g, lse, delta, acc, sums, kv, wq):
    tokens, keys = q.shape[0], kv.shape[0]
    block = math.gcd(keys, 1024)
    rows = pl.BlockSpec((block, WIDTH), lambda i: (i, 0))

    def body(q_ref, g_ref, lse_ref, delta_ref, ai_ref, si_ref, kv_ref, w_ref, d_ref, dq_ref, sum_ref, send_ref, acc_s):
        @pl.when(pl.program_id(0) == 0)
        def _():
            acc_s[...] = ai_ref[...]
            sum_ref[...] = si_ref[...]

        attend_back_step(q_ref, g_ref, lse_ref, delta_ref, kv_ref, d_ref, acc_s, sum_ref)

        @pl.when(pl.program_id(0) == pl.num_programs(0) - 1)
        def _():
            dq = jnp.transpose(acc_s[...] * 0.125).astype(BF16)
            dq_ref[...] = dq
            sum_ref[0:1, :] = column_sum(dq.astype(F32))
            send_ref[...] = mm_t(dq[tokens // 2 :], w_ref[:, :HALF]).astype(BF16)

    return pl.pallas_call(
        body,
        grid=(keys // block,),
        in_specs=[
            whole_spec(tokens, HALF),
            whole_spec(tokens, HALF),
            whole_spec(8, tokens),
            whole_spec(8, tokens),
            whole_spec(HALF, tokens),
            whole_spec(8, HALF),
            rows,
            whole_spec(*wq.shape),
        ],
        out_specs=[
            rows,
            whole_spec(tokens, HALF),
            whole_spec(8, HALF),
            whole_spec(tokens // 2, WIDTH),
        ],
        out_shape=[
            shape((keys, WIDTH), BF16),
            shape((tokens, HALF), BF16),
            shape((8, HALF), F32),
            shape((tokens // 2, WIDTH), BF16),
        ],
        scratch_shapes=[pltpu.VMEM((HALF, tokens), F32)],
        compiler_params=pltpu.CompilerParams(vmem_limit_bytes=20 * MIB),
        cost_estimate=attend_back_cost(tokens, keys),
        name="attend_back_last",
    )(q, g, lse, delta, acc, sums, kv, wq)


def input_part_other(dkv, wkv):
    keys = dkv.shape[0]
    block = math.gcd(keys, 1024)
    rows = pl.BlockSpec((block, WIDTH), lambda i: (i, 0))

    def body(d_ref, w_ref, out_ref):
        out_ref[...] = mm_t(d_ref[...], w_ref[...]).astype(BF16)

    return pl.pallas_call(
        body,
        grid=(keys // block,),
        in_specs=[rows, whole_spec(*wkv.shape)],
        out_specs=rows,
        out_shape=shape((keys, WIDTH), BF16),
        compiler_params=pltpu.CompilerParams(vmem_limit_bytes=12 * MIB),
        cost_estimate=pl.CostEstimate(flops=1, bytes_accessed=1, transcendentals=0),
        name="input_part_other",
    )(dkv, wkv)


def input_part_own(dkv, wkv, got, dq, wq, q_got):
    keys = dkv.shape[0]
    tokens = q_got.shape[0]
    block = math.gcd(keys // 2, 512)
    half = keys // 2 // block
    rows = pl.BlockSpec((block, WIDTH), lambda i: (i, 0))

    def body(d_ref, w_ref, g_ref, dq_ref, wq_ref, qg_ref, keep_ref, send_ref, part_s):
        step = pl.program_id(0)
        part_s[...] = mm_t(d_ref[...], w_ref[...]) + g_ref[...].astype(F32)

        @pl.when(step == 0)
        def _():
            part_s[:tokens, :] += mm_t(dq_ref[:tokens, :], wq_ref[:, :HALF]) + qg_ref[...].astype(
                F32
            )

        @pl.when(step < half)
        def _():
            keep_ref[...] = part_s[...].astype(BF16)

        @pl.when(step >= half)
        def _():
            send_ref[...] = part_s[...].astype(BF16)

    return pl.pallas_call(
        body,
        grid=(2 * half,),
        in_specs=[
            rows,
            whole_spec(*wkv.shape),
            rows,
            whole_spec(*dq.shape),
            whole_spec(*wq.shape),
            whole_spec(*q_got.shape),
        ],
        out_specs=[
            pl.BlockSpec((block, WIDTH), lambda i: (jnp.minimum(i, half - 1), 0)),
            pl.BlockSpec((block, WIDTH), lambda i: (jnp.maximum(i - half, 0), 0)),
        ],
        out_shape=[shape((keys // 2, WIDTH), BF16)] * 2,
        scratch_shapes=[pltpu.VMEM((block, WIDTH), F32)],
        compiler_params=pltpu.CompilerParams(vmem_limit_bytes=12 * MIB),
        cost_estimate=pl.CostEstimate(flops=1, bytes_accessed=1, transcendentals=0),
        name="input_part_own",
    )(dkv, wkv, got, dq, wq, q_got)


def spread(zs, rows, cols, args, fill, name, scratch, limit=14):
    count = len(args)

    def body(*refs):
        ins, outs, held = refs[:count], refs[count : count + 4], refs[count + 4 :]
        write = fill(ins, held)
        here = place()
        for k in range(zs):
            for side in range(4):
                write(outs[side], k, chip_of(here, side // 2, side % 2, k, zs))

    return kernel(
        body,
        args,
        [shape((zs, rows, cols), BF16)] * 4,
        name,
        limit=limit,
        scratch=[pltpu.VMEM(dims, BF16) for dims in scratch],
        flops=2 * 10**9,
        bytes_accessed=6 * 10**6,
    )


def spread_slow(full, zs):
    full = to_distance(full.reshape(2, zs, 2, *full.shape[1:]))
    full = full.reshape(4, zs, *full.shape[3:])
    return full[0], full[1], full[2], full[3]


def spread_rest(first2, grad_inner, active, grad_outer2, zs):
    units = active.shape[1]
    rows, hidden = WIDTH // (4 * zs), units // (4 * zs)
    if rows % 16:
        w1 = t_mm(first2, grad_inner).astype(BF16).reshape(4 * zs, rows, units)
        w2 = t_mm(active, grad_outer2).astype(BF16).reshape(4 * zs, hidden, WIDTH)
        return spread_slow(jnp.concatenate([w1[:, :, :WIDTH], w1[:, :, WIDTH:], w2], axis=1), zs)

    late = hidden // 2
    most = 2 * rows + hidden - late

    def body(f_ref, gi_ref, a_ref, go_ref, *outs):
        outs, late_ref, (w1_s, w2_s) = outs[:4], outs[4], outs[5:]
        w1_s[...] = t_mm(f_ref[...], gi_ref[...]).astype(BF16)
        w2_s[...] = t_mm(a_ref[...], go_ref[...]).astype(BF16)
        here = place()
        for k in range(zs):
            for side in range(4):
                chip = chip_of(here, side // 2, side % 2, k, zs)
                at, down = rows_at(chip, rows), chip * hidden
                outs[side][k, :rows, :] = w1_s[at, :WIDTH]
                outs[side][k, rows : 2 * rows, :] = w1_s[at, WIDTH:]
                outs[side][k, 2 * rows :, :] = w2_s[pl.ds(pl.multiple_of(down, 16), hidden - late), :]
                late_ref[k, side] = w2_s[pl.ds(pl.multiple_of(down + hidden - late, 16), late), :]

    return kernel(
        body,
        (first2, grad_inner, active, grad_outer2),
        [shape((zs, most, WIDTH), BF16)] * 4 + [shape((zs, 4, late, WIDTH), BF16)],
        "spread_rest",
        scratch=[pltpu.VMEM((WIDTH, units), BF16), pltpu.VMEM((units, WIDTH), BF16)],
    )


def spread_qkv(zs, x_own, x_got, dq, qv, mid, top, unit, g_kv, ctx, ctx_got, low, low_got):
    tokens = x_own.shape[0]
    rows = WIDTH // (4 * zs)
    cols = WIDE + WIDTH + HALF

    def fill(ins, held):
        part_s = held[0]
        xo, xg, dq_r, qv_r, mid_r, top_r, unit_r, c_r, cg_r, l_r, lg_r, *kv_rs = ins
        core = place()[3]
        part_s[:, :HALF] = (
            t_mm(xo[...], dq_r[:tokens, :]) + t_mm(xg[...], dq_r[tokens:, :])
        ).astype(BF16)
        zero = jnp.zeros((2, HALF), F32)
        sums = jnp.concatenate(
            [
                jnp.concatenate(halves(core, qv_r[0:2, :], zero), axis=1),
                mid_r[0:3, :],
                top_r[0:4, :],
                unit_r[...],
                jnp.zeros((AUX - 17, WIDTH), F32),
            ],
            axis=0,
        )
        part_s[:, HALF:WIDE] = jnp.transpose(sums).astype(BF16)
        if len(kv_rs) == 1:
            part_s[:, WIDE : WIDE + WIDTH] = kv_rs[0][...]
        else:
            xk, dk, xl, dl = kv_rs
            part_s[:, WIDE : WIDE + WIDTH] = (t_mm(xk[...], dk[...]) + t_mm(xl[...], dl[...])).astype(
                BF16
            )
        lows = (l_r[:, HALF:], lg_r[:, HALF:])
        part_s[pl.ds(pl.multiple_of(core * HALF, HALF), HALF), WIDE + WIDTH :] = (
            t_mm(c_r[:tokens, :], lows[0]) + t_mm(c_r[tokens:, :], lows[1])
        ).astype(BF16)
        part_s[pl.ds(pl.multiple_of((1 - core) * HALF, HALF), HALF), WIDE + WIDTH :] = (
            t_mm(cg_r[tokens:, :], lows[0]) + t_mm(cg_r[:tokens, :], lows[1])
        ).astype(BF16)

        def write(out, n, chip):
            out[n] = part_s[rows_at(chip, rows), :]

        return write

    args = (x_own, x_got, dq, qv, mid, top, unit, ctx, ctx_got, low, low_got, *g_kv)
    if rows % 16 == 0:
        return spread(zs, rows, cols, args, fill, "spread_qkv", ((WIDTH, cols),), 24)

    def body(*refs):
        fill(refs[:12], refs[12:])

    full = kernel(body, args, [shape((WIDTH, cols), BF16)], "fill_qkv")[0]
    return spread_slow(full.reshape(4 * zs, rows, cols), zs)


def finish_sums(qkv, rest, more, rows):
    count, cols = len(qkv), qkv[0].shape[1]
    hidden = rest[0].shape[0] - 4 * rows
    wide = cols + 2 * WIDTH

    def body(*refs):
        ins, (own_ref, send_ref, outer_ref, both_s) = refs[:-4], refs[-4:]
        core = place()[3]
        both_s[:, :cols] = sum(ref[...].astype(F32) for ref in ins[:count])
        low = sum(ref[...].astype(F32) for ref in ins[count : count + len(rest)])
        if more:
            top = sum(ref[...].astype(F32) for ref in ins[count + len(rest) :])
            most = top.shape[0]
            low = jnp.concatenate([low[:most] + top, low[most:]], axis=0)
        both_s[:, cols : cols + WIDTH] = low[: 2 * rows]
        both_s[:, cols + WIDTH :] = low[2 * rows : 4 * rows]
        outer_ref[...] = low[4 * rows :]
        halves_of = (both_s[:rows, :], both_s[rows:, :])
        own_ref[...] = jnp.where(core == 0, *halves_of)
        send_ref[...] = jnp.where(core == 1, *halves_of)

    return kernel(
        body,
        (*qkv, *rest, *more),
        [shape((rows, wide), F32)] * 2 + [shape((hidden, WIDTH), F32)],
        "finish_sums",
        limit=8,
        scratch=[pltpu.VMEM((2 * rows, wide), F32)],
    )


def finish_rows(own, got, hidden, per):
    rows = own.shape[0]
    base = WIDE + WIDTH + HALF
    chips = (own.shape[1] - base) // hidden

    def body(own_ref, got_ref, *outs):
        core = place()[3]
        left = jnp.where(core == 0, own_ref[...], got_ref[...])
        right = jnp.where(core == 0, got_ref[...], own_ref[...])
        for out, lo in zip(outs, (0, WIDE, WIDE + HALF, WIDE + WIDTH)):
            out[:, :HALF] = left[:, lo : lo + HALF]
            out[:, HALF:] = right[:, lo : lo + HALF]
        outs[4][...] = jnp.concatenate(
            [
                side[:, base + i * hidden : base + (i + 1) * hidden]
                for i in range(chips)
                for side in (left, right)
            ],
            axis=1,
        )
        small = left[:, HALF:WIDE] + right[:, HALF:WIDE]
        if rows < AUX:
            small = jnp.concatenate([small, jnp.zeros((AUX - rows, AUX), F32)], axis=0)
        small = jnp.transpose(small)
        for j in range(9):
            outs[5 + j][...] = small[j, :rows]
        for j in range(per):
            outs[14][pl.ds(j * rows, rows)] = small[9 + j, :rows]

    outs = kernel(
        body,
        (own, got),
        [shape((rows, WIDTH), F32)] * 4
        + [shape((rows, 2 * chips * hidden), F32)]
        + [shape((rows,), F32)] * 9
        + [shape((hidden,), F32)],
        "finish_rows",
        limit=8,
    )
    return (*outs[:5], outs[5:])


def shards(
    layer_input,
    query_weight,
    query_bias,
    key_weight,
    value_weight,
    value_bias,
    mixer_weight,
    mixer_bias,
    first_gain,
    first_shift,
    inner_weight,
    inner_bias,
    outer_weight,
    outer_bias,
    second_gain,
    second_shift,
    head_weight,
    out_cotangent,
    term_cotangent,
):
    core = place()[3]
    chips = lax.axis_size("ctx")
    zs = chips // 4
    inputs = layer_input[0]
    tokens = inputs.shape[0]
    rows = query_weight.shape[0]
    hidden = outer_weight.shape[0]
    ff = inner_weight.shape[1]
    units = ff // 2
    per = hidden // rows

    def in_order(own, other, axis):
        return jnp.stack(halves(core, own, other), axis=axis)

    own, send = pack(
        (query_weight, key_weight, value_weight, mixer_weight),
        inner_weight,
        (
            query_bias,
            value_bias,
            mixer_bias,
            first_gain,
            first_shift,
            outer_bias,
            second_gain,
            second_shift,
            head_weight,
            inner_bias,
        ),
    )
    block, rest = join(own, swap_core(send), outer_weight)
    x_got = swap_core(inputs)
    first = 2 * rows * (units // HALF)
    most, part_far = first + hidden + hidden // 3, 3 * first // 4
    every = tuple(range(zs))
    barrier = lax.optimization_barrier
    part_row = 2 * rows
    if zs == 4:
        near_y, near_x = swap_y(rest[None]), swap_x(rest[None])
        near_y, near_x, qkv = barrier((near_y, near_x, along_z_pieces(block)))
        x_own, first_piece = barrier((inputs, qkv[1]))
        qkv = jnp.stack([qkv[0], first_piece, *qkv[2:]])
        flat = qkv.reshape(first, -1)
        sent_y = swap_y(jnp.concatenate([flat, near_x[0, first:]], axis=1))
        sent_x = swap_x(jnp.concatenate([flat, near_y[0, :first]], axis=1))
        sent_y, sent_x, x_along = barrier((sent_y, sent_x, along_z_pieces(x_own)))
        x_along = jnp.stack(x_along)
        cols = flat.shape[1]
        qkv_y, qkv_x = (sent[:, :cols].reshape(qkv.shape) for sent in (sent_y, sent_x))
        near_far = [sent[None, :, cols:] for sent in (sent_x, sent_y)]
        rest_sent, x_along = barrier((rest[:most], x_along))
        x_y, qkv_far, pieces = barrier(
            (swap_y(x_along), far_out(qkv_y, qkv_x, part_row), along_z_pieces(rest_sent))
        )
        square = jnp.stack(
            [rest[most:], near_y[0, most:], near_x[0, most:], near_far[1][0, most - first :]]
        )
        pieces, square = barrier((jnp.stack(pieces[1:]), square))
        rest_y, rest_x = swap_y(pieces), swap_x(pieces)
    else:
        qkv, x_along, pieces = (along_z_pieces(v) for v in (block, inputs, rest))
        x_y, rest_y, rest_x = swap_y(x_along), swap_y(pieces), swap_x(pieces)
        qkv_y, qkv_x = swap_y(qkv), swap_x(qkv)
        qkv_far = far_out(qkv_y, qkv_x, part_row)
    wq, wkv, mixer_own = build_qkv(
        *sources([(every, qkv, qkv_y, qkv_x, *qkv_far)], part_row), part_row
    )
    mixer_got = swap_core(mixer_own)
    xo = jnp.concatenate([x_along, x_y]).reshape(2 * zs * tokens, WIDTH)
    xc = swap_core(xo)

    q_scaled, kvo, vecs, bias, top, total, weighted = attend_first(inputs, x_got, xo, wq, wkv)
    kvc, o_exact, ctx, lse = attend_last(q_scaled, xc, wkv, bias, top, total, weighted)
    if zs == 4:
        rest_y, rest_x, ctx, *late = barrier(
            (rest_y, rest_x, ctx, swap_z(square, 1), swap_z(square, 2))
        )
        w_inner, w_outer = build_split(
            (rest[None], near_y, near_x, *near_far),
            (pieces, rest_y, rest_x, *far_out(rest_y, rest_x, part_far)),
            (*late, swap_z(square, 3)),
            2 * rows,
            hidden,
            (part_far, first, most),
        )
    else:
        away = [(every, pieces, rest_y, rest_x, *far_out(rest_y, rest_x, first))]
        w_inner, w_outer = build_rest(*sources(away, first), 2 * rows, hidden)
    ctx_got = swap_core(ctx)
    i_bias = unit_bias(vecs, chips, per, rows)
    first_low, first_rows, first_normed, first_scale = mix(
        ctx, ctx_got, mixer_own, mixer_got, vecs, inputs
    )

    first2, active, slope, mine, away = feed(
        first_low, swap_core(first_low), w_inner, i_bias, w_outer
    )
    final_low, term, grad_second, grad_outer, top_sums = crown(
        mine, swap_core(away), first_rows, vecs, out_cotangent[0], term_cotangent
    )
    grad_outer2, grad_inner, mine, away, inner_sums = feed_back(
        grad_outer, swap_core(grad_outer), slope, w_inner, w_outer
    )
    got = swap_core(away)
    keep, rest_y, rest_x, far, *late = spread_rest(first2, grad_inner, active, grad_outer2, zs)
    mine, keep, rest_y, rest_x, far, *late = barrier((mine, keep, rest_y, rest_x, far, *late))
    part_far = far.shape[1] // 2
    over_x, over_y = swap_x(far[:, :part_far]), swap_y(far[:, part_far:])

    grad_residual, low, low_send, mid_sums = mix_back(
        mine, got, grad_second, first_normed, first_scale, vecs, mixer_own, mixer_got
    )
    low_got = swap_core(low_send)
    dkvc, g_both, delta, acc, qv_sums = attend_back_first(
        q_scaled, low, low_got, o_exact, lse, kvc
    )
    if zs == 4:
        (late,) = late
        over_x, over_y, delta, kvo, late_1, late_2, late_3, square = barrier(
            (over_x, over_y, delta, kvo, swap_z(late[1], 1), swap_z(late[2], 2), late[3], late[0])
        )
        late_3 = swap_z(late_3, 3)
    else:
        over_x, over_y, dkvc, kvo = barrier((over_x, over_y, dkvc, kvo))
    away = swap_core(input_part_other(dkvc, wkv))
    rest_y = jnp.concatenate([rest_y[:, : part_far] + over_x, rest_y[:, part_far :]], axis=1)
    rest_x = jnp.concatenate([rest_x[:, : part_far], rest_x[:, part_far :] + over_y], axis=1)
    at = 1 if zs == 4 else 0
    got_y, got_x = swap_y(rest_y[at:]), swap_x(rest_x[at:])
    dkvo, dq, qv_sums, q_away = attend_back_last(
        q_scaled, g_both, lse, delta, acc, qv_sums, kvo, wq
    )

    part, part_y = input_part_own(dkvo, wkv, away, dq, wq, swap_core(q_away))
    dq, dkvo, part, part_y = barrier((dq, dkvo, part, part_y))
    if zs == 4:
        g_kv = (xo, dkvo, xc, dkvc)
    else:
        g_kv = ((t_mm(xo, dkvo) + t_mm(xc, dkvc)).astype(BF16),)
    g_qkv, qkv_y, qkv_x, qkv_far = spread_qkv(
        zs,
        inputs,
        x_got,
        dq,
        qv_sums,
        mid_sums,
        top_sums,
        unit_rows(inner_sums, chips, per, rows),
        g_kv,
        ctx,
        ctx_got,
        low,
        low_got,
    )
    part, part_y = part.reshape(zs, tokens, WIDTH), part_y.reshape(zs, tokens, WIDTH)
    if zs == 4:
        got_y, got_x, part_y, qkv_far, late_3 = barrier((got_y, got_x, part_y, qkv_far, late_3))
        square = square + late_1 + late_2 + late_3
        g_rest = keep[1:] + got_y + got_x
        qkv_far, got_part, far, g_rest = barrier(
            (
                swap_x(qkv_far),
                swap_y(part_y),
                swap_x(square[3]),
                [swap_z(g_rest[k - 1], k) for k in range(1, zs)],
            )
        )
        part = part + got_part
        qkv_x, qkv_far = barrier((qkv_x, qkv_far))
        got_y, got_x, parts = barrier(
            (
                swap_y(qkv_y + qkv_far),
                swap_x(qkv_x),
                [swap_z(part[k], k) for k in range(1, zs)],
            )
        )
        near_y = jnp.concatenate([rest_y[0], square[1] + far])
        near_x = jnp.concatenate([rest_x[0], square[2]])
        near_y, near_x, parts = barrier((near_y, near_x, parts))
        total = part[0].astype(F32)
        for value in parts:
            total = total + value.astype(F32)
        g_qkv = g_qkv + got_y + got_x
        near_y, near_x, pieces = barrier(
            (
                swap_y(near_y),
                swap_x(near_x),
                [swap_z(g_qkv[k], k) for k in range(1, zs)],
            )
        )
        g_qkv = [g_qkv[0], *pieces]
        g_whole = [jnp.concatenate([keep[0], square[0]]), near_y, near_x]
    else:
        g_whole, g_rest = [sum_z([(every, keep + got_y + got_x)])], []
        part = part + swap_y(part_y)
        total = sum_z([(every, part)])
        qkv_y, qkv_x = fan_far(qkv_y, qkv_x, qkv_far, 2 * rows)
        g_qkv = [sum_z([(every, g_qkv + swap_y(qkv_y) + swap_x(qkv_x))])]
    input_grad = (grad_residual + total).astype(BF16)

    own, send, g_outer = finish_sums(g_qkv, g_whole, g_rest, rows)
    g_query, g_key, g_value, g_mixer, g_inner, vectors = finish_rows(
        own, swap_core(send), hidden, per
    )
    return (
        final_low[None],
        term,
        input_grad[None],
        g_query,
        vectors[0],
        g_key,
        g_value,
        vectors[1],
        g_mixer,
        vectors[2],
        vectors[3],
        vectors[4],
        g_inner,
        vectors[9],
        g_outer,
        vectors[5],
        vectors[6],
        vectors[7],
        vectors[8],
    )


def pick(value, index, axis):
    return lax.dynamic_index_in_dim(value, index, axis, keepdims=False)


def solution(mesh):
    both = ("seq", "ctx")
    tok, mat, vec = P("seq", "ctx", None), P(both, None), P(both)
    term = P("seq", "ctx")
    in_specs = (
        tok, mat, vec, mat, mat, vec, mat, vec, vec, vec,
        mat, vec, mat, vec, vec, vec, vec, tok, term,
    )
    out_specs = (
        tok, term, tok, mat, vec, mat, mat, vec, mat, vec,
        vec, vec, mat, vec, mat, vec, vec, vec, vec,
    )
    return jax.shard_map(
        shards, mesh=mesh, in_specs=in_specs, out_specs=out_specs, check_vma=False
    )
```

```python
import math

import jax
import jax.numpy as jnp
from jax import lax
from jax.experimental import pallas as pl
from jax.experimental.pallas import tpu as pltpu
from jax.sharding import PartitionSpec as P

HEADS = 12
HD = 64
WIDTH = HEADS * HD
HALF = WIDTH // 2
NH = HEADS // 2
EPSILON = 1e-12
ROOT_HALF = 0.7071067811865476
GAUSS_FACTOR = 0.3989422804014327
F32 = jnp.float32
BF16 = jnp.bfloat16
AUX = 128
WIDE = HALF + AUX
MIB = 2**20


def mm(a, b):
    return lax.dot_general(a, b, (((1,), (0,)), ((), ())), preferred_element_type=F32)


def mm_t(a, b):
    return lax.dot_general(a, b, (((1,), (1,)), ((), ())), preferred_element_type=F32)


def t_mm(a, b):
    return lax.dot_general(a, b, (((0,), (0,)), ((), ())), preferred_element_type=F32)


def shape(dims, dtype):
    return jax.ShapeDtypeStruct(dims, dtype)


def swap_ctx(value, bit):
    n = lax.axis_size("ctx")
    return lax.ppermute(value, "ctx", [(i, i ^ bit) for i in range(n)])


def swap_core(value):
    return swap_ctx(value, 1)


def swap_y(value):
    return swap_ctx(value, 2)


def swap_x(value):
    return lax.ppermute(value, "seq", [(0, 1), (1, 0)])


def swap_z(value, k):
    return swap_ctx(value, 4 * k)


def place():
    at = lax.axis_index("ctx")
    return lax.axis_index("seq"), at // 4, (at // 2) % 2, at % 2


def z_groups():
    n = lax.axis_size("ctx")
    return [[i + 4 * j for j in range(n // 4)] for i in range(4)]


def turned(blocks, z, axis=0):
    zs = blocks.shape[axis]
    lead = blocks.shape[:axis]
    rest = blocks.shape[axis + 1 :]
    bit = 1
    while bit < zs:
        pairs = blocks.reshape(*lead, zs // (2 * bit), 2, bit, *rest)
        flipped = jnp.flip(pairs, len(lead) + 1)
        blocks = jnp.where((z & bit) == 0, pairs, flipped).reshape(*lead, zs, *rest)
        bit *= 2
    return blocks


def along_z_pieces(block):
    zs = lax.axis_size("ctx") // 4
    if zs > 4:
        every = lax.all_gather(block, "ctx", axis_index_groups=z_groups())
        return turned(every, lax.axis_index("ctx") // 4)
    return [block] + [swap_z(block, k) for k in range(1, zs)]


def far_out(by_y, by_x, row):
    if row == by_y.shape[1]:
        return (swap_x(by_y),)
    return swap_x(by_y[:, :row]), swap_y(by_x[:, row:])


def sources(groups, row):
    arrays, where = [], {}
    for ks, *blocks in groups:
        at = len(arrays)
        arrays += blocks
        for i, k in enumerate(ks):
            last = ((at + 3, i), (at + 4, i, row)) if len(blocks) > 4 else ((at + 3, i), (at + 3, i, 0))
            where[k] = (*(((at + j, i), (at + j, i, 0)) for j in range(3)), last)
    return arrays, where


def by_distance(arrays, where, row=0):
    def whole(first, rest):
        top = arrays[first[0]][first[1]][:row]
        return jnp.concatenate([top, arrays[rest[0]][rest[1]][row - rest[2] :]])

    blocks = [[whole(*side) for side in where[k]] for k in sorted(where)]
    full = jnp.stack([jnp.stack(four) for four in blocks], axis=1)
    return full.reshape(2, 2, *full.shape[1:])


def fan_far(by_y, by_x, far, row):
    if row == far.shape[1]:
        return by_y + swap_x(far), by_x
    over_x, over_y = swap_x(far[:, :row]), swap_y(far[:, row:])
    by_y = jnp.concatenate([by_y[:, :row] + over_x, by_y[:, row:]], axis=1)
    by_x = jnp.concatenate([by_x[:, :row], by_x[:, row:] + over_y], axis=1)
    return by_y, by_x


def sum_z(groups):
    zs = lax.axis_size("ctx") // 4
    if zs > 4:
        ((_, along),) = groups
        every = turned(along, lax.axis_index("ctx") // 4)
        every = lax.all_to_all(every, "ctx", 0, 0, axis_index_groups=z_groups())
        return jnp.sum(every.astype(F32), axis=0)
    total = None
    for ks, blocks in groups:
        for i, k in enumerate(ks):
            part = (blocks[i] if k == 0 else swap_z(blocks[i], k)).astype(F32)
            total = part if total is None else total + part
    return total


def to_mesh_order(blocks):
    x, z, y, _ = place()
    blocks = turned(blocks, z, 2)
    for axis, bit in enumerate((x, y)):
        blocks = jnp.where(bit == 0, blocks, jnp.flip(blocks, axis))
    return jnp.swapaxes(blocks, 1, 2)


def to_distance(blocks):
    x, z, y, _ = place()
    blocks = turned(jnp.swapaxes(blocks, 1, 2), z, 2)
    for axis, bit in enumerate((x, y)):
        blocks = jnp.where(bit == 0, blocks, jnp.flip(blocks, axis))
    return blocks


def chip_of(here, xr, yr, k, zs):
    x, z, y, _ = here
    return ((x ^ xr) * zs + (z ^ k)) * 2 + (y ^ yr)


def rows_at(chip, rows):
    return pl.ds(pl.multiple_of(chip * rows, 16), rows)


def kernel(body, args, outs, name, limit=14, scratch=(), flops=0, bytes_accessed=0):
    return pl.pallas_call(
        body,
        in_specs=[pl.BlockSpec(memory_space=pltpu.VMEM) for _ in args],
        out_specs=[pl.BlockSpec(memory_space=pltpu.VMEM) for _ in outs],
        out_shape=list(outs),
        scratch_shapes=list(scratch),
        compiler_params=pltpu.CompilerParams(vmem_limit_bytes=limit * MIB),
        cost_estimate=pl.CostEstimate(flops=1, bytes_accessed=1, transcendentals=0),
        name=name,
    )(*args)


def pack(weights, inner, vectors):
    rows, hidden = inner.shape[0], vectors[-1].shape[0]
    count = len(weights)
    every = (*weights, inner, *vectors)
    base = WIDE + WIDTH + HALF
    chips = inner.shape[1] // (2 * hidden)
    cols = base + chips * hidden

    def body(*refs):
        n = len(every)
        ins, (own_ref, send_ref), held = refs[:n], refs[n : n + 2], refs[n + 2 : 2 * n + 2]
        flat_s, sems = refs[-2:]
        copies = [pltpu.make_async_copy(i, h, sems.at[j]) for j, (i, h) in enumerate(zip(ins, held))]
        for copy in copies:
            copy.start()
        flat_s[...] = jnp.zeros(flat_s.shape, F32)
        for copy in copies:
            copy.wait()
        ws, inner_ref, vs = held[:count], held[count], held[count + 1 :]
        core = place()[3]
        at = 0
        for v in vs:
            for j in range(v.shape[0] // rows):
                flat_s[at : at + 1, :rows] = v[pl.ds(j * rows, rows)].astype(F32).reshape(1, rows)
                at += 1
        aux = jnp.transpose(flat_s[...])[:rows, :].astype(BF16)
        places = (0, WIDE, WIDE + HALF, WIDE + WIDTH)
        whole = inner_ref[...]
        units = [
            jnp.concatenate(
                [
                    whole[:, (2 * i + side) * hidden : (2 * i + side + 1) * hidden]
                    for i in range(chips)
                ],
                axis=1,
            )
            for side in range(2)
        ]
        for out, side in ((own_ref, core), (send_ref, 1 - core)):
            out[:, HALF:WIDE] = aux
            for w, lo in zip(ws, places):
                out[:, lo : lo + HALF] = jnp.where(side == 0, w[:, :HALF], w[:, HALF:])
            out[:, base:] = jnp.where(side == 0, units[0], units[1])

    return pl.pallas_call(
        body,
        in_specs=[pl.BlockSpec(memory_space=pl.ANY) for _ in every],
        out_specs=[pl.BlockSpec(memory_space=pltpu.VMEM)] * 2,
        out_shape=[shape((rows, cols), BF16)] * 2,
        scratch_shapes=[pltpu.VMEM(a.shape, BF16) for a in every]
        + [pltpu.VMEM((AUX, AUX), F32), pltpu.SemaphoreType.DMA((len(every),))],
        compiler_params=pltpu.CompilerParams(vmem_limit_bytes=56 * MIB),
        name="pack",
    )(*every)


def join(own, got, outer):
    rows, hidden = own.shape[0], outer.shape[0]
    base = WIDE + WIDTH + HALF
    quarters = (own.shape[1] - base) // HALF
    core = place()[3]
    both = jnp.concatenate(halves(core, own, got))
    return both[:, :base], jnp.concatenate(
        [both[:, base + j * HALF : base + (j + 1) * HALF] for j in range(quarters)]
        + [outer[:, :HALF], outer[:, HALF:]]
    )


def build_qkv(arrays, where, row):
    zs, rows = len(where), arrays[0].shape[1]
    ends = (0, WIDE, WIDE + WIDTH, WIDE + WIDTH + HALF)
    if rows % 16:
        full = to_mesh_order(by_distance(arrays, where, row)).reshape(WIDTH, -1)
        return [full[:, lo:hi] for lo, hi in zip(ends, ends[1:])]

    def body(*refs):
        outs = refs[len(arrays) :]
        here = place()
        for k in range(zs):
            for side, ((a, i), (b, n, back)) in enumerate(where[k]):
                at = chip_of(here, side // 2, side % 2, k, zs) * rows
                top = pl.ds(pl.multiple_of(at, 16), row)
                for out, lo, hi in zip(outs, ends, ends[1:]):
                    out[top, :] = refs[a][i, :row, lo:hi]

    return kernel(
        body,
        arrays,
        [shape((WIDTH, hi - lo), BF16) for lo, hi in zip(ends, ends[1:])],
        "build_qkv",
        flops=10**6,
        bytes_accessed=4 * 10**6,
    )


def build_split(near, far, late, rows, hidden, cuts):
    zs = len(late) + 1
    quarters = zs * 4 * hidden // HALF
    count = len(near) + len(far)

    def body(*refs):
        nears, fars, lates = refs[: len(near)], refs[len(near) : count], refs[count:-2]
        w1_ref, w2_ref = refs[-2:]
        here = place()

        def read(k, side, lo, n):
            if k > 0 and lo >= cuts[2]:
                return lates[k - 1][side, lo - cuts[2] : lo - cuts[2] + n, :]
            refs_of, at, row = (nears, 0, cuts[1]) if k == 0 else (fars, k - 1, cuts[0])
            if side < 3:
                return refs_of[side][at, lo : lo + n, :]
            if lo < row:
                return refs_of[3][at, lo : lo + n, :]
            return refs_of[4][at, lo - row : lo - row + n, :]

        for k in range(zs):
            for side in range(4):
                chip = chip_of(here, side // 2, side % 2, k, zs)
                to, down = rows_at(chip, rows), rows_at(chip, hidden)
                for j in range(quarters):
                    w1_ref[to, j * HALF : (j + 1) * HALF] = read(k, side, j * rows, rows)
                lo = quarters * rows
                w2_ref[down, :HALF] = read(k, side, lo, hidden)
                lo += hidden
                part = cuts[2] - lo
                down = pl.ds(pl.multiple_of(chip * hidden, 16), part)
                w2_ref[down, HALF:] = read(k, side, lo, part)
                down = pl.ds(pl.multiple_of(chip * hidden + part, 16), hidden - part)
                w2_ref[down, HALF:] = read(k, side, lo + part, hidden - part)

    return kernel(
        body,
        (*near, *far, *late),
        (shape((WIDTH, zs * 4 * hidden), BF16), shape((zs * 4 * hidden, WIDTH), BF16)),
        "build_split",
    )


def build_rest(arrays, where, rows, hidden):
    zs = len(where)
    units = zs * 4 * hidden
    quarters = units // HALF
    first = quarters * rows
    if rows % 16:
        full = to_mesh_order(by_distance(arrays, where, first)).reshape(4 * zs, -1, HALF)
        w1 = jnp.swapaxes(full[:, :first].reshape(4 * zs, quarters, rows, HALF), 1, 2)
        w2 = jnp.swapaxes(full[:, first:].reshape(4 * zs, 2, hidden, HALF), 1, 2)
        return w1.reshape(WIDTH, units), w2.reshape(units, WIDTH)

    def body(*refs):
        w1_ref, w2_ref = refs[len(arrays) :]
        here = place()
        for k in range(zs):
            for side, ((a, i), (b, n, back)) in enumerate(where[k]):
                chip = chip_of(here, side // 2, side % 2, k, zs)
                to, down = rows_at(chip, rows), rows_at(chip, hidden)
                for j in range(quarters):
                    w1_ref[to, j * HALF : (j + 1) * HALF] = refs[a][i, j * rows : (j + 1) * rows, :]
                for j in range(2):
                    lo = first + j * hidden - back
                    w2_ref[down, j * HALF : (j + 1) * HALF] = refs[b][n, lo : lo + hidden, :]

    return kernel(
        body,
        arrays,
        (shape((WIDTH, units), BF16), shape((units, WIDTH), BF16)),
        "build_rest",
        flops=10**6,
        bytes_accessed=10**7,
    )


def whole_spec(*dims):
    return pl.BlockSpec(dims, lambda i: (0,) * len(dims))


def attend_step(q_ref, kv_ref, m_ref, l_ref, acc_ref):
    for h in range(NH):
        lo = h * HD
        qh = q_ref[:, lo : lo + HD]
        kh = kv_ref[:, lo : lo + HD]
        vh = kv_ref[:, HALF + lo : HALF + lo + HD]
        s = mm_t(kh, qh)
        before = m_ref[h : h + 1, :]
        top = jnp.maximum(before, jnp.max(s, axis=0, keepdims=True))
        p = jnp.exp(s - top)
        factor = jnp.exp(before - top)
        m_ref[h : h + 1, :] = top
        l_ref[h : h + 1, :] = l_ref[h : h + 1, :] * factor + jnp.sum(p, axis=0, keepdims=True)
        acc_ref[lo : lo + HD, :] = acc_ref[lo : lo + HD, :] * factor + t_mm(vh, p.astype(BF16))


def keys_values(x_ref, w_ref, v_bias, kv_ref):
    kv_ref[:, :HALF] = mm(x_ref[...], w_ref[:, :HALF]).astype(BF16)
    kv_ref[:, HALF:] = (mm(x_ref[...], w_ref[:, HALF:]) + v_bias).astype(BF16)


def attend_cost(tokens, keys):
    return pl.CostEstimate(flops=1, bytes_accessed=1, transcendentals=0)


def attend_first(own, got, xo, wq, wkv):
    tokens, keys = own.shape[0], xo.shape[0]
    block = math.gcd(keys, 1024)
    rows = pl.BlockSpec((block, WIDTH), lambda i: (i, 0))

    def body(o_ref, g_ref, x_ref, wq_ref, wkv_ref, q_ref, kv_ref, vec_ref, b_ref, m_ref, l_ref, acc_ref):
        @pl.when(pl.program_id(0) == 0)
        def _():
            core = place()[3]
            vecs = jnp.transpose(wq_ref[:, HALF:].astype(F32))
            vec_ref[...] = vecs[:16]
            b_ref[...] = jnp.where(core == 0, vecs[:8, :HALF], vecs[:8, HALF:])
            for i, ref in enumerate((o_ref, g_ref)):
                part = mm(ref[...], wq_ref[:, :HALF]) + b_ref[0:1, :]
                q_ref[i * tokens : (i + 1) * tokens, :] = part.astype(BF16) * BF16(0.125)
            m_ref[...] = jnp.full(m_ref.shape, -1e30, F32)
            l_ref[...] = jnp.zeros(l_ref.shape, F32)
            acc_ref[...] = jnp.zeros(acc_ref.shape, F32)

        keys_values(x_ref, wkv_ref, b_ref[1:2, :], kv_ref)
        attend_step(q_ref, kv_ref, m_ref, l_ref, acc_ref)

    return pl.pallas_call(
        body,
        grid=(keys // block,),
        in_specs=[
            whole_spec(tokens, WIDTH),
            whole_spec(tokens, WIDTH),
            rows,
            whole_spec(*wq.shape),
            whole_spec(*wkv.shape),
        ],
        out_specs=[
            whole_spec(2 * tokens, HALF),
            rows,
            whole_spec(16, WIDTH),
            whole_spec(8, HALF),
            whole_spec(8, 2 * tokens),
            whole_spec(8, 2 * tokens),
            whole_spec(HALF, 2 * tokens),
        ],
        out_shape=[
            shape((2 * tokens, HALF), BF16),
            shape((keys, WIDTH), BF16),
            shape((16, WIDTH), F32),
            shape((8, HALF), F32),
            shape((8, 2 * tokens), F32),
            shape((8, 2 * tokens), F32),
            shape((HALF, 2 * tokens), F32),
        ],
        compiler_params=pltpu.CompilerParams(vmem_limit_bytes=20 * MIB),
        cost_estimate=attend_cost(tokens, keys),
        name="attend_first",
    )(own, got, xo, wq, wkv)


def attend_last(q, xc, wkv, bias, top, total, weighted):
    tokens, keys = q.shape[0], xc.shape[0]
    block = math.gcd(keys, 1024)
    rows = pl.BlockSpec((block, WIDTH), lambda i: (i, 0))

    def body(q_ref, x_ref, w_ref, b_ref, mi_ref, li_ref, ai_ref, kv_ref, o_ref, ctx_ref, lse_ref, m_s, l_s, acc_s):
        @pl.when(pl.program_id(0) == 0)
        def _():
            m_s[...] = mi_ref[...]
            l_s[...] = li_ref[...]
            acc_s[...] = ai_ref[...]

        keys_values(x_ref, w_ref, b_ref[1:2, :], kv_ref)
        attend_step(q_ref, kv_ref, m_s, l_s, acc_s)

        @pl.when(pl.program_id(0) == pl.num_programs(0) - 1)
        def _():
            lse_ref[...] = m_s[...] + jnp.log(l_s[...])
            for h in range(NH):
                lo = h * HD
                o_ref[lo : lo + HD, :] = acc_s[lo : lo + HD, :] / l_s[h : h + 1, :]
            ctx_ref[...] = jnp.transpose(o_ref[...]).astype(BF16)

    return pl.pallas_call(
        body,
        grid=(keys // block,),
        in_specs=[
            whole_spec(tokens, HALF),
            rows,
            whole_spec(*wkv.shape),
            whole_spec(8, HALF),
            whole_spec(8, tokens),
            whole_spec(8, tokens),
            whole_spec(HALF, tokens),
        ],
        out_specs=[
            rows,
            whole_spec(HALF, tokens),
            whole_spec(tokens, HALF),
            whole_spec(8, tokens),
        ],
        out_shape=[
            shape((keys, WIDTH), BF16),
            shape((HALF, tokens), F32),
            shape((tokens, HALF), BF16),
            shape((8, tokens), F32),
        ],
        scratch_shapes=[
            pltpu.VMEM((8, tokens), F32),
            pltpu.VMEM((8, tokens), F32),
            pltpu.VMEM((HALF, tokens), F32),
        ],
        compiler_params=pltpu.CompilerParams(vmem_limit_bytes=20 * MIB),
        cost_estimate=attend_cost(tokens // 2, keys),
        name="attend_last",
    )(q, xc, wkv, bias, top, total, weighted)


def unit_places(chips, per, rows, core):
    units = chips * per * rows
    unit = lax.broadcasted_iota(jnp.int32, (WIDTH, units), 1)
    at = lax.broadcasted_iota(jnp.int32, (WIDTH, units), 0)
    chip, inside = unit // (per * rows), lax.rem(unit, rows)
    return (at == chip * (2 * rows) + core * rows + inside).astype(BF16)


def unit_bias(vecs, chips, per, rows):
    units = chips * per * rows

    def body(v_ref, out_ref):
        every = mm(v_ref[...].astype(BF16), unit_places(chips, per, rows, place()[3]))
        turn = lax.rem(lax.broadcasted_iota(jnp.int32, (16, units), 1) // rows, per)
        row = lax.broadcasted_iota(jnp.int32, (16, units), 0)
        out_ref[...] = column_sum(jnp.where(row == 9 + turn, every, 0.0))

    return kernel(body, (vecs,), (shape((1, units), F32),), "unit_bias", flops=10**8)[0]


def unit_rows(sums, chips, per, rows):
    units = chips * per * rows

    def body(s_ref, out_ref):
        turn = lax.rem(lax.broadcasted_iota(jnp.int32, (8, units), 1) // rows, per)
        row = lax.broadcasted_iota(jnp.int32, (8, units), 0)
        spread_out = jnp.where(row == turn, s_ref[...], 0.0).astype(BF16)
        out_ref[...] = mm_t(spread_out, unit_places(chips, per, rows, place()[3]))

    return kernel(body, (sums,), (shape((8, WIDTH), F32),), "unit_rows", flops=10**8)[0]


def norm_forward(residual, gain, shift):
    center = residual - jnp.mean(residual, axis=-1, keepdims=True)
    scale = lax.rsqrt(jnp.mean(center * center, axis=-1, keepdims=True) + EPSILON)
    normed = center * scale
    return normed * gain + shift, normed, scale


def norm_backward(grad_out, normed, scale, gain):
    grad_normed = grad_out * gain
    return scale * (
        grad_normed
        - jnp.mean(grad_normed, axis=-1, keepdims=True)
        - normed * jnp.mean(grad_normed * normed, axis=-1, keepdims=True)
    )


def column_sum(value):
    return jnp.sum(value, axis=0, keepdims=True)


def halves(core, own, other):
    left = jnp.where(core == 0, own, other)
    right = jnp.where(core == 0, other, own)
    return left, right


def mix(ctx, ctx_got, mixer_own, mixer_got, vecs, inputs):
    tokens = inputs.shape[0]

    def body(o_ref, g_ref, mo_ref, mg_ref, v_ref, x_ref, low_ref, row_ref, n_ref, s_ref):
        core = place()[3]
        mine = pl.ds(pl.multiple_of(core * HALF, HALF), HALF)
        others = pl.ds(pl.multiple_of((1 - core) * HALF, HALF), HALF)
        parts = [
            mm(o_ref[:tokens, :], ref[mine, :]) + mm(g_ref[tokens:, :], ref[others, :])
            for ref in (mo_ref, mg_ref)
        ]
        attended = jnp.concatenate(halves(core, *parts), axis=1) + v_ref[2:3, :]
        rows, normed, scale = norm_forward(
            x_ref[...].astype(F32) + attended, v_ref[3:4, :], v_ref[4:5, :]
        )
        low_ref[...] = rows.astype(BF16)
        row_ref[...] = rows
        n_ref[...] = normed
        s_ref[...] = scale

    return kernel(
        body,
        (ctx, ctx_got, mixer_own, mixer_got, vecs, inputs),
        (
            shape((tokens, WIDTH), BF16),
            shape((tokens, WIDTH), F32),
            shape((tokens, WIDTH), F32),
            shape((tokens, 1), F32),
        ),
        "mix",
        flops=10**9,
        bytes_accessed=3 * 10**6,
    )


def feed(own, got, w_inner, i_bias, w_outer):
    tokens = own.shape[0]
    units = w_inner.shape[1]

    def body(o_ref, g_ref, w1_ref, b_ref, w2_ref, two_ref, act_ref, slope_ref, mine_ref, send_ref):
        two_ref[:tokens, :] = o_ref[...]
        two_ref[tokens:, :] = g_ref[...]
        u = mm(two_ref[...], w1_ref[...]) + b_ref[...]
        cdf = 0.5 * (1.0 + lax.erf(u * ROOT_HALF))
        slope_ref[...] = cdf + u * jnp.exp(-0.5 * u * u) * GAUSS_FACTOR
        act_ref[...] = (u * cdf).astype(BF16)
        part = mm(act_ref[...], w2_ref[...])
        mine_ref[...] = part[:tokens]
        send_ref[...] = part[tokens:]

    return kernel(
        body,
        (own, got, w_inner, i_bias, w_outer),
        (
            shape((2 * tokens, WIDTH), BF16),
            shape((2 * tokens, units), BF16),
            shape((2 * tokens, units), F32),
            shape((tokens, WIDTH), F32),
            shape((tokens, WIDTH), F32),
        ),
        "feed",
        flops=3 * 10**9,
        bytes_accessed=8 * 10**6,
    )


def crown(mine, got, first_rows, vecs, out_cot, term_cot):
    tokens = mine.shape[0]

    def body(
        m_ref, g_ref, f_ref, v_ref, oc_ref, tc_ref, out_ref, term_ref, gs_ref, go_ref, sum_ref
    ):
        gain = v_ref[6:7, :]
        head = v_ref[8:9, :]
        outer = m_ref[...] + g_ref[...] + v_ref[5:6, :]
        rows, normed, scale = norm_forward(f_ref[...] + outer, gain, v_ref[7:8, :])
        out_ref[...] = rows.astype(BF16)
        logits = jnp.sum(rows * head, axis=-1, keepdims=True)
        small = jnp.exp(-jnp.abs(logits))
        term = jnp.maximum(logits, 0.0) + jnp.log1p(small)
        term_ref[...] = jnp.transpose(jnp.broadcast_to(term, (tokens, 128)))[0:1, :]
        sig = jnp.where(logits >= 0.0, 1.0, small) / (1.0 + small)
        cot = jnp.transpose(jnp.broadcast_to(tc_ref[...], (128, tokens)))[:, 0:1]
        slope = cot * sig
        grad_final = oc_ref[...].astype(F32) + slope * head
        grad = norm_backward(grad_final, normed, scale, gain)
        low = grad.astype(BF16)
        gs_ref[...] = grad
        go_ref[...] = low
        sum_ref[...] = jnp.concatenate(
            [
                column_sum(low.astype(F32)),
                column_sum(grad_final * normed),
                column_sum(grad_final),
                column_sum(slope * rows),
                jnp.zeros((4, WIDTH), F32),
            ],
            axis=0,
        )

    return kernel(
        body,
        (mine, got, first_rows, vecs, out_cot, term_cot),
        (
            shape((tokens, WIDTH), BF16),
            shape((1, tokens), F32),
            shape((tokens, WIDTH), F32),
            shape((tokens, WIDTH), BF16),
            shape((8, WIDTH), F32),
        ),
        "crown",
        flops=10**8,
        bytes_accessed=3 * 10**6,
    )


def feed_back(own, got, slope, w_inner, w_outer):
    tokens = own.shape[0]
    units = w_inner.shape[1]

    def body(o_ref, g_ref, s_ref, w1_ref, w2_ref, two_ref, gi_ref, mine_ref, send_ref, sum_ref):
        two_ref[:tokens, :] = o_ref[...]
        two_ref[tokens:, :] = g_ref[...]
        low = (mm_t(two_ref[...], w2_ref[...]) * s_ref[...]).astype(BF16)
        gi_ref[...] = low
        sum_ref[...] = column_sum(low.astype(F32))
        part = mm_t(gi_ref[...], w1_ref[...])
        mine_ref[...] = part[:tokens]
        send_ref[...] = part[tokens:]

    return kernel(
        body,
        (own, got, slope, w_inner, w_outer),
        (
            shape((2 * tokens, WIDTH), BF16),
            shape((2 * tokens, units), BF16),
            shape((tokens, WIDTH), F32),
            shape((tokens, WIDTH), F32),
            shape((1, units), F32),
        ),
        "feed_back",
        flops=3 * 10**9,
        bytes_accessed=8 * 10**6,
    )


def mix_back(mine, got, grad_second, normed, scale, vecs, mixer_own, mixer_got):
    tokens = mine.shape[0]

    def body(
        m_ref, g_ref, gs_ref, n_ref, s_ref, v_ref, mo_ref, mg_ref, res_ref, keep_ref, send_ref, sum_ref
    ):
        core = place()[3]
        first = gs_ref[...] + m_ref[...] + g_ref[...]
        normal = n_ref[...]
        grad = norm_backward(first, normal, s_ref[...], v_ref[3:4, :])
        res_ref[...] = grad
        low = grad.astype(BF16)
        sum_ref[...] = jnp.concatenate(
            [
                column_sum(low.astype(F32)),
                column_sum(first * normal),
                column_sum(first),
                jnp.zeros((5, WIDTH), F32),
            ],
            axis=0,
        )
        mine_low, other_low = halves(core, low[:, :HALF], low[:, HALF:])
        ctx = (mm_t(mine_low, mo_ref[...]) + mm_t(other_low, mg_ref[...])).astype(BF16)
        mine_ctx, other_ctx = halves(core, ctx[:, :HALF], ctx[:, HALF:])
        keep_ref[:, :HALF] = mine_ctx
        keep_ref[:, HALF:] = mine_low
        send_ref[:, :HALF] = other_ctx
        send_ref[:, HALF:] = other_low

    return kernel(
        body,
        (mine, got, grad_second, normed, scale, vecs, mixer_own, mixer_got),
        (
            shape((tokens, WIDTH), F32),
            shape((tokens, WIDTH), BF16),
            shape((tokens, WIDTH), BF16),
            shape((8, WIDTH), F32),
        ),
        "mix_back",
        flops=10**9,
        bytes_accessed=4 * 10**6,
    )


def attend_back_step(q_ref, g_ref, lse_ref, delta_ref, kv_ref, out_ref, acc_ref, sum_ref):
    held = []
    for h in range(NH):
        lo = h * HD
        qh = q_ref[:, lo : lo + HD]
        gh = g_ref[:, lo : lo + HD]
        kh = kv_ref[:, lo : lo + HD]
        vh = kv_ref[:, HALF + lo : HALF + lo + HD]
        p = jnp.exp(mm_t(kh, qh) - lse_ref[h : h + 1, :])
        dp = mm_t(vh, gh)
        ds = (p * (dp - delta_ref[h : h + 1, :])).astype(BF16)
        acc_ref[lo : lo + HD, :] += t_mm(kh, ds)
        held.append((mm(ds, qh).astype(BF16), mm(p.astype(BF16), gh).astype(BF16)))
        if h % 2 == 1:
            (dk0, dv0), (dk1, dv1) = held
            held = []
            at = lo - HD
            dv = jnp.concatenate([dv0, dv1], axis=1)
            out_ref[:, at : at + 2 * HD] = jnp.concatenate([dk0, dk1], axis=1)
            out_ref[:, HALF + at : HALF + at + 2 * HD] = dv
            sum_ref[1:2, at : at + 2 * HD] += column_sum(dv.astype(F32))


def attend_back_cost(tokens, keys):
    return pl.CostEstimate(flops=1, bytes_accessed=1, transcendentals=0)


def attend_back_first(q, low, low_got, o, lse, kv):
    tokens, keys = q.shape[0], kv.shape[0]
    block = math.gcd(keys, 1024)
    rows = pl.BlockSpec((block, WIDTH), lambda i: (i, 0))

    def body(q_ref, go_ref, gc_ref, o_ref, lse_ref, kv_ref, d_ref, g_ref, delta_ref, acc_ref, sum_ref):
        @pl.when(pl.program_id(0) == 0)
        def _():
            acc_ref[...] = jnp.zeros(acc_ref.shape, F32)
            sum_ref[...] = jnp.zeros(sum_ref.shape, F32)
            g_ref[: tokens // 2, :] = go_ref[:, :HALF]
            g_ref[tokens // 2 :, :] = gc_ref[:, :HALF]
            prod = jnp.transpose(g_ref[...].astype(F32)) * o_ref[...]
            for h in range(NH):
                delta_ref[h : h + 1, :] = column_sum(prod[h * HD : (h + 1) * HD, :])

        attend_back_step(q_ref, g_ref, lse_ref, delta_ref, kv_ref, d_ref, acc_ref, sum_ref)

    return pl.pallas_call(
        body,
        grid=(keys // block,),
        in_specs=[
            whole_spec(tokens, HALF),
            whole_spec(tokens // 2, WIDTH),
            whole_spec(tokens // 2, WIDTH),
            whole_spec(HALF, tokens),
            whole_spec(8, tokens),
            rows,
        ],
        out_specs=[
            rows,
            whole_spec(tokens, HALF),
            whole_spec(8, tokens),
            whole_spec(HALF, tokens),
            whole_spec(8, HALF),
        ],
        out_shape=[
            shape((keys, WIDTH), BF16),
            shape((tokens, HALF), BF16),
            shape((8, tokens), F32),
            shape((HALF, tokens), F32),
            shape((8, HALF), F32),
        ],
        compiler_params=pltpu.CompilerParams(vmem_limit_bytes=20 * MIB),
        cost_estimate=attend_back_cost(tokens, keys),
        name="attend_back_first",
    )(q, low, low_got, o, lse, kv)


def attend_back_last(q, g, lse, delta, acc, sums, kv, wq):
    tokens, keys = q.shape[0], kv.shape[0]
    block = math.gcd(keys, 1024)
    rows = pl.BlockSpec((block, WIDTH), lambda i: (i, 0))

    def body(q_ref, g_ref, lse_ref, delta_ref, ai_ref, si_ref, kv_ref, w_ref, d_ref, dq_ref, sum_ref, send_ref, acc_s):
        @pl.when(pl.program_id(0) == 0)
        def _():
            acc_s[...] = ai_ref[...]
            sum_ref[...] = si_ref[...]

        attend_back_step(q_ref, g_ref, lse_ref, delta_ref, kv_ref, d_ref, acc_s, sum_ref)

        @pl.when(pl.program_id(0) == pl.num_programs(0) - 1)
        def _():
            dq = jnp.transpose(acc_s[...] * 0.125).astype(BF16)
            dq_ref[...] = dq
            sum_ref[0:1, :] = column_sum(dq.astype(F32))
            send_ref[...] = mm_t(dq[tokens // 2 :], w_ref[:, :HALF]).astype(BF16)

    return pl.pallas_call(
        body,
        grid=(keys // block,),
        in_specs=[
            whole_spec(tokens, HALF),
            whole_spec(tokens, HALF),
            whole_spec(8, tokens),
            whole_spec(8, tokens),
            whole_spec(HALF, tokens),
            whole_spec(8, HALF),
            rows,
            whole_spec(*wq.shape),
        ],
        out_specs=[
            rows,
            whole_spec(tokens, HALF),
            whole_spec(8, HALF),
            whole_spec(tokens // 2, WIDTH),
        ],
        out_shape=[
            shape((keys, WIDTH), BF16),
            shape((tokens, HALF), BF16),
            shape((8, HALF), F32),
            shape((tokens // 2, WIDTH), BF16),
        ],
        scratch_shapes=[pltpu.VMEM((HALF, tokens), F32)],
        compiler_params=pltpu.CompilerParams(vmem_limit_bytes=20 * MIB),
        cost_estimate=attend_back_cost(tokens, keys),
        name="attend_back_last",
    )(q, g, lse, delta, acc, sums, kv, wq)


def input_part_other(dkv, wkv):
    keys = dkv.shape[0]
    block = math.gcd(keys, 1024)
    rows = pl.BlockSpec((block, WIDTH), lambda i: (i, 0))

    def body(d_ref, w_ref, out_ref):
        out_ref[...] = mm_t(d_ref[...], w_ref[...]).astype(BF16)

    return pl.pallas_call(
        body,
        grid=(keys // block,),
        in_specs=[rows, whole_spec(*wkv.shape)],
        out_specs=rows,
        out_shape=shape((keys, WIDTH), BF16),
        compiler_params=pltpu.CompilerParams(vmem_limit_bytes=12 * MIB),
        cost_estimate=pl.CostEstimate(flops=1, bytes_accessed=1, transcendentals=0),
        name="input_part_other",
    )(dkv, wkv)


def input_part_own(dkv, wkv, got, dq, wq, q_got):
    keys = dkv.shape[0]
    tokens = q_got.shape[0]
    block = math.gcd(keys // 2, 512)
    half = keys // 2 // block
    rows = pl.BlockSpec((block, WIDTH), lambda i: (i, 0))

    def body(d_ref, w_ref, g_ref, dq_ref, wq_ref, qg_ref, keep_ref, send_ref, part_s):
        step = pl.program_id(0)
        part_s[...] = mm_t(d_ref[...], w_ref[...]) + g_ref[...].astype(F32)

        @pl.when(step == 0)
        def _():
            part_s[:tokens, :] += mm_t(dq_ref[:tokens, :], wq_ref[:, :HALF]) + qg_ref[...].astype(
                F32
            )

        @pl.when(step < half)
        def _():
            keep_ref[...] = part_s[...].astype(BF16)

        @pl.when(step >= half)
        def _():
            send_ref[...] = part_s[...].astype(BF16)

    return pl.pallas_call(
        body,
        grid=(2 * half,),
        in_specs=[
            rows,
            whole_spec(*wkv.shape),
            rows,
            whole_spec(*dq.shape),
            whole_spec(*wq.shape),
            whole_spec(*q_got.shape),
        ],
        out_specs=[
            pl.BlockSpec((block, WIDTH), lambda i: (jnp.minimum(i, half - 1), 0)),
            pl.BlockSpec((block, WIDTH), lambda i: (jnp.maximum(i - half, 0), 0)),
        ],
        out_shape=[shape((keys // 2, WIDTH), BF16)] * 2,
        scratch_shapes=[pltpu.VMEM((block, WIDTH), F32)],
        compiler_params=pltpu.CompilerParams(vmem_limit_bytes=12 * MIB),
        cost_estimate=pl.CostEstimate(flops=1, bytes_accessed=1, transcendentals=0),
        name="input_part_own",
    )(dkv, wkv, got, dq, wq, q_got)


def spread(zs, rows, cols, args, fill, name, scratch, limit=14):
    count = len(args)

    def body(*refs):
        ins, outs, held = refs[:count], refs[count : count + 4], refs[count + 4 :]
        write = fill(ins, held)
        here = place()
        for k in range(zs):
            for side in range(4):
                write(outs[side], k, chip_of(here, side // 2, side % 2, k, zs))

    return kernel(
        body,
        args,
        [shape((zs, rows, cols), BF16)] * 4,
        name,
        limit=limit,
        scratch=[pltpu.VMEM(dims, BF16) for dims in scratch],
        flops=2 * 10**9,
        bytes_accessed=6 * 10**6,
    )


def spread_slow(full, zs):
    full = to_distance(full.reshape(2, zs, 2, *full.shape[1:]))
    full = full.reshape(4, zs, *full.shape[3:])
    return full[0], full[1], full[2], full[3]


def spread_rest(first2, grad_inner, active, grad_outer2, zs):
    units = active.shape[1]
    rows, hidden = WIDTH // (4 * zs), units // (4 * zs)
    if rows % 16:
        w1 = t_mm(first2, grad_inner).astype(BF16).reshape(4 * zs, rows, units)
        w2 = t_mm(active, grad_outer2).astype(BF16).reshape(4 * zs, hidden, WIDTH)
        return spread_slow(jnp.concatenate([w1[:, :, :WIDTH], w1[:, :, WIDTH:], w2], axis=1), zs)

    late = hidden // 2
    most = 2 * rows + hidden - late

    def body(f_ref, gi_ref, a_ref, go_ref, *outs):
        outs, late_ref, (w1_s, w2_s) = outs[:4], outs[4], outs[5:]
        w1_s[...] = t_mm(f_ref[...], gi_ref[...]).astype(BF16)
        w2_s[...] = t_mm(a_ref[...], go_ref[...]).astype(BF16)
        here = place()
        for k in range(zs):
            for side in range(4):
                chip = chip_of(here, side // 2, side % 2, k, zs)
                at, down = rows_at(chip, rows), chip * hidden
                outs[side][k, :rows, :] = w1_s[at, :WIDTH]
                outs[side][k, rows : 2 * rows, :] = w1_s[at, WIDTH:]
                outs[side][k, 2 * rows :, :] = w2_s[pl.ds(pl.multiple_of(down, 16), hidden - late), :]
                late_ref[k, side] = w2_s[pl.ds(pl.multiple_of(down + hidden - late, 16), late), :]

    return kernel(
        body,
        (first2, grad_inner, active, grad_outer2),
        [shape((zs, most, WIDTH), BF16)] * 4 + [shape((zs, 4, late, WIDTH), BF16)],
        "spread_rest",
        scratch=[pltpu.VMEM((WIDTH, units), BF16), pltpu.VMEM((units, WIDTH), BF16)],
    )


def spread_qkv(zs, x_own, x_got, dq, qv, mid, top, unit, g_kv, ctx, ctx_got, low, low_got):
    tokens = x_own.shape[0]
    rows = WIDTH // (4 * zs)
    cols = WIDE + WIDTH + HALF

    def fill(ins, held):
        part_s = held[0]
        xo, xg, dq_r, qv_r, mid_r, top_r, unit_r, c_r, cg_r, l_r, lg_r, *kv_rs = ins
        core = place()[3]
        part_s[:, :HALF] = (
            t_mm(xo[...], dq_r[:tokens, :]) + t_mm(xg[...], dq_r[tokens:, :])
        ).astype(BF16)
        zero = jnp.zeros((2, HALF), F32)
        sums = jnp.concatenate(
            [
                jnp.concatenate(halves(core, qv_r[0:2, :], zero), axis=1),
                mid_r[0:3, :],
                top_r[0:4, :],
                unit_r[...],
                jnp.zeros((AUX - 17, WIDTH), F32),
            ],
            axis=0,
        )
        part_s[:, HALF:WIDE] = jnp.transpose(sums).astype(BF16)
        if len(kv_rs) == 1:
            part_s[:, WIDE : WIDE + WIDTH] = kv_rs[0][...]
        else:
            xk, dk, xl, dl = kv_rs
            part_s[:, WIDE : WIDE + WIDTH] = (t_mm(xk[...], dk[...]) + t_mm(xl[...], dl[...])).astype(
                BF16
            )
        lows = (l_r[:, HALF:], lg_r[:, HALF:])
        part_s[pl.ds(pl.multiple_of(core * HALF, HALF), HALF), WIDE + WIDTH :] = (
            t_mm(c_r[:tokens, :], lows[0]) + t_mm(c_r[tokens:, :], lows[1])
        ).astype(BF16)
        part_s[pl.ds(pl.multiple_of((1 - core) * HALF, HALF), HALF), WIDE + WIDTH :] = (
            t_mm(cg_r[tokens:, :], lows[0]) + t_mm(cg_r[:tokens, :], lows[1])
        ).astype(BF16)

        def write(out, n, chip):
            out[n] = part_s[rows_at(chip, rows), :]

        return write

    args = (x_own, x_got, dq, qv, mid, top, unit, ctx, ctx_got, low, low_got, *g_kv)
    if rows % 16 == 0:
        return spread(zs, rows, cols, args, fill, "spread_qkv", ((WIDTH, cols),), 24)

    def body(*refs):
        fill(refs[:12], refs[12:])

    full = kernel(body, args, [shape((WIDTH, cols), BF16)], "fill_qkv")[0]
    return spread_slow(full.reshape(4 * zs, rows, cols), zs)


def finish_sums(qkv, rest, more, rows):
    count, cols = len(qkv), qkv[0].shape[1]
    hidden = rest[0].shape[0] - 4 * rows
    wide = cols + 2 * WIDTH

    def body(*refs):
        ins, (own_ref, send_ref, outer_ref, both_s) = refs[:-4], refs[-4:]
        core = place()[3]
        both_s[:, :cols] = sum(ref[...].astype(F32) for ref in ins[:count])
        low = sum(ref[...].astype(F32) for ref in ins[count : count + len(rest)])
        if more:
            top = sum(ref[...].astype(F32) for ref in ins[count + len(rest) :])
            most = top.shape[0]
            low = jnp.concatenate([low[:most] + top, low[most:]], axis=0)
        both_s[:, cols : cols + WIDTH] = low[: 2 * rows]
        both_s[:, cols + WIDTH :] = low[2 * rows : 4 * rows]
        outer_ref[...] = low[4 * rows :]
        halves_of = (both_s[:rows, :], both_s[rows:, :])
        own_ref[...] = jnp.where(core == 0, *halves_of)
        send_ref[...] = jnp.where(core == 1, *halves_of)

    return kernel(
        body,
        (*qkv, *rest, *more),
        [shape((rows, wide), F32)] * 2 + [shape((hidden, WIDTH), F32)],
        "finish_sums",
        limit=8,
        scratch=[pltpu.VMEM((2 * rows, wide), F32)],
    )


def finish_rows(own, got, hidden, per):
    rows = own.shape[0]
    base = WIDE + WIDTH + HALF
    chips = (own.shape[1] - base) // hidden

    def body(own_ref, got_ref, *outs):
        core = place()[3]
        left = jnp.where(core == 0, own_ref[...], got_ref[...])
        right = jnp.where(core == 0, got_ref[...], own_ref[...])
        for out, lo in zip(outs, (0, WIDE, WIDE + HALF, WIDE + WIDTH)):
            out[:, :HALF] = left[:, lo : lo + HALF]
            out[:, HALF:] = right[:, lo : lo + HALF]
        outs[4][...] = jnp.concatenate(
            [
                side[:, base + i * hidden : base + (i + 1) * hidden]
                for i in range(chips)
                for side in (left, right)
            ],
            axis=1,
        )
        small = left[:, HALF:WIDE] + right[:, HALF:WIDE]
        if rows < AUX:
            small = jnp.concatenate([small, jnp.zeros((AUX - rows, AUX), F32)], axis=0)
        small = jnp.transpose(small)
        for j in range(9):
            outs[5 + j][...] = small[j, :rows]
        for j in range(per):
            outs[14][pl.ds(j * rows, rows)] = small[9 + j, :rows]

    outs = kernel(
        body,
        (own, got),
        [shape((rows, WIDTH), F32)] * 4
        + [shape((rows, 2 * chips * hidden), F32)]
        + [shape((rows,), F32)] * 9
        + [shape((hidden,), F32)],
        "finish_rows",
        limit=8,
    )
    return (*outs[:5], outs[5:])


def shards(
    layer_input,
    query_weight,
    query_bias,
    key_weight,
    value_weight,
    value_bias,
    mixer_weight,
    mixer_bias,
    first_gain,
    first_shift,
    inner_weight,
    inner_bias,
    outer_weight,
    outer_bias,
    second_gain,
    second_shift,
    head_weight,
    out_cotangent,
    term_cotangent,
):
    core = place()[3]
    chips = lax.axis_size("ctx")
    zs = chips // 4
    inputs = layer_input[0]
    tokens = inputs.shape[0]
    rows = query_weight.shape[0]
    hidden = outer_weight.shape[0]
    ff = inner_weight.shape[1]
    units = ff // 2
    per = hidden // rows

    def in_order(own, other, axis):
        return jnp.stack(halves(core, own, other), axis=axis)

    own, send = pack(
        (query_weight, key_weight, value_weight, mixer_weight),
        inner_weight,
        (
            query_bias,
            value_bias,
            mixer_bias,
            first_gain,
            first_shift,
            outer_bias,
            second_gain,
            second_shift,
            head_weight,
            inner_bias,
        ),
    )
    block, rest = join(own, swap_core(send), outer_weight)
    x_got = swap_core(inputs)
    first = 2 * rows * (units // HALF)
    most, part_far = first + hidden + hidden // 3, 3 * first // 4
    every = tuple(range(zs))
    barrier = lax.optimization_barrier
    part_row = 2 * rows
    if zs == 4:
        near_y, near_x = swap_y(rest[None]), swap_x(rest[None])
        near_y, near_x, qkv = barrier((near_y, near_x, along_z_pieces(block)))
        x_own, first_piece = barrier((inputs, qkv[1]))
        qkv = jnp.stack([qkv[0], first_piece, *qkv[2:]])
        flat = qkv.reshape(first, -1)
        sent_y = swap_y(jnp.concatenate([flat, near_x[0, first:]], axis=1))
        sent_x = swap_x(jnp.concatenate([flat, near_y[0, :first]], axis=1))
        sent_y, sent_x, x_along = barrier((sent_y, sent_x, along_z_pieces(x_own)))
        x_along = jnp.stack(x_along)
        cols = flat.shape[1]
        qkv_y, qkv_x = (sent[:, :cols].reshape(qkv.shape) for sent in (sent_y, sent_x))
        near_far = [sent[None, :, cols:] for sent in (sent_x, sent_y)]
        rest_sent, x_along = barrier((rest[:most], x_along))
        x_y, qkv_far, pieces = barrier(
            (swap_y(x_along), far_out(qkv_y, qkv_x, part_row), along_z_pieces(rest_sent))
        )
        square = jnp.stack(
            [rest[most:], near_y[0, most:], near_x[0, most:], near_far[1][0, most - first :]]
        )
        pieces = jnp.stack(pieces[1:])
        rest_y, rest_x = swap_y(pieces), swap_x(pieces)
    else:
        qkv, x_along, pieces = (along_z_pieces(v) for v in (block, inputs, rest))
        x_y, rest_y, rest_x = swap_y(x_along), swap_y(pieces), swap_x(pieces)
        qkv_y, qkv_x = swap_y(qkv), swap_x(qkv)
        qkv_far = far_out(qkv_y, qkv_x, part_row)
    wq, wkv, mixer_own = build_qkv(
        *sources([(every, qkv, qkv_y, qkv_x, *qkv_far)], part_row), part_row
    )
    mixer_got = swap_core(mixer_own)
    xo = jnp.concatenate([x_along, x_y]).reshape(2 * zs * tokens, WIDTH)
    xc = swap_core(xo)

    q_scaled, kvo, vecs, bias, top, total, weighted = attend_first(inputs, x_got, xo, wq, wkv)
    kvc, o_exact, ctx, lse = attend_last(q_scaled, xc, wkv, bias, top, total, weighted)
    if zs == 4:
        rest_y, rest_x, ctx, *late = barrier(
            (rest_y, rest_x, ctx, swap_z(square, 1), swap_z(square, 2))
        )
        w_inner, w_outer = build_split(
            (rest[None], near_y, near_x, *near_far),
            (pieces, rest_y, rest_x, *far_out(rest_y, rest_x, part_far)),
            (*late, swap_z(square, 3)),
            2 * rows,
            hidden,
            (part_far, first, most),
        )
    else:
        away = [(every, pieces, rest_y, rest_x, *far_out(rest_y, rest_x, first))]
        w_inner, w_outer = build_rest(*sources(away, first), 2 * rows, hidden)
    ctx_got = swap_core(ctx)
    i_bias = unit_bias(vecs, chips, per, rows)
    first_low, first_rows, first_normed, first_scale = mix(
        ctx, ctx_got, mixer_own, mixer_got, vecs, inputs
    )

    first2, active, slope, mine, away = feed(
        first_low, swap_core(first_low), w_inner, i_bias, w_outer
    )
    final_low, term, grad_second, grad_outer, top_sums = crown(
        mine, swap_core(away), first_rows, vecs, out_cotangent[0], term_cotangent
    )
    grad_outer2, grad_inner, mine, away, inner_sums = feed_back(
        grad_outer, swap_core(grad_outer), slope, w_inner, w_outer
    )
    got = swap_core(away)
    keep, rest_y, rest_x, far, *late = spread_rest(first2, grad_inner, active, grad_outer2, zs)
    mine, keep, rest_y, rest_x, far, *late = barrier((mine, keep, rest_y, rest_x, far, *late))
    part_far = far.shape[1] // 2
    over_x, over_y = swap_x(far[:, :part_far]), swap_y(far[:, part_far:])

    grad_residual, low, low_send, mid_sums = mix_back(
        mine, got, grad_second, first_normed, first_scale, vecs, mixer_own, mixer_got
    )
    low_got = swap_core(low_send)
    dkvc, g_both, delta, acc, qv_sums = attend_back_first(
        q_scaled, low, low_got, o_exact, lse, kvc
    )
    if zs == 4:
        (late,) = late
        over_x, over_y, delta, kvo, late_1, late_2, late_3, square = barrier(
            (over_x, over_y, delta, kvo, swap_z(late[1], 1), swap_z(late[2], 2), late[3], late[0])
        )
        late_3 = swap_z(late_3, 3)
    else:
        over_x, over_y, dkvc, kvo = barrier((over_x, over_y, dkvc, kvo))
    away = swap_core(input_part_other(dkvc, wkv))
    rest_y = jnp.concatenate([rest_y[:, : part_far] + over_x, rest_y[:, part_far :]], axis=1)
    rest_x = jnp.concatenate([rest_x[:, : part_far], rest_x[:, part_far :] + over_y], axis=1)
    at = 1 if zs == 4 else 0
    got_y, got_x = swap_y(rest_y[at:]), swap_x(rest_x[at:])
    dkvo, dq, qv_sums, q_away = attend_back_last(
        q_scaled, g_both, lse, delta, acc, qv_sums, kvo, wq
    )

    part, part_y = input_part_own(dkvo, wkv, away, dq, wq, swap_core(q_away))
    dq, dkvo, part, part_y = barrier((dq, dkvo, part, part_y))
    if zs == 4:
        g_kv = (xo, dkvo, xc, dkvc)
    else:
        g_kv = ((t_mm(xo, dkvo) + t_mm(xc, dkvc)).astype(BF16),)
    g_qkv, qkv_y, qkv_x, qkv_far = spread_qkv(
        zs,
        inputs,
        x_got,
        dq,
        qv_sums,
        mid_sums,
        top_sums,
        unit_rows(inner_sums, chips, per, rows),
        g_kv,
        ctx,
        ctx_got,
        low,
        low_got,
    )
    part, part_y = part.reshape(zs, tokens, WIDTH), part_y.reshape(zs, tokens, WIDTH)
    if zs == 4:
        got_y, got_x, part_y, qkv_far, late_3 = barrier((got_y, got_x, part_y, qkv_far, late_3))
        square = square + late_1 + late_2 + late_3
        g_rest = keep[1:] + got_y + got_x
        qkv_far, got_part, far, g_rest = barrier(
            (
                swap_x(qkv_far),
                swap_y(part_y),
                swap_x(square[3]),
                [swap_z(g_rest[k - 1], k) for k in range(1, zs)],
            )
        )
        part = part + got_part
        qkv_x, qkv_far = barrier((qkv_x, qkv_far))
        got_y, got_x, parts = barrier(
            (
                swap_y(qkv_y + qkv_far),
                swap_x(qkv_x),
                [swap_z(part[k], k) for k in range(1, zs)],
            )
        )
        near_y = jnp.concatenate([rest_y[0], square[1] + far])
        near_x = jnp.concatenate([rest_x[0], square[2]])
        near_y, near_x, parts = barrier((near_y, near_x, parts))
        total = part[0].astype(F32)
        for value in parts:
            total = total + value.astype(F32)
        g_qkv = g_qkv + got_y + got_x
        near_y, near_x, pieces = barrier(
            (
                swap_y(near_y),
                swap_x(near_x),
                [swap_z(g_qkv[k], k) for k in range(1, zs)],
            )
        )
        g_qkv = [g_qkv[0], *pieces]
        g_whole = [jnp.concatenate([keep[0], square[0]]), near_y, near_x]
    else:
        g_whole, g_rest = [sum_z([(every, keep + got_y + got_x)])], []
        part = part + swap_y(part_y)
        total = sum_z([(every, part)])
        qkv_y, qkv_x = fan_far(qkv_y, qkv_x, qkv_far, 2 * rows)
        g_qkv = [sum_z([(every, g_qkv + swap_y(qkv_y) + swap_x(qkv_x))])]
    input_grad = (grad_residual + total).astype(BF16)

    own, send, g_outer = finish_sums(g_qkv, g_whole, g_rest, rows)
    g_query, g_key, g_value, g_mixer, g_inner, vectors = finish_rows(
        own, swap_core(send), hidden, per
    )
    return (
        final_low[None],
        term,
        input_grad[None],
        g_query,
        vectors[0],
        g_key,
        g_value,
        vectors[1],
        g_mixer,
        vectors[2],
        vectors[3],
        vectors[4],
        g_inner,
        vectors[9],
        g_outer,
        vectors[5],
        vectors[6],
        vectors[7],
        vectors[8],
    )


def pick(value, index, axis):
    return lax.dynamic_index_in_dim(value, index, axis, keepdims=False)


def solution(mesh):
    both = ("seq", "ctx")
    tok, mat, vec = P("seq", "ctx", None), P(both, None), P(both)
    term = P("seq", "ctx")
    in_specs = (
        tok, mat, vec, mat, mat, vec, mat, vec, vec, vec,
        mat, vec, mat, vec, vec, vec, vec, tok, term,
    )
    out_specs = (
        tok, term, tok, mat, vec, mat, mat, vec, mat, vec,
        vec, vec, mat, vec, mat, vec, vec, vec, vec,
    )
    return jax.shard_map(
        shards, mesh=mesh, in_specs=in_specs, out_specs=out_specs, check_vma=False
    )
```
